128 devices in a mesh: seq: 2 (over y_lo), fsdp: 64 (over z, y_hi, x, core).
Axes of the slice: x: 4, y: 4 (y_hi: 2, y_lo: 2; y = y_hi * 2 + y_lo), z: 4, core: 2. Of those that a mesh axis runs over, the one named last changes fastest.
Arguments:
- inputs: bfloat16 [64, 256, 1536], P('fsdp', 'seq'), may hold values from -6 to 6
- cotangent: bfloat16 [64, 256, 1536], P('fsdp', 'seq'), may hold values from -6 to 6
- attn_weight: float32 [1536, 3584], P('fsdp'), may hold values from -4 to 4
- attn_moment_one: float32 [1536, 3584], P('fsdp'), may hold values from -16384 to 16384
- attn_moment_two: float32 [1536, 3584], P('fsdp'), may hold values from 0 to 262144, as said below
- mlp_weight: float32 [1536, 26880], P('fsdp'), may hold values from -4 to 4
- mlp_moment_one: float32 [1536, 26880], P('fsdp'), may hold values from -16384 to 16384
- mlp_moment_two: float32 [1536, 26880], P('fsdp'), may hold values from 0 to 262144, as said below
- vectors: float32 [5120], P('fsdp'), may hold values from -2 to 2, as said below
- vector_moment_one: float32 [5120], P('fsdp'), may hold values from -16384 to 16384
- vector_moment_two: float32 [5120], P('fsdp'), may hold values from 0 to 262144, as said below
Outputs:
- output: bfloat16 [64, 256, 1536], P('fsdp', 'seq')
- input_grad: float32 [64, 256, 1536], P('fsdp', 'seq')
- attn_moment_one_new: float32 [1536, 3584], P('fsdp')
- attn_moment_two_new: float32 [1536, 3584], P('fsdp')
- attn_weight_new: float32 [1536, 3584], P('fsdp')
- mlp_moment_one_new: float32 [1536, 26880], P('fsdp')
- mlp_moment_two_new: float32 [1536, 26880], P('fsdp')
- mlp_weight_new: float32 [1536, 26880], P('fsdp')
- vector_moment_one_new: float32 [5120], P('fsdp')
- vector_moment_two_new: float32 [5120], P('fsdp')
- vectors_new: float32 [5120], P('fsdp')
The draws below stay inside these ranges and needn't reach their ends.
Inputs may be any that keep to these rules, and one draw needn't show every extreme that they name: `attn_moment_two`: positive. `mlp_moment_two`: positive. `vectors`: gains lie in 0.6 to 1.4. `vector_moment_two`: positive.
All inputs are finite; a program needn't handle non-finite values.
Results may differ from the reference program's by a relative error of at most 0.018.
Values may be sent and summed in bfloat16 or wider, within the bound.
No kernel may reach another device: no remote copies, remote signals or barrier semaphores. Data moves between devices by JAX's collectives and lax.ppermute only.
A program may use at most 832 MiB of HBM per device.

```python
import math
import jax
import jax.numpy as jnp
from jax import lax

D = 1536
H = 12
KV = 2
HD = 128
FF = 8960
STEP = 10
SEQ_LEN = 256
SEQS = 64
TOKENS = 16384
QKV = 2048
ATTN_COLS = 3584
VEC = 5120


def column_scales(col_widths, col_values):
    return jnp.concatenate([jnp.full((col_width,), col_value, jnp.float32) for col_width, col_value in zip(col_widths, col_values)])


def attn_grad_scales():
    return column_scales([D, KV * HD, KV * HD, D], [2.0 * math.sqrt(TOKENS), 3.0 * math.sqrt(TOKENS), math.sqrt(TOKENS), 32.0 * math.sqrt(TOKENS / SEQ_LEN)])


def mlp_grad_scales():
    return column_scales([2 * FF, FF], [1.6 * math.sqrt(D * TOKENS / FF), 0.6 * math.sqrt(TOKENS)])


def vector_grad_scales():
    return column_scales([D, D, D, KV * HD, KV * HD], [4.0 * math.sqrt(TOKENS), 2.4 * math.sqrt(TOKENS), 1.8 * math.sqrt(TOKENS), 3.3 * math.sqrt(TOKENS), 0.2 * math.sqrt(SEQ_LEN * TOKENS)])


def first_moment(key, shape, grad_scales):
    noise = jnp.clip(jax.random.normal(key, shape, jnp.float32), -4.0, 4.0)
    return noise * (grad_scales * (0.1 / 0.9))


def second_moment(key, shape, grad_scales):
    factor = jnp.exp(jax.random.uniform(key, shape, jnp.float32, 0.0, math.log(4.0)))
    return factor * (grad_scales * grad_scales * (0.05 / 0.95))


def draw_attn_weight(key, part):
    key = jax.random.fold_in(key, 1)
    noise = jnp.clip(jax.random.normal(key, (D, ATTN_COLS), jnp.float32), -4.0, 4.0)
    return noise * column_scales([D + KV * HD, KV * HD, D], [D ** (-0.5), 8.0 * D ** (-0.5), 0.05 * math.sqrt(SEQ_LEN / D)])


def draw_attn_moment_one(key, part):
    key = jax.random.fold_in(key, 2)
    return first_moment(key, (D, ATTN_COLS), attn_grad_scales())


def draw_attn_moment_two(key, part):
    key = jax.random.fold_in(key, 3)
    return second_moment(key, (D, ATTN_COLS), attn_grad_scales())


def draw_mlp_weight(key, part):
    key = jax.random.fold_in(key, 4)
    noise = jnp.clip(jax.random.normal(key, (D, 3 * FF), jnp.float32), -4.0, 4.0)
    return noise * column_scales([2 * FF, FF], [D ** (-0.5), 3.0 * FF ** (-0.5)])


def draw_mlp_moment_one(key, part):
    key = jax.random.fold_in(key, 5)
    return first_moment(key, (D, 3 * FF), mlp_grad_scales())


def draw_mlp_moment_two(key, part):
    key = jax.random.fold_in(key, 6)
    return second_moment(key, (D, 3 * FF), mlp_grad_scales())


def draw_vectors(key, part):
    key = jax.random.fold_in(key, 7)
    gain_key, bias_key = jax.random.split(key)
    gains = jax.random.uniform(gain_key, (2 * D,), jnp.float32, 0.6, 1.4)
    biases = jnp.clip(0.5 * jax.random.normal(bias_key, (QKV,), jnp.float32), -2.0, 2.0)
    return jnp.concatenate([gains, biases])


def draw_vector_moment_one(key, part):
    key = jax.random.fold_in(key, 8)
    return first_moment(key, (VEC,), vector_grad_scales())


def draw_vector_moment_two(key, part):
    key = jax.random.fold_in(key, 9)
    return second_moment(key, (VEC,), vector_grad_scales())


def block_levels(key, dims, shards, least, largest):
    gain, own = 1.0, jax.random.fold_in(key, 6)
    for axis_at, parts in shards:
        heights = jnp.exp(jax.random.uniform(jax.random.fold_in(own, axis_at), (parts,), jnp.float32, least / len(shards), largest / len(shards)))
        gain = gain * jnp.repeat(heights, dims[axis_at] // parts).reshape([-1 if axis == axis_at else 1 for axis in range(len(dims))])
    return gain


def normal_values(key, shape, deviation, limit, cuts=(), kind=jnp.bfloat16):
    factor_of = block_levels(key, shape, cuts, -0.22, 0.18) if cuts else 1.0
    drawn = jax.random.normal(key, shape, jnp.float32) * deviation * factor_of
    return jnp.minimum(jnp.maximum(drawn, -limit), limit).astype(kind)


def setup_inputs(seed: int = 0) -> dict:
    keys = jax.random.split(jax.random.key(seed), 12)
    return {
        "inputs": normal_values(keys[0], (SEQS, SEQ_LEN, D), 1.0, 6.0, ((0, 64), (1, 2))),
        "cotangent": normal_values(keys[1], (SEQS, SEQ_LEN, D), 1.0, 6.0, ((0, 64), (1, 2))),
        "attn_weight": draw_attn_weight(jax.random.fold_in(keys[11], 71), 0),
        "attn_moment_one": draw_attn_moment_one(jax.random.fold_in(keys[11], 71), 0),
        "attn_moment_two": draw_attn_moment_two(jax.random.fold_in(keys[11], 71), 0),
        "mlp_weight": draw_mlp_weight(jax.random.fold_in(keys[11], 71), 0),
        "mlp_moment_one": draw_mlp_moment_one(jax.random.fold_in(keys[11], 71), 0),
        "mlp_moment_two": draw_mlp_moment_two(jax.random.fold_in(keys[11], 71), 0),
        "vectors": draw_vectors(jax.random.fold_in(keys[11], 71), 0),
        "vector_moment_one": draw_vector_moment_one(jax.random.fold_in(keys[11], 71), 0),
        "vector_moment_two": draw_vector_moment_two(jax.random.fold_in(keys[11], 71), 0),
    }


@jax.custom_vjp
def low(v):
    return lax.optimization_barrier(v.astype(jnp.bfloat16)).astype(jnp.float32)

@jax.custom_vjp
def low_back(v):
    return v

def low_keep(v):
    return (low(v), None)

def low_pass(kept, grad):
    return (grad,)

def back_keep(v):
    return (v, None)

def back_low(kept, grad):
    return (low(grad),)
low.defvjp(low_keep, low_pass)
low_back.defvjp(back_keep, back_low)
norm_eps = 1e-06
rope_base = 1000000.0
precise = lax.Precision.HIGHEST

def rms_scale(values):
    return values * lax.rsqrt(lax.optimization_barrier(jnp.mean(values * values, axis=-1, keepdims=True)) + norm_eps)

def rotary_tables(length, head_dim):
    half_dim = head_dim // 2
    freqs = rope_base ** (-jnp.arange(half_dim, dtype=jnp.float32) * 2.0 / head_dim)
    angles = jnp.arange(length, dtype=jnp.float32)[:, None] * freqs[None, :]
    angles = jnp.concatenate([angles, angles], axis=1)
    return (jnp.cos(angles), jnp.sin(angles))

def rotate(values, cos_table, sin_table):
    half_dim = values.shape[-1] // 2
    turned = jnp.concatenate([-values[..., half_dim:], values[..., :half_dim]], axis=-1)
    return values * cos_table[:, None, :] + turned * sin_table[:, None, :]

def layer(inputs, attn_w, mlp_w, vec_w):
    attn_w = low(attn_w)
    mlp_w = low(mlp_w)
    vec_w = low(vec_w)
    blocks, length = (inputs.shape[0], inputs.shape[1])
    gain_one = vec_w[:D]
    gain_two = vec_w[D:2 * D]
    biases = vec_w[2 * D:]
    normed = low(rms_scale(inputs) * gain_one)
    projected = jnp.einsum('bld,de->ble', normed, attn_w[:, :QKV], precision=precise) + biases
    query_pre = low_back(projected[..., :D]).reshape(blocks, length, H, HD)
    key_pre = low_back(projected[..., D:D + KV * HD]).reshape(blocks, length, KV, HD)
    value_heads = low(low_back(projected[..., D + KV * HD:])).reshape(blocks, length, KV, HD)
    cos_table, sin_table = rotary_tables(length, HD)
    query_heads = low(rotate(query_pre, cos_table, sin_table)).reshape(blocks, length, KV, H // KV, HD)
    key_heads = low(rotate(key_pre, cos_table, sin_table))
    scores = low_back(jnp.einsum('blkgd,bmkd->bkglm', query_heads, key_heads, precision=precise) * HD ** (-0.5))
    causal = jnp.arange(length)[:, None] >= jnp.arange(length)[None, :]
    scores = jnp.where(causal, scores, -1e+30)
    row_max = lax.optimization_barrier(jnp.max(scores, axis=-1, keepdims=True))
    log_total = row_max + jnp.log(lax.optimization_barrier(jnp.sum(jnp.exp(scores - row_max), axis=-1, keepdims=True)))
    attn_probs = low(jnp.exp(scores - log_total))
    attended = jnp.einsum('bkglm,bmkd->blkgd', attn_probs, value_heads, precision=precise).reshape(blocks, length, D)
    attended = low(low_back(attended))
    branch = low_back(jnp.einsum('bld,de->ble', attended, attn_w[:, QKV:], precision=precise))
    middle = inputs + branch
    second = low(rms_scale(middle) * gain_two)
    gate_up = jnp.einsum('bld,df->blf', second, mlp_w[:, :2 * FF], precision=precise)
    gate_value = low_back(gate_up[..., :FF])
    up_value = low_back(gate_up[..., FF:])
    hidden = low(jax.nn.silu(gate_value) * up_value)
    return middle + jnp.einsum('blf,df->bld', hidden, mlp_w[:, 2 * FF:], precision=precise)

def adam_update(weight, moment_one, moment_two, gradient, step_rate):
    moment_one = 0.9 * moment_one + 0.1 * gradient
    moment_two = 0.95 * moment_two + 0.05 * gradient * gradient
    first_hat = moment_one / (1.0 - 0.9 ** STEP)
    second_hat = moment_two / (1.0 - 0.95 ** STEP)
    updated = weight - step_rate * (first_hat / (jnp.sqrt(second_hat) + 1e-08) + 0.1 * weight)
    return (moment_one, moment_two, updated)

def reference(inputs, cotangent, attn_weight, attn_moment_one, attn_moment_two, mlp_weight, mlp_moment_one, mlp_moment_two, vectors, vector_moment_one, vector_moment_two):
    seqs, length = (inputs.shape[0], inputs.shape[1])
    per_block = math.gcd(seqs, max(1, 4096 // length))
    shaped_in = inputs.astype(jnp.float32).reshape(seqs // per_block, per_block, length, D)
    shaped_co = cotangent.astype(jnp.float32).reshape(seqs // per_block, per_block, length, D)

    def scan_step(totals, block_pair):
        block_in, block_co = block_pair
        block_out, pullback = jax.vjp(layer, block_in, attn_weight, mlp_weight, vectors)
        grad_in, grad_attn, grad_mlp, grad_vec = pullback(block_co)
        totals = (totals[0] + grad_attn, totals[1] + grad_mlp, totals[2] + grad_vec)
        return (totals, (block_out, grad_in))
    start_totals = (jnp.zeros(attn_weight.shape, jnp.float32), jnp.zeros(mlp_weight.shape, jnp.float32), jnp.zeros(vectors.shape, jnp.float32))
    totals, (outputs, input_grads) = lax.scan(scan_step, start_totals, (shaped_in, shaped_co))
    output = outputs.reshape(seqs, length, D).astype(jnp.bfloat16)
    input_grad = input_grads.reshape(seqs, length, D)
    attn_one, attn_two, attn_new = adam_update(attn_weight, attn_moment_one, attn_moment_two, totals[0], 0.05)
    mlp_one, mlp_two, mlp_new = adam_update(mlp_weight, mlp_moment_one, mlp_moment_two, totals[1], 0.02)
    vec_one, vec_two, vec_new = adam_update(vectors, vector_moment_one, vector_moment_two, totals[2], 0.5)
    return (output, input_grad, attn_one, attn_two, attn_new, mlp_one, mlp_two, mlp_new, vec_one, vec_two, vec_new)
```

```python
import jax
import jax.numpy as jnp
from jax import lax
from jax.experimental import pallas as pl
from jax.experimental.pallas import tpu as pltpu
from jax.sharding import Mesh
from jax.sharding import PartitionSpec as P

D = 1536
H = 12
KV = 2
HD = 128
FF = 8960
STEP = 10
QKV = 2048
ROWS = 24
TOK = 128
LEN = 256
HALF = D // 2
GROUP = H // KV
COLS = GROUP * HD + 2 * HD
FFT = 1152

norm_eps = 1e-06
rope_base = 1000000.0
f32 = jnp.float32
bf16 = jnp.bfloat16
contract_rows = (((0,), (0,)), ((), ()))
contract_cols = (((1,), (1,)), ((), ()))
score_scale = HD ** (-0.5)
FSDP = ("z", "yh", "x", "core")


def dot(a, b):
    return jnp.dot(a, b, preferred_element_type=f32)


def dot_tn(a, b):
    return lax.dot_general(a, b, contract_rows, preferred_element_type=f32)


def dot_nt(a, b):
    return lax.dot_general(a, b, contract_cols, preferred_element_type=f32)


def split_dot(a, b):
    high = a.astype(bf16)
    low = (a - high.astype(f32)).astype(bf16)
    return dot(high, b) + dot(low, b)


def ring_send(values, axis, shift):
    size = {"z": 4, "x": 4, "yh": 2, "core": 2, "seq": 2}[axis]
    return lax.ppermute(values, axis, [(i, (i + shift) % size) for i in range(size)])


def y_send(values, shift):
    place = lambda y: (y % 2) * 2 + y // 2
    return lax.ppermute(
        values, ("seq", "yh"), [(place(i), place((i + shift) % 4)) for i in range(4)]
    )


def swap_both(values):
    return lax.ppermute(values, ("yh", "core"), [(i, 3 - i) for i in range(4)])


def ring_gather(values, send):
    return jnp.concatenate([values, send(values, 1), send(values, -1), send(values, 2)], axis=0)


def ring_reduce(values, send):
    rows = values.shape[0] // 4
    parts = [values[i * rows : (i + 1) * rows] for i in range(4)]
    low = [p.astype(bf16) for p in parts]
    got = [send(low[1], -1), send(low[2], 1), send(low[3], 2)]
    return parts[0] + got[0].astype(f32) + got[1].astype(f32) + got[2].astype(f32)


def pair_reduce(values, send):
    rows = values.shape[0] // 2
    return values[:rows] + send(values[rows:].astype(bf16)).astype(f32)


def gather_rows(values):
    values = ring_gather(values, lambda v, k: ring_send(v, "x", k))
    values = jnp.concatenate([values, ring_send(values, "yh", 1)], axis=0)
    values = ring_gather(values, lambda v, k: ring_send(v, "z", k))
    return jnp.concatenate([values, ring_send(values, "core", 1)], axis=0)


def reduce_rows(values):
    values = pair_reduce(values, lambda v: ring_send(v, "core", 1))
    values = ring_reduce(values, lambda v, k: ring_send(v, "z", k))
    values = pair_reduce(values, lambda v: ring_send(v, "yh", 1))
    return ring_reduce(values, lambda v, k: ring_send(v, "x", k))


def gather_tokens(values):
    values = ring_gather(values, y_send)
    return jnp.concatenate([values, ring_send(values, "core", 1)], axis=0)


def reduce_tokens(values):
    values = pair_reduce(values, lambda v: ring_send(v, "core", 1))
    return ring_reduce(values, y_send)


def near(index):
    return jnp.where(index == 1, -1, jnp.where(index == 0, 0, index - 1))


def gathered_rows(shape, dim):
    j = lax.broadcasted_iota(jnp.int32, shape, dim)
    r, xi, yi, zi, ci = j % 24, (j // 24) % 4, (j // 96) % 2, (j // 192) % 4, j // 768
    z = (lax.axis_index("z") + near(zi) + 4) % 4
    x = (lax.axis_index("x") + near(xi) + 4) % 4
    yh = (lax.axis_index("yh") + yi) % 2
    core = (lax.axis_index("core") + ci) % 2
    return z * 384 + yh * 192 + x * 48 + core * 24 + r


def mlp_rows(shape, dim):
    j = lax.broadcasted_iota(jnp.int32, shape, dim)
    r, core, yh, x, z = j % 24, (j // 24) % 2, (j // 48) % 2, (j // 96) % 4, j // 384
    return z * 384 + yh * 192 + x * 48 + core * 24 + r


def rotary_tables(positions):
    half_dim = HD // 2
    freqs = rope_base ** (-jnp.arange(half_dim, dtype=f32) * 2.0 / HD)
    angles = positions.astype(f32)[:, None] * freqs[None, :]
    cos, sin = jnp.cos(angles), jnp.sin(angles)
    return jnp.concatenate([cos, cos], axis=1), jnp.concatenate([-sin, sin], axis=1)


def causal_mask(half):
    row = (lax.broadcasted_iota(jnp.int32, (LEN, LEN), 0) + half * TOK) % LEN
    col = (lax.broadcasted_iota(jnp.int32, (LEN, LEN), 1) + half * TOK) % LEN
    return row >= col


def attend_kernel(half_ref, qkv_ref, bias_ref, cos_ref, sin_ref, low_ref, out_ref, log_ref):
    cos, sin = cos_ref[...], sin_ref[...]
    mask = causal_mask(half_ref[0])

    def rotated(start):
        z = qkv_ref[:, start : start + HD] + bias_ref[:, start : start + HD]
        return (z * cos + pltpu.roll(z, HD // 2, 1) * sin).astype(bf16)

    key = rotated(GROUP * HD)
    low_ref[:, GROUP * HD : (GROUP + 1) * HD] = key
    value = (qkv_ref[:, (GROUP + 1) * HD :] + bias_ref[:, (GROUP + 1) * HD :]).astype(bf16)
    low_ref[:, (GROUP + 1) * HD :] = value
    for h in range(GROUP):
        query = rotated(h * HD)
        low_ref[:, h * HD : (h + 1) * HD] = query
        scores = jnp.where(mask, dot_nt(query, key) * score_scale, -1e30)
        top = jnp.max(scores, axis=-1, keepdims=True)
        total = top + jnp.log(jnp.sum(jnp.exp(scores - top), axis=-1, keepdims=True))
        log_ref[h] = jnp.broadcast_to(total, (LEN, HD))
        probs = jnp.exp(scores - total).astype(bf16)
        out_ref[:, h * HD : (h + 1) * HD] = dot(probs, value).astype(bf16)


def attend(half, qkv, bias, cos, sin):
    vmem = pl.BlockSpec(memory_space=pltpu.VMEM)
    return pl.pallas_call(
        attend_kernel,
        out_shape=(
            jax.ShapeDtypeStruct((LEN, COLS), bf16),
            jax.ShapeDtypeStruct((LEN, GROUP * HD), bf16),
            jax.ShapeDtypeStruct((GROUP, LEN, HD), f32),
        ),
        in_specs=[pl.BlockSpec(memory_space=pltpu.SMEM)] + [vmem] * 4,
        out_specs=(vmem, vmem, vmem),
        compiler_params=pltpu.CompilerParams(vmem_limit_bytes=32 * 1024 * 1024),
    )(half, qkv, bias, cos, sin)


def attend_back_kernel(half_ref, low_ref, grad_ref, log_ref, cos_ref, sin_ref, out_ref, sum_ref):
    cos, sin = cos_ref[...], sin_ref[...]
    mask = causal_mask(half_ref[0])
    key = low_ref[:, GROUP * HD : (GROUP + 1) * HD]
    value = low_ref[:, (GROUP + 1) * HD :]

    def unrotated(z):
        return (z * cos - pltpu.roll(z, HD // 2, 1) * sin).astype(bf16)

    def put(start, block):
        out_ref[:, start : start + HD] = block
        sum_ref[:, start : start + HD] = jnp.sum(block.astype(f32), axis=0, keepdims=True)

    d_key = jnp.zeros((LEN, HD), f32)
    d_value = jnp.zeros((LEN, HD), f32)
    for h in range(GROUP):
        query = low_ref[:, h * HD : (h + 1) * HD]
        grad = grad_ref[:, h * HD : (h + 1) * HD]
        scores = jnp.where(mask, dot_nt(query, key) * score_scale, -1e30)
        total = log_ref[h]
        probs = jnp.exp(scores - jnp.concatenate([total, total], axis=1))
        d_probs = dot_nt(grad, value)
        delta = jnp.sum(probs * d_probs, axis=-1, keepdims=True)
        d_scores = (probs * (d_probs - delta)).astype(bf16)
        put(h * HD, unrotated(dot(d_scores, key) * score_scale))
        d_key += dot_tn(d_scores, query)
        d_value += dot_tn(probs.astype(bf16), grad)
    put(GROUP * HD, unrotated(d_key * score_scale))
    put((GROUP + 1) * HD, d_value.astype(bf16))


def attend_back(half, low, grad, logs, cos, sin):
    vmem = pl.BlockSpec(memory_space=pltpu.VMEM)
    return pl.pallas_call(
        attend_back_kernel,
        out_shape=(
            jax.ShapeDtypeStruct((LEN, COLS), bf16),
            jax.ShapeDtypeStruct((1, COLS), f32),
        ),
        in_specs=[pl.BlockSpec(memory_space=pltpu.SMEM)] + [vmem] * 5,
        out_specs=(vmem, vmem),
        compiler_params=pltpu.CompilerParams(vmem_limit_bytes=32 * 1024 * 1024),
    )(half, low, grad, logs, cos, sin)


def adam_update(weight, moment_one, moment_two, gradient, step_rate):
    moment_one = 0.9 * moment_one + 0.1 * gradient
    moment_two = 0.95 * moment_two + 0.05 * gradient * gradient
    first_hat = moment_one / (1.0 - 0.9**STEP)
    second_hat = moment_two / (1.0 - 0.95**STEP)
    updated = weight - step_rate * (first_hat / (jnp.sqrt(second_hat) + 1e-08) + 0.1 * weight)
    return (moment_one, moment_two, updated)


def one_hot(rows_of, shift=0):
    row = lax.broadcasted_iota(jnp.int32, (D, D), 0)
    return (row == (rows_of((D, D), 1) + shift) % D).astype(bf16)


def shards(
    inputs,
    cotangent,
    attn_weight,
    attn_moment_one,
    attn_moment_two,
    mlp_weight,
    mlp_moment_one,
    mlp_moment_two,
    vectors,
    vector_moment_one,
    vector_moment_two,
):
    half = lax.axis_index("seq")
    me = lax.axis_index("yh") * 2 + lax.axis_index("core")
    halves = half.astype(jnp.int32).reshape(1)
    x_own, dy_own = inputs[0], cotangent[0]
    x_all = jnp.concatenate([x_own, ring_send(x_own, "seq", 1)], axis=0)

    to_rel = one_hot(gathered_rows)
    to_feat = one_hot(gathered_rows, half * HALF)
    to_mlp = one_hot(mlp_rows)

    attn_low = attn_weight.astype(bf16)
    own_cols = lambda a, start, width: lax.dynamic_slice_in_dim(a, start + half * width, width, 1)
    vec_block = jnp.pad(vectors.astype(bf16)[None, :], ((0, ROWS - 1), (0, 48)))
    proj_block = jnp.concatenate(
        [
            own_cols(attn_low, 0, GROUP * HD),
            own_cols(attn_low, D, HD),
            own_cols(attn_low, D + KV * HD, HD),
            vec_block,
        ],
        axis=1,
    )
    out_block = dot(attn_low[:, QKV:], to_mlp).astype(bf16)
    proj_all = gather_rows(proj_block)
    out_w = gather_rows(out_block)
    proj_w = proj_all[:, :COLS]

    mlp_low = jnp.pad(
        mlp_weight.astype(bf16).reshape(ROWS, 3, FF), ((0, 0), (0, 0), (0, 8 * FFT - FF))
    )
    mlp_half = lax.dynamic_slice_in_dim(mlp_low, half * 4 * FFT, 4 * FFT, 2)
    mlp_blocks = mlp_half.reshape(ROWS, 3, 4, FFT).transpose(2, 0, 1, 3).reshape(4, ROWS, 3 * FFT)
    block = lambda a, i: lax.dynamic_index_in_dim(a, i, 0, keepdims=False)
    mlp_rel = jnp.stack(
        [
            block(mlp_blocks, me),
            ring_send(block(mlp_blocks, me ^ 1), "core", 1),
            ring_send(block(mlp_blocks, me ^ 2), "yh", 1),
            swap_both(block(mlp_blocks, me ^ 3)),
        ]
    )
    mlp_rows_own = jnp.concatenate([block(mlp_rel, me ^ q) for q in range(4)], axis=0)
    mlp_w = lax.all_gather(mlp_rows_own, ("z", "x"), axis=0, tiled=True)

    block_row = lax.broadcasted_iota(jnp.int32, (64, D), 0) * ROWS
    pick = (block_row == gathered_rows((64, D), 1)).astype(bf16)
    vec_all = dot(pick, proj_all[:, COLS:])[:, :80].reshape(1, 5120)
    gain_one = dot(vec_all[:, :D].astype(bf16), to_rel)
    gain_two = dot(vec_all[:, D : 2 * D].astype(bf16), to_mlp)
    bias_all = vec_all[:, 2 * D :]
    bias = jnp.concatenate(
        [
            own_cols(bias_all, 0, GROUP * HD),
            own_cols(bias_all, D, HD),
            own_cols(bias_all, D + KV * HD, HD),
        ],
        axis=1,
    )

    x_rel = dot(x_all, to_rel)
    x_mlp = dot(x_own, to_mlp)
    dy_low = dot(dy_own, to_mlp).astype(bf16)
    dy_all = gather_tokens(dy_low)
    inv_one = lax.rsqrt(jnp.mean(x_rel * x_rel, axis=-1, keepdims=True) + norm_eps)
    unit_one = x_rel * inv_one
    normed = (unit_one * gain_one).astype(bf16)
    cos, sin = rotary_tables((jnp.arange(LEN) + half * TOK) % LEN)
    low, heads_out, logs = attend(halves, dot(normed, proj_w), bias, cos, sin)
    attended = jnp.concatenate(
        [heads_out[:TOK], ring_send(heads_out[TOK:], "seq", 1)], axis=1
    )
    attended_rel = dot(attended, to_feat).astype(bf16)
    middle = x_mlp + dot(attended_rel, out_w)
    inv_two = lax.rsqrt(jnp.mean(middle * middle, axis=-1, keepdims=True) + norm_eps)
    unit_two = middle * inv_two
    second = (unit_two * gain_two).astype(bf16)

    second_all = gather_tokens(second)
    gate_up = dot(second_all, mlp_w[:, : 2 * FFT])
    gate, up = gate_up[:, :FFT], gate_up[:, FFT:]
    sigmoid_gate = jax.nn.sigmoid(gate)
    act = gate * sigmoid_gate
    hidden = (act * up).astype(bf16)
    d_hidden = dot(dy_all, mlp_w[:, 2 * FFT :])
    d_gate = d_hidden * up * (sigmoid_gate * (1.0 + gate * (1.0 - sigmoid_gate)))
    d_gate_up = jnp.concatenate([d_gate, d_hidden * act], axis=1).astype(bf16)
    d_second = reduce_tokens(dot_nt(d_gate_up, mlp_w[:, : 2 * FFT]))
    down = reduce_tokens(dot_nt(hidden, mlp_w[:, 2 * FFT :]))
    output = dot_nt((middle + down).astype(bf16), to_mlp).astype(bf16)[None]
    mlp_term = jnp.concatenate(
        [dot_tn(second_all, d_gate_up).astype(bf16), dot_tn(dy_all, hidden).astype(bf16)], axis=1
    )
    mlp_part = lax.psum_scatter(mlp_term, ("z", "x"), scatter_dimension=0, tiled=True)

    scaled_two = d_second * gain_two
    d_gain_two = jnp.sum(d_second * unit_two, axis=0, keepdims=True)
    d_middle = dy_low.astype(f32) + inv_two * (
        scaled_two - unit_two * jnp.mean(scaled_two * unit_two, axis=-1, keepdims=True)
    )

    d_branch = d_middle.astype(bf16)
    d_attended = dot_nt(dot_nt(d_branch, out_w).astype(bf16), to_feat).astype(bf16)
    d_heads = jnp.concatenate(
        [d_attended[:, :HALF], ring_send(d_attended[:, HALF:], "seq", 1)], axis=0
    )
    d_proj, d_proj_sum = attend_back(halves, low, d_heads, logs, cos, sin)
    d_normed = dot_nt(d_proj, proj_w)
    d_gain_one = jnp.sum(d_normed * unit_one, axis=0, keepdims=True)
    d_normed_own = d_normed[:TOK] + ring_send(d_normed[TOK:].astype(bf16), "seq", 1).astype(f32)
    scaled_one = d_normed_own * gain_one
    unit_own = unit_one[:TOK]
    through_norm = inv_one[:TOK] * (
        scaled_one - unit_own * jnp.mean(scaled_one * unit_own, axis=-1, keepdims=True)
    )
    input_grad = split_dot(d_middle, to_mlp.T) + split_dot(through_norm, to_rel.T)

    bias_zero = jnp.zeros((1, QKV), f32)
    put = lambda a, v, start, width: lax.dynamic_update_slice_in_dim(a, v, start + half * width, 1)
    d_bias = put(bias_zero, d_proj_sum[:, : GROUP * HD], 0, GROUP * HD)
    d_bias = put(d_bias, d_proj_sum[:, GROUP * HD : (GROUP + 1) * HD], D, HD)
    d_bias = put(d_bias, d_proj_sum[:, (GROUP + 1) * HD :], D + KV * HD, HD)
    vec_term = jnp.concatenate(
        [split_dot(d_gain_one, to_rel.T), split_dot(d_gain_two, to_mlp.T), d_bias], axis=1
    )
    vec_term = jnp.pad(vec_term.reshape(64, 80).astype(bf16), ((0, 0), (0, 48)))
    proj_part = reduce_rows(
        jnp.concatenate([dot_tn(normed, d_proj), dot_tn(pick, vec_term)], axis=1)
    )
    out_part = reduce_rows(dot_tn(attended_rel, d_branch))

    proj_low, out_low = proj_part.astype(bf16), out_part.astype(bf16)
    proj_other = ring_send(proj_low, "seq", 1)
    out_grad = out_low.astype(f32) + ring_send(out_low, "seq", 1).astype(f32)
    vec_grad = (proj_low[:1, COLS : COLS + 80].astype(f32) + proj_other[:1, COLS : COLS + 80].astype(f32))[0]
    first = jnp.where(half == 0, proj_low, proj_other).astype(f32)
    last = jnp.where(half == 0, proj_other, proj_low).astype(f32)
    query_end, key_end = GROUP * HD, (GROUP + 1) * HD
    attn_grad = jnp.concatenate(
        [
            first[:, :query_end],
            last[:, :query_end],
            first[:, query_end:key_end],
            last[:, query_end:key_end],
            first[:, key_end:COLS],
            last[:, key_end:COLS],
            split_dot(out_grad, to_mlp.T),
        ],
        axis=1,
    )

    mlp_parts = mlp_part.reshape(4, ROWS, 3 * FFT)
    grad_rel = jnp.stack(
        [
            block(mlp_parts, me),
            ring_send(block(mlp_parts, me ^ 1), "core", 1),
            ring_send(block(mlp_parts, me ^ 2), "yh", 1),
            swap_both(block(mlp_parts, me ^ 3)),
        ]
    )
    grad_half = jnp.stack([block(grad_rel, me ^ q) for q in range(4)])
    grad_other = ring_send(grad_half, "seq", 1)
    grad_all = jnp.concatenate(
        [jnp.where(half == 0, grad_half, grad_other), jnp.where(half == 0, grad_other, grad_half)]
    )
    mlp_grad = (
        grad_all.reshape(8, ROWS, 3, FFT)
        .transpose(1, 2, 0, 3)
        .reshape(ROWS, 3, 8 * FFT)[:, :, :FF]
        .reshape(ROWS, 3 * FF)
        .astype(f32)
    )

    attn_one, attn_two, attn_new = adam_update(
        attn_weight, attn_moment_one, attn_moment_two, attn_grad, 0.05
    )
    mlp_one, mlp_two, mlp_new = adam_update(
        mlp_weight, mlp_moment_one, mlp_moment_two, mlp_grad, 0.02
    )
    vec_one, vec_two, vec_new = adam_update(
        vectors, vector_moment_one, vector_moment_two, vec_grad, 0.5
    )
    return (
        output,
        input_grad[None],
        attn_one,
        attn_two,
        attn_new,
        mlp_one,
        mlp_two,
        mlp_new,
        vec_one,
        vec_two,
        vec_new,
    )


def solution(mesh):
    grid = Mesh(mesh.devices.reshape(2, 4, 2, 4, 2), ("seq",) + FSDP)
    tokens, rows, vector = P(FSDP, "seq", None), P(FSDP, None), P(FSDP)
    return jax.shard_map(
        shards,
        mesh=grid,
        in_specs=(tokens, tokens) + (rows,) * 6 + (vector,) * 3,
        out_specs=(tokens, tokens) + (rows,) * 6 + (vector,) * 3,
        check_vma=False,
    )
```

```python
import jax
import jax.numpy as jnp
from jax import lax
from jax.experimental import pallas as pl
from jax.experimental.pallas import tpu as pltpu
from jax.sharding import Mesh
from jax.sharding import PartitionSpec as P

D = 1536
H = 12
KV = 2
HD = 128
FF = 8960
STEP = 10
QKV = 2048
ROWS = 24
TOK = 128
LEN = 256
HALF = D // 2
GROUP = H // KV
COLS = GROUP * HD + 2 * HD
FFT = 1152

norm_eps = 1e-06
rope_base = 1000000.0
f32 = jnp.float32
bf16 = jnp.bfloat16
contract_rows = (((0,), (0,)), ((), ()))
contract_cols = (((1,), (1,)), ((), ()))
score_scale = HD ** (-0.5)
FSDP = ("z", "yh", "x", "core")


def dot(a, b):
    return jnp.dot(a, b, preferred_element_type=f32)


def dot_tn(a, b):
    return lax.dot_general(a, b, contract_rows, preferred_element_type=f32)


def dot_nt(a, b):
    return lax.dot_general(a, b, contract_cols, preferred_element_type=f32)


def split_dot(a, b):
    high = a.astype(bf16)
    low = (a - high.astype(f32)).astype(bf16)
    return dot(high, b) + dot(low, b)


def ring_send(values, axis, shift):
    size = {"z": 4, "x": 4, "yh": 2, "core": 2, "seq": 2}[axis]
    return lax.ppermute(values, axis, [(i, (i + shift) % size) for i in range(size)])


def y_send(values, shift):
    place = lambda y: (y % 2) * 2 + y // 2
    return lax.ppermute(
        values, ("seq", "yh"), [(place(i), place((i + shift) % 4)) for i in range(4)]
    )


def cross_send(values):
    return lax.ppermute(values, ("seq", "yh"), [(i, 3 - i) for i in range(4)])


def core_send(values):
    return ring_send(values, "core", 1)


def seq_send(values):
    return ring_send(values, "seq", 1)


def hold_kernel(*refs):
    pass


def hold(values, *after):
    anywhere = pl.BlockSpec(memory_space=pl.ANY)
    return pl.pallas_call(
        hold_kernel,
        out_shape=jax.ShapeDtypeStruct(values.shape, values.dtype),
        in_specs=[anywhere] * (1 + len(after)),
        out_specs=anywhere,
        input_output_aliases={0: 0},
    )(values, *after)


def ring_gather(values, send):
    return jnp.concatenate([values, send(values, 1), send(values, -1), send(values, 2)], axis=0)


def ring_reduce(values, send):
    rows = values.shape[0] // 4
    parts = [values[i * rows : (i + 1) * rows] for i in range(4)]
    low = [p.astype(bf16) for p in parts]
    got = [send(low[1], -1), send(low[2], 1), send(low[3], 2)]
    return parts[0] + got[0].astype(f32) + got[1].astype(f32) + got[2].astype(f32)


def pair_reduce(values, send):
    rows = values.shape[0] // 2
    return values[:rows] + send(values[rows:].astype(bf16)).astype(f32)


def z_send(values, shift):
    return ring_send(values, "z", shift)


def x_send(values, shift):
    return ring_send(values, "x", shift)


def both(values, send):
    return jnp.concatenate([values, send(values)], axis=0)


def gather_tokens(values):
    return both(ring_gather(values, y_send), core_send)


def reduce_tokens(values):
    return ring_reduce(pair_reduce(values, core_send), y_send)


def near(index):
    return jnp.where(index == 1, -1, jnp.where(index == 0, 0, index - 1))


def gathered_rows(shape, dim):
    j = lax.broadcasted_iota(jnp.int32, shape, dim)
    r, xi, yi, zi, ci = j % 24, (j // 24) % 4, (j // 96) % 2, (j // 192) % 4, j // 768
    z = (lax.axis_index("z") + near(zi) + 4) % 4
    x = (lax.axis_index("x") + near(xi) + 4) % 4
    yh = (lax.axis_index("yh") + yi) % 2
    core = (lax.axis_index("core") + ci) % 2
    return z * 384 + yh * 192 + x * 48 + core * 24 + r


def mlp_rows(shape, dim):
    j = lax.broadcasted_iota(jnp.int32, shape, dim)
    r, core, yh, x, z = j % 24, (j // 24) % 2, (j // 48) % 2, (j // 96) % 4, j // 384
    return z * 384 + yh * 192 + x * 48 + core * 24 + r


def rotary_tables(positions):
    half_dim = HD // 2
    freqs = rope_base ** (-jnp.arange(half_dim, dtype=f32) * 2.0 / HD)
    angles = positions.astype(f32)[:, None] * freqs[None, :]
    cos, sin = jnp.cos(angles), jnp.sin(angles)
    return jnp.concatenate([cos, cos], axis=1), jnp.concatenate([-sin, sin], axis=1)


def causal_mask(half):
    row = (lax.broadcasted_iota(jnp.int32, (LEN, LEN), 0) + half * TOK) % LEN
    col = (lax.broadcasted_iota(jnp.int32, (LEN, LEN), 1) + half * TOK) % LEN
    return row >= col


def attend_kernel(half_ref, qkv_ref, bias_ref, cos_ref, sin_ref, low_ref, out_ref, log_ref):
    cos, sin = cos_ref[...], sin_ref[...]
    mask = causal_mask(half_ref[0])

    def rotated(start):
        z = qkv_ref[:, start : start + HD] + bias_ref[:, start : start + HD]
        return (z * cos + pltpu.roll(z, HD // 2, 1) * sin).astype(bf16)

    key = rotated(GROUP * HD)
    low_ref[:, GROUP * HD : (GROUP + 1) * HD] = key
    value = (qkv_ref[:, (GROUP + 1) * HD :] + bias_ref[:, (GROUP + 1) * HD :]).astype(bf16)
    low_ref[:, (GROUP + 1) * HD :] = value
    for h in range(GROUP):
        query = rotated(h * HD)
        low_ref[:, h * HD : (h + 1) * HD] = query
        scores = jnp.where(mask, dot_nt(query, key) * score_scale, -1e30)
        top = jnp.max(scores, axis=-1, keepdims=True)
        total = top + jnp.log(jnp.sum(jnp.exp(scores - top), axis=-1, keepdims=True))
        log_ref[h] = jnp.broadcast_to(total, (LEN, HD))
        probs = jnp.exp(scores - total).astype(bf16)
        out_ref[:, h * HD : (h + 1) * HD] = dot(probs, value).astype(bf16)


def attend(half, qkv, bias, cos, sin):
    vmem = pl.BlockSpec(memory_space=pltpu.VMEM)
    return pl.pallas_call(
        attend_kernel,
        out_shape=(
            jax.ShapeDtypeStruct((LEN, COLS), bf16),
            jax.ShapeDtypeStruct((LEN, GROUP * HD), bf16),
            jax.ShapeDtypeStruct((GROUP, LEN, HD), f32),
        ),
        in_specs=[pl.BlockSpec(memory_space=pltpu.SMEM)] + [vmem] * 4,
        out_specs=(vmem, vmem, vmem),
        compiler_params=pltpu.CompilerParams(vmem_limit_bytes=32 * 1024 * 1024),
    )(half, qkv, bias, cos, sin)


def attend_back_kernel(half_ref, low_ref, grad_ref, log_ref, cos_ref, sin_ref, out_ref, sum_ref):
    cos, sin = cos_ref[...], sin_ref[...]
    mask = causal_mask(half_ref[0])
    key = low_ref[:, GROUP * HD : (GROUP + 1) * HD]
    value = low_ref[:, (GROUP + 1) * HD :]

    def unrotated(z):
        return (z * cos - pltpu.roll(z, HD // 2, 1) * sin).astype(bf16)

    def put(start, block):
        out_ref[:, start : start + HD] = block
        sum_ref[:, start : start + HD] = jnp.sum(block.astype(f32), axis=0, keepdims=True)

    d_key = jnp.zeros((LEN, HD), f32)
    d_value = jnp.zeros((LEN, HD), f32)
    for h in range(GROUP):
        query = low_ref[:, h * HD : (h + 1) * HD]
        grad = grad_ref[:, h * HD : (h + 1) * HD]
        scores = jnp.where(mask, dot_nt(query, key) * score_scale, -1e30)
        total = log_ref[h]
        probs = jnp.exp(scores - jnp.concatenate([total, total], axis=1))
        d_probs = dot_nt(grad, value)
        delta = jnp.sum(probs * d_probs, axis=-1, keepdims=True)
        d_scores = (probs * (d_probs - delta)).astype(bf16)
        put(h * HD, unrotated(dot(d_scores, key) * score_scale))
        d_key += dot_tn(d_scores, query)
        d_value += dot_tn(probs.astype(bf16), grad)
    put(GROUP * HD, unrotated(d_key * score_scale))
    put((GROUP + 1) * HD, d_value.astype(bf16))


def attend_back(half, low, grad, logs, cos, sin):
    vmem = pl.BlockSpec(memory_space=pltpu.VMEM)
    return pl.pallas_call(
        attend_back_kernel,
        out_shape=(
            jax.ShapeDtypeStruct((LEN, COLS), bf16),
            jax.ShapeDtypeStruct((1, COLS), f32),
        ),
        in_specs=[pl.BlockSpec(memory_space=pltpu.SMEM)] + [vmem] * 5,
        out_specs=(vmem, vmem),
        compiler_params=pltpu.CompilerParams(vmem_limit_bytes=32 * 1024 * 1024),
    )(half, low, grad, logs, cos, sin)


def cut_kernel(rank_ref, weight_ref, keep_ref, send_ref):
    col = lax.broadcasted_iota(jnp.int32, (ROWS, FFT), 1)
    for ref, i, flip in ((keep_ref, 0, 0), (keep_ref, 1, 6), (send_ref, 0, 1), (send_ref, 1, 7)):
        rank = rank_ref[0] ^ flip
        start = jnp.minimum(rank * FFT, FF - FFT)
        inside = col >= rank * FFT - start
        for k in range(3):
            piece = weight_ref[:, pl.ds(pl.multiple_of(k * FF + start, 128), FFT)]
            ref[i, :, k * FFT : (k + 1) * FFT] = jnp.where(inside, piece, 0.0).astype(bf16)


def cut(rank, weight):
    vmem = pl.BlockSpec(memory_space=pltpu.VMEM)
    block = jax.ShapeDtypeStruct((2, ROWS, 3 * FFT), bf16)
    return pl.pallas_call(
        cut_kernel,
        out_shape=(block, block),
        in_specs=[pl.BlockSpec(memory_space=pltpu.SMEM), vmem],
        out_specs=(vmem, vmem),
        compiler_params=pltpu.CompilerParams(vmem_limit_bytes=32 * 1024 * 1024),
    )(rank, weight)


def adam_update(weight, moment_one, moment_two, gradient, step_rate):
    moment_one = 0.9 * moment_one + 0.1 * gradient
    moment_two = 0.95 * moment_two + 0.05 * gradient * gradient
    first_hat = moment_one / (1.0 - 0.9**STEP)
    second_hat = moment_two / (1.0 - 0.95**STEP)
    updated = weight - step_rate * (first_hat / (jnp.sqrt(second_hat) + 1e-08) + 0.1 * weight)
    return (moment_one, moment_two, updated)


def one_hot(rows_of, shift=0):
    row = lax.broadcasted_iota(jnp.int32, (D, D), 0)
    return (row == (rows_of((D, D), 1) + shift) % D).astype(bf16)


def shards(
    inputs,
    cotangent,
    attn_weight,
    attn_moment_one,
    attn_moment_two,
    mlp_weight,
    mlp_moment_one,
    mlp_moment_two,
    vectors,
    vector_moment_one,
    vector_moment_two,
):
    half = lax.axis_index("seq")
    yh, core = lax.axis_index("yh"), lax.axis_index("core")
    side = half ^ yh
    rank = half * 4 + yh * 2 + core
    halves = half.astype(jnp.int32).reshape(1)
    x_own, dy_own = inputs[0], cotangent[0]
    ordered = lambda index, a, b: jnp.where(index == 0, jnp.stack([a, b]), jnp.stack([b, a]))

    mlp_keep, mlp_give = cut(rank.astype(jnp.int32).reshape(1), mlp_weight)
    mlp_got = core_send(mlp_give)
    mlp_cores = ordered(core, mlp_keep, mlp_got)
    mlp_block = ordered(yh, mlp_cores[:, 0], cross_send(mlp_cores[:, 1]))
    mlp_w = lax.all_gather(mlp_block.reshape(4 * ROWS, 3 * FFT), ("z", "x"), axis=0, tiled=True)

    x_all = both(x_own, seq_send)

    to_rel = one_hot(gathered_rows)
    to_feat = one_hot(gathered_rows, side * HALF)
    to_mlp = one_hot(mlp_rows)

    attn_low = attn_weight.astype(bf16)
    own_cols = lambda a, start, width: lax.dynamic_slice_in_dim(a, start + side * width, width, 1)
    vec_block = jnp.pad(vectors.astype(bf16)[None, :], ((0, ROWS - 1), (0, 48)))
    attn_block = jnp.concatenate(
        [
            own_cols(attn_low, 0, GROUP * HD),
            own_cols(attn_low, D, HD),
            own_cols(attn_low, D + KV * HD, HD),
            vec_block,
            dot(attn_low[:, QKV:], to_mlp).astype(bf16),
        ],
        axis=1,
    )
    attn_x = ring_gather(attn_block, x_send)
    proj_z = ring_gather(both(attn_x[:, : COLS + HD], cross_send), z_send)
    proj_all = both(proj_z, core_send)
    out_x = hold(attn_x[:, COLS + HD :], proj_z)
    out_w = both(ring_gather(both(out_x, cross_send), z_send), core_send)
    proj_w = proj_all[:, :COLS]

    block_row = lax.broadcasted_iota(jnp.int32, (64, D), 0) * ROWS
    pick = (block_row == gathered_rows((64, D), 1)).astype(bf16)
    vec_all = dot(pick, proj_all[:, COLS:])[:, :80].reshape(1, 5120)
    gain_one = dot(vec_all[:, :D].astype(bf16), to_rel)
    gain_two = dot(vec_all[:, D : 2 * D].astype(bf16), to_mlp)
    bias_all = vec_all[:, 2 * D :]
    bias = jnp.concatenate(
        [
            own_cols(bias_all, 0, GROUP * HD),
            own_cols(bias_all, D, HD),
            own_cols(bias_all, D + KV * HD, HD),
        ],
        axis=1,
    )

    x_rel = dot(x_all, to_rel)
    x_mlp = dot(x_own, to_mlp)
    dy_low = dot(dy_own, to_mlp).astype(bf16)
    dy_all = gather_tokens(hold(dy_low, proj_z))
    inv_one = lax.rsqrt(jnp.mean(x_rel * x_rel, axis=-1, keepdims=True) + norm_eps)
    unit_one = x_rel * inv_one
    normed = (unit_one * gain_one).astype(bf16)
    cos, sin = rotary_tables((jnp.arange(LEN) + half * TOK) % LEN)
    low, heads_out, logs = attend(halves, dot(normed, proj_w), bias, cos, sin)
    attended = jnp.concatenate(
        [heads_out[:TOK], seq_send(heads_out[TOK:])], axis=1
    )
    attended_rel = dot(attended, to_feat).astype(bf16)
    middle = x_mlp + dot(attended_rel, out_w)
    inv_two = lax.rsqrt(jnp.mean(middle * middle, axis=-1, keepdims=True) + norm_eps)
    unit_two = middle * inv_two
    second = (unit_two * gain_two).astype(bf16)

    second_all = gather_tokens(second)
    gate_up = dot(second_all, mlp_w[:, : 2 * FFT])
    gate, up = gate_up[:, :FFT], gate_up[:, FFT:]
    sigmoid_gate = jax.nn.sigmoid(gate)
    act = gate * sigmoid_gate
    hidden = (act * up).astype(bf16)
    d_hidden = dot(dy_all, mlp_w[:, 2 * FFT :])
    d_gate = d_hidden * up * (sigmoid_gate * (1.0 + gate * (1.0 - sigmoid_gate)))
    d_gate_up = jnp.concatenate([d_gate, d_hidden * act], axis=1).astype(bf16)
    mlp_term = jnp.concatenate(
        [dot_tn(second_all, d_gate_up).astype(bf16), dot_tn(dy_all, hidden).astype(bf16)], axis=1
    )
    mlp_part = lax.psum_scatter(mlp_term, ("z", "x"), scatter_dimension=0, tiled=True)
    d_second = reduce_tokens(dot_nt(hold(d_gate_up, mlp_term), mlp_w[:, : 2 * FFT]))
    down = reduce_tokens(dot_nt(hold(hidden, d_second), mlp_w[:, 2 * FFT :]))
    output = dot_nt((middle + down).astype(bf16), to_mlp).astype(bf16)[None]

    scaled_two = d_second * gain_two
    d_gain_two = jnp.sum(d_second * unit_two, axis=0, keepdims=True)
    d_middle = dy_low.astype(f32) + inv_two * (
        scaled_two - unit_two * jnp.mean(scaled_two * unit_two, axis=-1, keepdims=True)
    )

    d_branch = d_middle.astype(bf16)
    d_attended = dot_nt(dot_nt(d_branch, out_w).astype(bf16), to_feat).astype(bf16)
    d_heads = jnp.concatenate(
        [d_attended[:, :HALF], seq_send(d_attended[:, HALF:])], axis=0
    )
    d_proj, d_proj_sum = attend_back(halves, low, d_heads, logs, cos, sin)
    d_normed = dot_nt(d_proj, proj_w)
    d_gain_one = jnp.sum(d_normed * unit_one, axis=0, keepdims=True)
    d_normed_own = d_normed[:TOK] + seq_send(d_normed[TOK:].astype(bf16)).astype(f32)
    scaled_one = d_normed_own * gain_one
    unit_own = unit_one[:TOK]
    through_norm = inv_one[:TOK] * (
        scaled_one - unit_own * jnp.mean(scaled_one * unit_own, axis=-1, keepdims=True)
    )
    input_grad = split_dot(d_middle, to_mlp.T) + split_dot(through_norm, to_rel.T)

    bias_zero = jnp.zeros((1, QKV), f32)
    put = lambda a, v, start, width: lax.dynamic_update_slice_in_dim(a, v, start + side * width, 1)
    d_bias = put(bias_zero, d_proj_sum[:, : GROUP * HD], 0, GROUP * HD)
    d_bias = put(d_bias, d_proj_sum[:, GROUP * HD : (GROUP + 1) * HD], D, HD)
    d_bias = put(d_bias, d_proj_sum[:, (GROUP + 1) * HD :], D + KV * HD, HD)
    vec_term = jnp.concatenate(
        [split_dot(d_gain_one, to_rel.T), split_dot(d_gain_two, to_mlp.T), d_bias], axis=1
    )
    vec_term = jnp.pad(vec_term.reshape(64, 80).astype(bf16), ((0, 0), (0, 48)))
    out_term = pair_reduce(dot_tn(attended_rel, d_branch), core_send)
    out_term = pair_reduce(ring_reduce(out_term, z_send), cross_send)
    proj_term = jnp.concatenate([dot_tn(normed, d_proj), dot_tn(pick, vec_term)], axis=1)
    proj_term = pair_reduce(proj_term, core_send)
    proj_term = pair_reduce(ring_reduce(proj_term, z_send), cross_send)
    attn_part = ring_reduce(jnp.concatenate([proj_term, out_term], axis=1), x_send).astype(bf16)

    attn_other = seq_send(attn_part)
    out_grad = attn_part[:, COLS + HD :].astype(f32) + attn_other[:, COLS + HD :].astype(f32)
    vec_cols = slice(COLS, COLS + 80)
    vec_grad = attn_part[0, vec_cols].astype(f32) + attn_other[0, vec_cols].astype(f32)
    first = jnp.where(side == 0, attn_part, attn_other).astype(f32)
    last = jnp.where(side == 0, attn_other, attn_part).astype(f32)
    query_end, key_end = GROUP * HD, (GROUP + 1) * HD
    attn_grad = jnp.concatenate(
        [
            first[:, :query_end],
            last[:, :query_end],
            first[:, query_end:key_end],
            last[:, query_end:key_end],
            first[:, key_end:COLS],
            last[:, key_end:COLS],
            split_dot(out_grad, to_mlp.T),
        ],
        axis=1,
    )

    by_core = mlp_part.reshape(2, 2, ROWS, 3 * FFT)
    of_core = lambda c: lax.dynamic_index_in_dim(by_core, c, 1, keepdims=False)
    pair = jnp.stack([of_core(core), core_send(of_core(1 - core))], axis=1)
    near_rows = lax.dynamic_index_in_dim(pair, yh, 0, keepdims=False)
    far_rows = lax.dynamic_index_in_dim(pair, 1 - yh, 0, keepdims=False)
    by_flip = jnp.concatenate(
        [near_rows, ring_send(far_rows, "yh", 1), seq_send(near_rows), cross_send(far_rows)]
    )
    by_rank = [lax.dynamic_index_in_dim(by_flip, rank ^ r, 0, keepdims=False) for r in range(8)]
    by_rank = [p.reshape(ROWS, 3, FFT) for p in by_rank]
    by_rank[7] = by_rank[7][:, :, 8 * FFT - FF :]
    mlp_grad = jnp.concatenate(by_rank, axis=2).reshape(ROWS, 3 * FF).astype(f32)

    attn_one, attn_two, attn_new = adam_update(
        attn_weight, attn_moment_one, attn_moment_two, attn_grad, 0.05
    )
    mlp_one, mlp_two, mlp_new = adam_update(
        mlp_weight, mlp_moment_one, mlp_moment_two, mlp_grad, 0.02
    )
    vec_one, vec_two, vec_new = adam_update(
        vectors, vector_moment_one, vector_moment_two, vec_grad, 0.5
    )
    return (
        output,
        input_grad[None],
        attn_one,
        attn_two,
        attn_new,
        mlp_one,
        mlp_two,
        mlp_new,
        vec_one,
        vec_two,
        vec_new,
    )


def solution(mesh):
    grid = Mesh(mesh.devices.reshape(2, 4, 2, 4, 2), ("seq",) + FSDP)
    tokens, rows, vector = P(FSDP, "seq", None), P(FSDP, None), P(FSDP)
    return jax.shard_map(
        shards,
        mesh=grid,
        in_specs=(tokens, tokens) + (rows,) * 6 + (vector,) * 3,
        out_specs=(tokens, tokens) + (rows,) * 6 + (vector,) * 3,
        check_vma=False,
    )
```

```python
import jax
import jax.numpy as jnp
from jax import lax
from jax.experimental import pallas as pl
from jax.experimental.pallas import tpu as pltpu
from jax.sharding import Mesh
from jax.sharding import PartitionSpec as P

D = 1536
H = 12
KV = 2
HD = 128
FF = 8960
STEP = 10
QKV = 2048
ROWS = 24
TOK = 128
LEN = 256
HALF = D // 2
GROUP = H // KV
QUERY = GROUP * HD
COLS = QUERY + 2 * HD
FFT = 1152
UNIT = FFT // 3
PIECE = D // 4
MIB = 1024 * 1024

norm_eps = 1e-06
rope_base = 1000000.0
f32 = jnp.float32
bf16 = jnp.bfloat16
contract_rows = (((0,), (0,)), ((), ()))
contract_cols = (((1,), (1,)), ((), ()))
score_scale = HD ** (-0.5)
FSDP = ("z", "yh", "x", "core")
SIZES = {"seq": 2, "z": 4, "yh": 2, "x": 4, "core": 2}


def dot(a, b):
    return jnp.dot(a, b, preferred_element_type=f32)


def dot_tn(a, b):
    return lax.dot_general(a, b, contract_rows, preferred_element_type=f32)


def dot_nt(a, b):
    return lax.dot_general(a, b, contract_cols, preferred_element_type=f32)


def split_dot(a, b):
    high = a.astype(bf16)
    low = (a - high.astype(f32)).astype(bf16)
    return dot_nt(high, b) + dot_nt(low, b)


def ring_send(values, axis, shift):
    size = SIZES[axis]
    return lax.ppermute(values, axis, [(i, (i + shift) % size) for i in range(size)])


def x_send(values, shift):
    return ring_send(values, "x", shift)


def z_send(values, shift):
    return ring_send(values, "z", shift)


def y_send(values, shift):
    place = lambda y: (y % 2) * 2 + y // 2
    return lax.ppermute(
        values, ("seq", "yh"), [(place(i), place((i + shift) % 4)) for i in range(4)]
    )


def cross_send(values):
    return lax.ppermute(values, ("seq", "yh"), [(i, 3 - i) for i in range(4)])


def core_send(values):
    return ring_send(values, "core", 1)


def seq_send(values):
    return ring_send(values, "seq", 1)


def ring_parts(values, send):
    return [values, send(values, 1), send(values, -1), send(values, 2)]


def pair_reduce(values, send):
    rows = values.shape[0] // 2
    return values[:rows] + send(values[rows:].astype(bf16)).astype(f32)


def ring_collect(parts, send):
    return [parts[0], send(parts[1], -1), send(parts[2], 1), send(parts[3], 2)]


def gather_tokens(values):
    parts = ring_parts(values, y_send)
    return parts + [core_send(p) for p in parts]


def near(index):
    return jnp.where(index == 1, -1, jnp.where(index == 0, 0, index - 1))


def gathered_blocks(count):
    j = jnp.arange(count, dtype=jnp.int32)
    xi, zi, yi, ci = j % 4, (j // 4) % 4, (j // 16) % 2, j // 32
    z = (lax.axis_index("z") + near(zi) + 4) % 4
    x = (lax.axis_index("x") + near(xi) + 4) % 4
    yh = (lax.axis_index("yh") + yi) % 2
    core = (lax.axis_index("core") + ci) % 2
    return z * 16 + yh * 8 + x * 2 + core


def call(
    kernel, outs, *args, us=1, smem=0, in_hbm=(), outs_hbm=False, scratch=(), limit=8, after=()
):
    vmem, hbm = pl.BlockSpec(memory_space=pltpu.VMEM), pl.BlockSpec(memory_space=pltpu.HBM)
    specs = [
        pl.BlockSpec(memory_space=pltpu.SMEM) if i < smem else hbm if i in in_hbm else vmem
        for i in range(len(args))
    ] + [pl.BlockSpec(memory_space=pl.ANY)] * len(after)
    used = len(args)
    args = [
        pltpu.with_memory_space_constraint(a, pltpu.HBM) if i in in_hbm else a
        for i, a in enumerate(args)
    ]
    place = pltpu.HBM if outs_hbm else jax.ShapeDtypeStruct
    return pl.pallas_call(
        lambda *refs: kernel(*refs[:used], *refs[used + len(after) :]),
        out_shape=tuple(place(shape, kind) for shape, kind in outs),
        in_specs=specs,
        out_specs=(hbm if outs_hbm else vmem,) * len(outs),
        scratch_shapes=list(scratch),
        cost_estimate=pl.CostEstimate(flops=us * 10**7, bytes_accessed=us * 10**4, transcendentals=0),
        compiler_params=pltpu.CompilerParams(vmem_limit_bytes=limit * MIB),
    )(*args, *after)


def hold_kernel(*refs):
    pass


def hold(values, *after):
    anywhere = pl.BlockSpec(memory_space=pl.ANY)
    return pl.pallas_call(
        hold_kernel,
        out_shape=jax.ShapeDtypeStruct(values.shape, values.dtype),
        in_specs=[anywhere] * (1 + len(after)),
        out_specs=anywhere,
        input_output_aliases={0: 0},
    )(values, *after)


def join_kernel(*refs):
    out_ref, row = refs[-1], 0
    for ref in refs[:-1]:
        out_ref[row : row + ref.shape[0], :] = ref[...]
        row += ref.shape[0]


def join(parts, after=()):
    rows = sum(p.shape[0] for p in parts)
    return call(join_kernel, [((rows, parts[0].shape[1]), bf16)], *parts, after=after)[0]


def sum_kernel(count, given, outs):
    groups = []
    for i in range(0, len(given), count):
        total = given[i][...].astype(f32)
        for ref in given[i + 1 : i + count]:
            total = total + ref[...].astype(f32)
        groups.append(total)
    rows, col = outs[0].shape[0], 0
    for total in groups:
        for i, ref in enumerate(outs):
            part = total[i * rows : (i + 1) * rows, :]
            ref[:, col : col + total.shape[1]] = part.astype(ref.dtype)
        col += total.shape[1]


def add_up(parts, pieces=1, count=None, after=()):
    count = count or len(parts)
    cols = sum(p.shape[1] for p in parts[::count])
    outs = [((parts[0].shape[0] // pieces, cols), bf16)] * pieces
    kernel = lambda *refs: sum_kernel(count, refs[: len(parts)], refs[len(parts) :])
    return call(kernel, outs, *parts, after=after)


def place_kernel(rows_ref, out_ref):
    row = lax.broadcasted_iota(jnp.int32, (D, PIECE), 0)
    for i in range(4):
        cols = slice(i * PIECE, (i + 1) * PIECE)
        out_ref[:, cols] = jnp.where(row == rows_ref[:1, cols], 1.0, 0.0).astype(bf16)


def one_hot(rows):
    return call(place_kernel, [((D, D), bf16)], jnp.broadcast_to(rows[None, :], (8, D)))[0]


def rotary_tables(positions):
    half_dim = HD // 2
    freqs = rope_base ** (-jnp.arange(half_dim, dtype=f32) * 2.0 / HD)
    angles = positions.astype(f32)[:, None] * freqs[None, :]
    cos, sin = jnp.cos(angles), jnp.sin(angles)
    return jnp.concatenate([cos, cos], axis=1), jnp.concatenate([-sin, sin], axis=1)


def causal_mask(half):
    row = (lax.broadcasted_iota(jnp.int32, (LEN, LEN), 0) + half * TOK) % LEN
    col = (lax.broadcasted_iota(jnp.int32, (LEN, LEN), 1) + half * TOK) % LEN
    return row >= col


def norm_scale(values):
    return lax.rsqrt(jnp.mean(values * values, axis=-1, keepdims=True) + norm_eps)


def attend_kernel(
    half_ref, x_ref, gain_ref, w0, w1, w2, w3, bias_ref, cos_ref, sin_ref,
    normed_ref, low_ref, own_ref, give_ref, log_ref, qkv_ref,
):
    x = x_ref[...].astype(f32)
    normed_ref[...] = (x * norm_scale(x) * gain_ref[...]).astype(bf16)
    total = bias_ref[...]
    for i, w in enumerate((w0, w1, w2, w3)):
        total = total + dot(normed_ref[:, i * PIECE : (i + 1) * PIECE], w[:, :COLS])
    qkv_ref[...] = total
    cos, sin = cos_ref[...], sin_ref[...]
    mask = causal_mask(half_ref[0])

    def rotated(start):
        z = qkv_ref[:, start : start + HD]
        return (z * cos + pltpu.roll(z, HD // 2, 1) * sin).astype(bf16)

    key = rotated(QUERY)
    low_ref[:, QUERY : QUERY + HD] = key
    value = qkv_ref[:, QUERY + HD :].astype(bf16)
    low_ref[:, QUERY + HD :] = value
    for h in range(GROUP):
        query = rotated(h * HD)
        low_ref[:, h * HD : (h + 1) * HD] = query
        scores = jnp.where(mask, dot_nt(query, key) * score_scale, -1e30)
        top = jnp.max(scores, axis=-1, keepdims=True)
        total = top + jnp.log(jnp.sum(jnp.exp(scores - top), axis=-1, keepdims=True))
        log_ref[h] = jnp.broadcast_to(total, (LEN, HD))
        probs = jnp.exp(scores - total).astype(bf16)
        out = dot(probs, value).astype(bf16)
        own_ref[:, h * HD : (h + 1) * HD] = out[:TOK, :]
        give_ref[:, h * HD : (h + 1) * HD] = out[TOK:, :]


def attend(half, x_rel, gain, proj, bias, cos, sin, after):
    outs = [
        ((LEN, D), bf16),
        ((LEN, COLS), bf16),
        ((TOK, QUERY), bf16),
        ((TOK, QUERY), bf16),
        ((GROUP, LEN, HD), f32),
    ]
    scratch = [pltpu.VMEM((LEN, COLS), f32)]
    return call(
        attend_kernel, outs, half, x_rel, gain, *proj, bias, cos, sin, us=5, smem=1, scratch=scratch, after=after
    )


def branch_kernel(
    x_ref, a0_ref, a1_ref, place_ref, w0, w1, w2, w3, gain_ref, rel_ref, middle_ref, second_ref
):
    middle = x_ref[...].astype(f32)
    for i, w in enumerate((w0, w1, w2, w3)):
        cols = slice(i * PIECE, (i + 1) * PIECE)
        rel = dot(a0_ref[...], place_ref[:HALF, cols]) + dot(a1_ref[...], place_ref[HALF:, cols])
        rel_ref[:, cols] = rel.astype(bf16)
        middle = middle + dot(rel_ref[:, cols], w[...])
    middle_ref[...] = middle
    second_ref[...] = (middle * norm_scale(middle) * gain_ref[...]).astype(bf16)


def branch(x, a0, a1, place, out_w, gain):
    outs = [((TOK, D), bf16), ((TOK, D), f32), ((TOK, D), bf16)]
    return call(branch_kernel, outs, x, a0, a1, place, *out_w, gain, us=4)


def ff_kernel(*refs):
    h_parts, dy_parts, refs = refs[:8], refs[8:16], refs[16:]
    w_ref, hid_out, dgu_out, term_ref, h_all, dy_all, w, hid, dgu, in_sem, w_sem, out_sem, t_sem = refs
    tokens = []
    for k, (parts, whole) in enumerate(((h_parts, h_all), (dy_parts, dy_all))):
        for i, part in enumerate(parts):
            copy = pltpu.make_async_copy(part, whole.at[pl.ds(i * TOK, TOK), :], in_sem.at[k, i])
            copy.start()
            tokens.append(copy)
    loads = []
    for j in range(3):
        for k, (start, width) in enumerate(((2 * UNIT * j, 2 * UNIT), (2 * FFT + UNIT * j, UNIT))):
            for y in range(2):
                copy = pltpu.make_async_copy(
                    w_ref.at[:, :, y, :, pl.ds(start, width)],
                    w.at[:, y, :, :, pl.ds(start, width)],
                    w_sem.at[j * 4 + k * 2 + y],
                )
                copy.start()
                loads.append(copy)
    for copy in tokens:
        copy.wait()
    tile = 512
    for j in range(3):
        for copy in loads[4 * j : 4 * j + 4]:
            copy.wait()

        @pl.loop(0, 8 * TOK // tile)
        def _(m):
            rows = pl.ds(pl.multiple_of(m * tile, tile), tile)
            pair = slice(2 * UNIT * j, 2 * UNIT * (j + 1))
            last = slice(2 * FFT + UNIT * j, 2 * FFT + UNIT * (j + 1))
            gate_up = dot(h_all[rows, :], w[:, :, :, :, pair].reshape(D, 2 * UNIT))
            d_hidden = dot(dy_all[rows, :], w[:, :, :, :, last].reshape(D, UNIT))
            gate, up = gate_up[:, :UNIT], gate_up[:, UNIT:]
            sigmoid_gate = jax.nn.sigmoid(gate)
            act = gate * sigmoid_gate
            hid[rows, UNIT * j : UNIT * (j + 1)] = (act * up).astype(bf16)
            d_gate = d_hidden * up * (sigmoid_gate * (1.0 + gate * (1.0 - sigmoid_gate)))
            dgu[rows, 2 * UNIT * j : 2 * UNIT * j + UNIT] = d_gate.astype(bf16)
            dgu[rows, 2 * UNIT * j + UNIT : 2 * UNIT * (j + 1)] = (d_hidden * act).astype(bf16)

    outs = [
        pltpu.make_async_copy(hid, hid_out, out_sem.at[0]),
        pltpu.make_async_copy(dgu, dgu_out, out_sem.at[1]),
    ]
    for copy in outs:
        copy.start()
    for z in range(4):
        cols = slice(z * PIECE, (z + 1) * PIECE)
        for start in range(0, 3 * FFT, 2 * UNIT):
            width = min(2 * UNIT, 3 * FFT - start)
            if start < 2 * FFT:
                out = dot_tn(h_all[:, cols], dgu[:, start : start + width])
            else:
                out = dot_tn(dy_all[:, cols], hid[:, start - 2 * FFT : start - 2 * FFT + width])
            w[z, :, :, :, start : start + width] = out.astype(bf16).reshape(2, 4, 48, width)
        for y in range(2):
            copy = pltpu.make_async_copy(w.at[z, y], term_ref.at[z, :, y], t_sem.at[z, y])
            copy.start()
            outs.append(copy)
    for copy in outs:
        copy.wait()


def feed_forward(h_parts, dy_parts, w):
    tokens = 8 * TOK
    outs = [((tokens, FFT), bf16), ((tokens, 2 * FFT), bf16), ((4, 4, 2, 48, 3 * FFT), bf16)]
    scratch = [
        pltpu.VMEM((tokens, D), bf16),
        pltpu.VMEM((tokens, D), bf16),
        pltpu.VMEM((4, 2, 4, 48, 3 * FFT), bf16),
        pltpu.VMEM((tokens, FFT), bf16),
        pltpu.VMEM((tokens, 2 * FFT), bf16),
        pltpu.SemaphoreType.DMA((2, 8)),
        pltpu.SemaphoreType.DMA((12,)),
        pltpu.SemaphoreType.DMA((2,)),
        pltpu.SemaphoreType.DMA((4, 2)),
    ]
    return call(
        ff_kernel, outs, *h_parts, *dy_parts, w, us=30, in_hbm=range(17), outs_hbm=True, scratch=scratch, limit=30
    )


def back_kernel(start, act_hbm, w_ref, put, act_ref, w, act_sem, w_sem):
    width = w.shape[-1]
    copy = pltpu.make_async_copy(act_hbm, act_ref, act_sem)
    copy.start()
    loads = []
    for z in range(4):
        for y in range(2):
            load = pltpu.make_async_copy(
                w_ref.at[z, :, y, :, pl.ds(start, width)], w.at[z, y], w_sem.at[z, y]
            )
            load.start()
            loads.append(load)
    copy.wait()
    for z in range(4):
        for load in loads[2 * z : 2 * z + 2]:
            load.wait()
        wz = w[z].reshape(PIECE, width)
        for m in range(4):
            put(z, m, dot_nt(act_ref[m * 2 * TOK : (m + 1) * 2 * TOK, :], wz))


def back_scratch(act):
    return [
        pltpu.VMEM(act.shape, bf16),
        pltpu.VMEM((4, 2, 4, 48, act.shape[1]), bf16),
        pltpu.SemaphoreType.DMA,
        pltpu.SemaphoreType.DMA((4, 2)),
    ]


def terms_kernel(start, act_hbm, w_ref, own_ref, give_ref, *scratch):
    def put(z, m, out):
        ref = own_ref if m < 2 else give_ref
        row = m % 2 * 2 * TOK
        ref[row : row + 2 * TOK, z * PIECE : (z + 1) * PIECE] = out.astype(ref.dtype)

    back_kernel(start, act_hbm, w_ref, put, *scratch)


def back_terms(start, act, w, us, after):
    outs = [((4 * TOK, D), f32), ((4 * TOK, D), bf16)]
    return call(
        lambda *refs: terms_kernel(start, *refs),
        outs, act, w, us=us, in_hbm=(0, 1), scratch=back_scratch(act), limit=20, after=after,
    )


def d_second_terms(d_gate_up, w, after):
    return back_terms(0, d_gate_up, w, 12, after)


def down_terms(hidden, w):
    return back_terms(2 * FFT, hidden, w, 8, ())


def add_kernel(own_ref, got_ref, keep_ref, g1_ref, g2_ref, g3_ref):
    for i, ref in enumerate((keep_ref, g1_ref, g2_ref, g3_ref)):
        rows = slice(i * TOK, (i + 1) * TOK)
        ref[...] = (own_ref[rows, :] + got_ref[rows, :].astype(f32)).astype(ref.dtype)


def reduce_tokens(own, give, after=()):
    outs = [((TOK, D), f32)] + [((TOK, D), bf16)] * 3
    return ring_collect(call(add_kernel, outs, own, core_send(give), after=after), y_send)


def d_branch_kernel(
    p0, p1, p2, p3, middle_ref, gain_ref, dy_ref, w0, w1, w2, w3, place_ref,
    d_middle_ref, e_ref, own_ref, give_ref, d_gain_ref,
):
    d_second = p0[...] + p1[...].astype(f32) + p2[...].astype(f32) + p3[...].astype(f32)
    middle = middle_ref[...]
    inv = norm_scale(middle)
    unit = middle * inv
    scaled = d_second * gain_ref[...]
    d_gain_ref[...] = jnp.sum(d_second * unit, axis=0, keepdims=True)
    d_middle = dy_ref[...].astype(f32) + inv * (
        scaled - unit * jnp.mean(scaled * unit, axis=-1, keepdims=True)
    )
    d_middle_ref[...] = d_middle
    e_ref[...] = d_middle.astype(bf16)
    own = jnp.zeros((TOK, HALF), f32)
    give = jnp.zeros((TOK, HALF), f32)
    for i, w in enumerate((w0, w1, w2, w3)):
        cols = slice(i * PIECE, (i + 1) * PIECE)
        rel = dot_nt(e_ref[...], w[...]).astype(bf16)
        own += dot_nt(rel, place_ref[:HALF, cols])
        give += dot_nt(rel, place_ref[HALF:, cols])
    own_ref[...] = own.astype(bf16)
    give_ref[...] = give.astype(bf16)


def d_branch(parts, middle, gain, dy, out_w, place):
    outs = [
        ((TOK, D), f32),
        ((TOK, D), bf16),
        ((TOK, HALF), bf16),
        ((TOK, HALF), bf16),
        ((1, D), f32),
    ]
    return call(d_branch_kernel, outs, *parts, middle, gain, dy, *out_w, place, us=5)


def out_term_kernel(a_ref, e_ref, t0, t1, t2, t3):
    for i, ref in enumerate((t0, t1, t2, t3)):
        ref[...] = dot_tn(a_ref[:, i * PIECE : (i + 1) * PIECE], e_ref[...]).astype(bf16)


def out_terms(a_rel, e):
    return call(out_term_kernel, [((PIECE, D), bf16)] * 4, a_rel, e, us=2)


def attend_back_kernel(
    half_ref, low_ref, d0_ref, d1_ref, log_ref, cos_ref, sin_ref, normed_ref, x_ref, w0, w1, w2, w3,
    t0, t1, t2, t3, sum_ref, own_ref, give_ref, d_gain_ref, grad_ref, out_ref, dh_ref,
):
    cos, sin = cos_ref[...], sin_ref[...]
    mask = causal_mask(half_ref[0])
    grad_ref[:TOK, :] = d0_ref[...]
    grad_ref[TOK:, :] = d1_ref[...]
    key = low_ref[:, QUERY : QUERY + HD]
    value = low_ref[:, QUERY + HD :]

    def unrotated(z):
        return (z * cos - pltpu.roll(z, HD // 2, 1) * sin).astype(bf16)

    def put(start, block):
        out_ref[:, start : start + HD] = block
        sum_ref[:, start : start + HD] = jnp.sum(block.astype(f32), axis=0, keepdims=True)

    d_key = jnp.zeros((LEN, HD), f32)
    d_value = jnp.zeros((LEN, HD), f32)
    for h in range(GROUP):
        query = low_ref[:, h * HD : (h + 1) * HD]
        grad = grad_ref[:, h * HD : (h + 1) * HD]
        scores = jnp.where(mask, dot_nt(query, key) * score_scale, -1e30)
        total = log_ref[h]
        probs = jnp.exp(scores - jnp.concatenate([total, total], axis=1))
        d_probs = dot_nt(grad, value)
        delta = jnp.sum(probs * d_probs, axis=-1, keepdims=True)
        d_scores = (probs * (d_probs - delta)).astype(bf16)
        put(h * HD, unrotated(dot(d_scores, key) * score_scale))
        d_key += dot_tn(d_scores, query)
        d_value += dot_tn(probs.astype(bf16), grad)
    put(QUERY, unrotated(d_key * score_scale))
    put(QUERY + HD, d_value.astype(bf16))
    for i, ref in enumerate((t0, t1, t2, t3)):
        ref[...] = dot_tn(normed_ref[:, i * PIECE : (i + 1) * PIECE], out_ref[...]).astype(bf16)
    for i, w in enumerate((w0, w1, w2, w3)):
        dh_ref[:, i * PIECE : (i + 1) * PIECE] = dot_nt(out_ref[...], w[:, :COLS])
    own_ref[...] = dh_ref[:TOK, :]
    give_ref[...] = dh_ref[TOK:, :].astype(bf16)
    x = x_ref[...].astype(f32)
    d_gain_ref[...] = jnp.sum(dh_ref[...] * (x * norm_scale(x)), axis=0, keepdims=True)


def attend_back(half, low, d0, d1, logs, cos, sin, normed, x_rel, proj, after):
    outs = [((PIECE, COLS), bf16)] * 4 + [
        ((1, COLS), f32),
        ((TOK, D), f32),
        ((TOK, D), bf16),
        ((1, D), f32),
    ]
    scratch = [
        pltpu.VMEM((LEN, QUERY), bf16),
        pltpu.VMEM((LEN, COLS), bf16),
        pltpu.VMEM((LEN, D), f32),
    ]
    return call(
        attend_back_kernel, outs, half, low, d0, d1, logs, cos, sin, normed, x_rel, *proj,
        us=6, smem=1, scratch=scratch, after=after,
    )


def input_grad_kernel(own_ref, got_ref, x_ref, gain_ref, d_middle_ref, place_ref, out_ref):
    scaled = (own_ref[...] + got_ref[...].astype(f32)) * gain_ref[...]
    x = x_ref[:TOK, :].astype(f32)
    inv = norm_scale(x)
    unit = x * inv
    through = inv * (scaled - unit * jnp.mean(scaled * unit, axis=-1, keepdims=True))
    out_ref[...] = d_middle_ref[...] + split_dot(through, place_ref[...])


def cut_kernel(rank_ref, weight_ref, keep_ref, send_ref):
    col = lax.broadcasted_iota(jnp.int32, (ROWS, UNIT), 1)
    for ref, i, flip in ((keep_ref, 0, 0), (keep_ref, 1, 6), (send_ref, 0, 1), (send_ref, 1, 7)):
        rank = rank_ref[0] ^ flip
        start = jnp.minimum(rank * FFT, FF - FFT)
        for j in range(3):
            inside = col >= rank * FFT - start - j * UNIT
            for k, to in enumerate((2 * UNIT * j, 2 * UNIT * j + UNIT, 2 * FFT + UNIT * j)):
                first = pl.multiple_of(k * FF + start + j * UNIT, 128)
                piece = weight_ref[:, pl.ds(first, UNIT)]
                ref[i, :, to : to + UNIT] = jnp.where(inside, piece, 0.0).astype(bf16)


def cut(rank, weight):
    return call(cut_kernel, [((2, ROWS, 3 * FFT), bf16)] * 2, rank, weight, smem=1)


def order_kernel(place_ref, keep_ref, got_ref, *outs):
    place = place_ref[0]
    for i, ref in enumerate(outs):
        ref[place] = keep_ref[i]
        ref[1 - place] = got_ref[i]


def attn_cut_kernel(side_ref, weight_ref, vec_ref, out_ref):
    side = side_ref[0]
    for start, width, to in ((0, QUERY, 0), (D, HD, QUERY), (D + KV * HD, HD, QUERY + HD)):
        first = pl.multiple_of(start + side * width, 128)
        out_ref[:, to : to + width] = weight_ref[:, pl.ds(first, width)].astype(bf16)
    out_ref[:, COLS : COLS + HD] = vec_ref[...]
    out_ref[:, COLS + HD :] = weight_ref[:, QKV:].astype(bf16)


def adam_update(weight, moment_one, moment_two, gradient, step_rate):
    moment_one = 0.9 * moment_one + 0.1 * gradient
    moment_two = 0.95 * moment_two + 0.05 * gradient * gradient
    first_hat = moment_one / (1.0 - 0.9**STEP)
    second_hat = moment_two / (1.0 - 0.95**STEP)
    updated = weight - step_rate * (first_hat / (jnp.sqrt(second_hat) + 1e-08) + 0.1 * weight)
    return (moment_one, moment_two, updated)


def ff_adam_kernel(rank_ref, g0, g1, g2, g3, w_ref, one_ref, two_ref, one_out, two_out, w_out):
    k = pl.program_id(0)

    def put(block, cols):
        results = adam_update(w_ref[:, cols], one_ref[:, cols], two_ref[:, cols], block.astype(f32), 0.02)
        for ref, value in zip((one_out, two_out, w_out), results):
            ref[:, cols] = value

    for flip in range(8):
        grad = (g0, g1, g2, g3)[flip // 2]
        rank = rank_ref[0] ^ flip
        for j in range(3):
            first = jnp.where(k == 2, 2 * FFT + UNIT * j, 2 * UNIT * j + UNIT * k)
            first = pl.multiple_of(first, 128)

            @pl.when(rank < 7)
            def _():
                block = grad[flip % 2, :, pl.ds(first, UNIT)]
                put(block, pl.ds(pl.multiple_of(rank * FFT + j * UNIT, 128), UNIT))

            skip = max(0, 8 * FFT - FF - j * UNIT)
            if skip < UNIT:

                @pl.when(rank == 7)
                def _():
                    block = grad[flip % 2, :, pl.ds(pl.multiple_of(first + skip, 128), UNIT - skip)]
                    start = FF - FFT + j * UNIT + skip
                    put(block, slice(start, start + UNIT - skip))


def ff_adam(rank, grads, weight, moment_one, moment_two):
    third = pl.BlockSpec((ROWS, FF), lambda k: (0, k))
    whole = pl.BlockSpec((2, ROWS, 3 * FFT), lambda k: (0, 0, 0))
    return pl.pallas_call(
        ff_adam_kernel,
        grid=(3,),
        out_shape=(jax.ShapeDtypeStruct((ROWS, 3 * FF), f32),) * 3,
        in_specs=[pl.BlockSpec(memory_space=pltpu.SMEM)] + [whole] * 4 + [third] * 3,
        out_specs=(third,) * 3,
        compiler_params=pltpu.CompilerParams(vmem_limit_bytes=32 * MIB),
    )(rank, *grads, weight, moment_one, moment_two)


def attn_adam_kernel(side_ref, part_ref, other_ref, w_ref, one_ref, two_ref, one_out, two_out, w_out):
    def put(grad, start):
        cols = slice(start, start + grad.shape[1])
        results = adam_update(w_ref[:, cols], one_ref[:, cols], two_ref[:, cols], grad, 0.05)
        for ref, value in zip((one_out, two_out, w_out), results):
            ref[:, cols] = value

    part, other = part_ref[...].astype(f32), other_ref[...].astype(f32)
    own_first = side_ref[0] == 0
    first = jnp.where(own_first, part[:, :COLS], other[:, :COLS])
    last = jnp.where(own_first, other[:, :COLS], part[:, :COLS])
    put(first[:, :QUERY], 0)
    put(last[:, :QUERY], QUERY)
    put(first[:, QUERY : QUERY + HD], D)
    put(last[:, QUERY : QUERY + HD], D + HD)
    put(first[:, QUERY + HD :], D + KV * HD)
    put(last[:, QUERY + HD :], D + KV * HD + HD)
    put(part[:, COLS + HD :] + other[:, COLS + HD :], QKV)


def shards(
    inputs,
    cotangent,
    attn_weight,
    attn_moment_one,
    attn_moment_two,
    mlp_weight,
    mlp_moment_one,
    mlp_moment_two,
    vectors,
    vector_moment_one,
    vector_moment_two,
):
    half = lax.axis_index("seq")
    yh, core = lax.axis_index("yh"), lax.axis_index("core")
    side = half ^ yh
    rank = half * 4 + yh * 2 + core
    scalar = lambda v: v.astype(jnp.int32).reshape(1)
    x_own, dy_own = inputs[0], cotangent[0]

    vec_own = jnp.pad(vectors.astype(bf16)[None, :], ((0, 15), (0, 48)))
    vec_pair = jnp.concatenate([vec_own[:1], cross_send(vec_own)[:1]])
    vec_block = jnp.concatenate([vec_pair, core_send(jnp.pad(vec_pair, ((0, 14), (0, 0))))[:2]])
    vec_block = jnp.pad(vec_block, ((0, ROWS - 4), (0, 0)))

    mlp_keep, mlp_give = cut(scalar(rank), mlp_weight)
    mlp_got = core_send(mlp_give)
    (attn_block,) = call(
        attn_cut_kernel, [((ROWS, COLS + HD + D), bf16)], scalar(side), attn_weight, vec_block, smem=1
    )
    block = ((2, ROWS, 3 * FFT), bf16)
    mlp_near, mlp_far = call(
        order_kernel, [block, block], scalar(core), mlp_keep, mlp_got, smem=1, after=[attn_block]
    )
    mlp_far = cross_send(mlp_far)
    attn_x = join(ring_parts(attn_block, x_send))
    (mlp_block,) = call(
        order_kernel, [((2,) + block[0], bf16)], scalar(yh), mlp_near[None], mlp_far[None], smem=1, after=[attn_x]
    )
    mlp_w = lax.all_gather(mlp_block.reshape(4 * ROWS, 3 * FFT), ("z", "x"), axis=0, tiled=True)
    mlp_w = mlp_w.reshape(4, 4, 2, 48, 3 * FFT)

    blocks = gathered_blocks(64)
    rows = (blocks[:, None] * ROWS + jnp.arange(ROWS, dtype=jnp.int32)[None, :]).reshape(D)
    to_rel = one_hot(rows)
    to_feat = one_hot((rows + side * HALF) % D)
    x_all = jnp.concatenate([x_own, seq_send(x_own)], axis=0)
    x_rel = dot(x_all, to_rel).astype(bf16)
    dy_parts = gather_tokens(hold(dy_own, attn_x))

    proj_z = join(
        ring_parts(attn_x[:, : COLS + HD], z_send), after=[x_rel, to_feat] + dy_parts[1:4]
    )
    proj_y = cross_send(proj_z)
    out_z = join(ring_parts(attn_x[:, COLS + HD :], z_send), after=[proj_y])
    out_y = cross_send(out_z)
    proj_w = [proj_z, proj_y, core_send(proj_z), core_send(proj_y)]

    place = jnp.arange(64, dtype=jnp.int32)
    by_vector = blocks[(place % 4) % 2 * 16 + (place % 4) // 2 * 32 + place // 4]
    pick = (place[:, None] == by_vector[None, :]).astype(bf16)
    vec_rel = proj_z[:, COLS:].reshape(16, ROWS, HD)[:, :4].reshape(64, HD)
    vec_all = dot(pick, vec_rel)[:, :80].reshape(1, 5120)
    gain_one = dot(vec_all[:, :D].astype(bf16), to_rel)
    gain_two = vec_all[:, D : 2 * D]
    bias_all = vec_all[:, 2 * D :]
    own_cols = lambda a, start, width: lax.dynamic_slice_in_dim(a, start + side * width, width, 1)
    bias = jnp.concatenate(
        [
            own_cols(bias_all, 0, QUERY),
            own_cols(bias_all, D, HD),
            own_cols(bias_all, D + KV * HD, HD),
        ],
        axis=1,
    )

    cos, sin = rotary_tables((jnp.arange(LEN) + half * TOK) % LEN)
    normed, low, heads_own, heads_give, logs = attend(
        scalar(half), x_rel, gain_one, proj_w, bias, cos, sin, after=[out_z]
    )
    heads_other = seq_send(heads_give)
    out_y = hold(out_y, heads_other)
    out_w = [out_z, out_y, core_send(out_z), core_send(out_y)]
    a_rel, middle, second = branch(x_own, heads_own, heads_other, to_feat, out_w, gain_two)

    hidden, d_gate_up, mlp_term = feed_forward(gather_tokens(second), dy_parts, mlp_w)
    mlp_part = lax.psum_scatter(
        mlp_term.reshape(D, 3 * FFT), ("z", "x"), scatter_dimension=0, tiled=True
    )
    down = reduce_tokens(*down_terms(hidden, mlp_w))
    d_second = reduce_tokens(*d_second_terms(d_gate_up, mlp_w, [down[0]]), after=down[1:])
    d_middle, e, d_own, d_give, d_gain_two = d_branch(
        d_second, middle, gain_two, dy_own, out_w, to_feat
    )

    d_other = seq_send(d_give)
    out_term = out_terms(a_rel, e)
    (out_far,) = add_up([out_term[1], core_send(out_term[3])])
    (out_near,) = add_up([out_term[0], core_send(out_term[2])])
    *proj_term, d_bias_own, dh_own, dh_give, d_gain_one = attend_back(
        scalar(half), low, d_own, d_other, logs, cos, sin, normed, x_rel, proj_w, [out_far]
    )

    by_core = mlp_part.reshape(2, 2, ROWS, 3 * FFT)
    of_core = lambda c: lax.dynamic_index_in_dim(by_core, c, 1, keepdims=False)
    pair = jnp.stack([of_core(core), core_send(of_core(1 - core))], axis=1)
    near_rows = lax.dynamic_index_in_dim(pair, yh, 0, keepdims=False)
    far_rows = lax.dynamic_index_in_dim(pair, 1 - yh, 0, keepdims=False)
    grads = [near_rows, ring_send(far_rows, "yh", 1), seq_send(near_rows), cross_send(far_rows)]
    (proj_far,) = add_up([proj_term[1], core_send(proj_term[3])])
    (proj_near,) = add_up([proj_term[0], core_send(proj_term[2])])
    out_parts = add_up([out_near, cross_send(out_far)], pieces=4)
    bias_zero = jnp.zeros((1, QKV), f32)
    put = lambda a, v, start, width: lax.dynamic_update_slice_in_dim(a, v, start + side * width, 1)
    d_bias = put(bias_zero, d_bias_own[:, :QUERY], 0, QUERY)
    d_bias = put(d_bias, d_bias_own[:, QUERY : QUERY + HD], D, HD)
    d_bias = put(d_bias, d_bias_own[:, QUERY + HD :], D + KV * HD, HD)
    vec_term = jnp.concatenate([split_dot(d_gain_one, to_rel), d_gain_two, d_bias], axis=1)
    vec_term = jnp.pad(vec_term.reshape(64, 80), ((0, 0), (0, 48))).astype(bf16)
    pick_rel = (place[:, None] == blocks[None, :]).astype(bf16)
    vec_term = dot_tn(pick_rel, vec_term)
    vec_term = pair_reduce(vec_term, core_send)
    vec_term = pair_reduce(vec_term, cross_send)
    vec_term = jnp.pad(vec_term[:, None, :], ((0, 0), (0, ROWS - 1), (0, 0))).reshape(PIECE, HD)
    vec_term = vec_term.astype(bf16)
    proj_parts = add_up(
        [proj_near, cross_send(proj_far), vec_term, jnp.zeros_like(vec_term)], pieces=4, count=2
    )
    proj_parts = ring_collect(proj_parts, z_send)
    out_parts = ring_collect(out_parts, z_send)
    attn_parts = add_up(proj_parts + out_parts, pieces=4, count=4, after=[pair])
    (attn_part,) = add_up(ring_collect(attn_parts, x_send), after=grads[1:])
    attn_other = seq_send(attn_part)
    vec_cols = slice(COLS, COLS + 80)
    vec_grad = attn_part[0, vec_cols].astype(f32) + attn_other[0, vec_cols].astype(f32)

    mlp_one, mlp_two, mlp_new = ff_adam(
        scalar(rank), grads, mlp_weight, mlp_moment_one, mlp_moment_two
    )
    attn_one, attn_two, attn_new = call(
        attn_adam_kernel,
        [((ROWS, QKV + D), f32)] * 3,
        scalar(side),
        attn_part,
        attn_other,
        attn_weight,
        attn_moment_one,
        attn_moment_two,
        smem=1,
    )

    total = down[0] + down[1].astype(f32) + down[2].astype(f32) + down[3].astype(f32)
    output = (middle + total).astype(bf16)[None]
    (input_grad,) = call(
        input_grad_kernel, [((TOK, D), f32)], dh_own, seq_send(dh_give), x_rel, gain_one, d_middle, to_rel,
        us=5, after=[proj_far],
    )
    vec_one, vec_two, vec_new = adam_update(
        vectors, vector_moment_one, vector_moment_two, vec_grad, 0.5
    )
    return (
        output,
        input_grad[None],
        attn_one,
        attn_two,
        attn_new,
        mlp_one,
        mlp_two,
        mlp_new,
        vec_one,
        vec_two,
        vec_new,
    )


def solution(mesh):
    grid = Mesh(mesh.devices.reshape(2, 4, 2, 4, 2), ("seq",) + FSDP)
    tokens, rows, vector = P(FSDP, "seq", None), P(FSDP, None), P(FSDP)
    return jax.shard_map(
        shards,
        mesh=grid,
        in_specs=(tokens, tokens) + (rows,) * 6 + (vector,) * 3,
        out_specs=(tokens, tokens) + (rows,) * 6 + (vector,) * 3,
        check_vma=False,
    )
```

```python
import math

import jax
import jax.numpy as jnp
from jax import lax
from jax.experimental import pallas as pl
from jax.experimental.pallas import tpu as pltpu
from jax.sharding import Mesh
from jax.sharding import PartitionSpec as P

D = 1536
H = 12
KV = 2
HD = 128
FF = 8960
STEP = 10
QKV = 2048
ROWS = 24
TOK = 128
LEN = 256
HALF = D // 2
GROUP = H // KV
QUERY = GROUP * HD
COLS = QUERY + 2 * HD
FFT = 1152
UNIT = FFT // 3
PIECE = D // 4
LINE = HALF // 4
MIB = 1024 * 1024

norm_eps = 1e-06
rope_base = 1000000.0
f32 = jnp.float32
bf16 = jnp.bfloat16
contract_rows = (((0,), (0,)), ((), ()))
contract_cols = (((1,), (1,)), ((), ()))
score_scale = HD ** (-0.5)
FSDP = ("z", "yh", "x", "core")
SIZES = {"seq": 2, "z": 4, "yh": 2, "x": 4, "core": 2}


def dot(a, b):
    return jnp.dot(a, b, preferred_element_type=f32)


def dot_tn(a, b):
    return lax.dot_general(a, b, contract_rows, preferred_element_type=f32)


def dot_nt(a, b):
    return lax.dot_general(a, b, contract_cols, preferred_element_type=f32)


def split_dot_nt(a, b):
    high = a.astype(bf16)
    low = (a - high.astype(f32)).astype(bf16)
    return dot_nt(high, b) + dot_nt(low, b)


def ring_send(values, axis, shift):
    size = SIZES[axis]
    return lax.ppermute(values, axis, [(i, (i + shift) % size) for i in range(size)])


def x_send(values, shift):
    return ring_send(values, "x", shift)


def z_send(values, shift):
    return ring_send(values, "z", shift)


def y_send(values, shift):
    place = lambda y: (y % 2) * 2 + y // 2
    return lax.ppermute(
        values, ("seq", "yh"), [(place(i), place((i + shift) % 4)) for i in range(4)]
    )


def cross_send(values):
    return lax.ppermute(values, ("seq", "yh"), [(i, 3 - i) for i in range(4)])


def core_send(values):
    return ring_send(values, "core", 1)


def seq_send(values):
    return ring_send(values, "seq", 1)


def ring_parts(values, send):
    return [values, send(values, 1), send(values, -1), send(values, 2)]


def pair_reduce(values, send):
    rows = values.shape[0] // 2
    return values[:rows] + send(values[rows:].astype(bf16)).astype(f32)


def ring_collect(parts, send):
    return [parts[0], send(parts[1], -1), send(parts[2], 1), send(parts[3], 2)]


def gather_tokens(values):
    parts = ring_parts(values, y_send)
    return parts + [core_send(p) for p in parts]


def near(index):
    return jnp.where(index == 1, -1, jnp.where(index == 0, 0, index - 1))


def gathered_blocks(count):
    j = jnp.arange(count, dtype=jnp.int32)
    xi, zi, yi, ci = j % 4, (j // 4) % 4, (j // 16) % 2, j // 32
    z = (lax.axis_index("z") + near(zi) + 4) % 4
    x = (lax.axis_index("x") + near(xi) + 4) % 4
    yh = (lax.axis_index("yh") + yi) % 2
    core = (lax.axis_index("core") + ci) % 2
    return z * 16 + yh * 8 + x * 2 + core


def call(
    kernel, outs, *args, us=1, smem=0, fetch=(), raw=(), store=(), raw_outs=False, scratch=(), room=6, after=()
):
    vmem, hbm = pl.BlockSpec(memory_space=pltpu.VMEM), pl.BlockSpec(memory_space=pltpu.HBM)
    fetch = [g if isinstance(g, tuple) else (g,) for g in fetch]
    far = set(raw) | {i for g in fetch for i in g}
    specs = [
        pl.BlockSpec(memory_space=pltpu.SMEM) if i < smem else hbm if i in far else vmem
        for i in range(len(args))
    ] + [pl.BlockSpec(memory_space=pl.ANY)] * len(after)
    buffers = []
    for g in fetch:
        rows = sum(args[i].shape[0] for i in g)
        buffers.append(((rows,) + args[g[0]].shape[1:], args[g[0]].dtype))
    buffers += [outs[i] for i in store]
    held = [pltpu.VMEM(shape, kind) for shape, kind in buffers]
    moves = max(1, sum(len(g) for g in fetch) + len(store))
    n_in, n_out, n_own = len(args), len(outs), len(scratch)

    def body(*refs):
        ins, refs = list(refs[:n_in]), refs[n_in + len(after) :]
        out_refs, own = list(refs[:n_out]), refs[n_out : n_out + n_own]
        held_refs, sems = refs[n_out + n_own : -1], refs[-1]
        copies, k = [], 0
        for g, ref in zip(fetch, held_refs):
            row = 0
            for i in g:
                rows = args[i].shape[0]
                copies.append(pltpu.make_async_copy(ins[i], ref.at[pl.ds(row, rows)], sems.at[k]))
                row, k = row + rows, k + 1
            ins[g[0]] = ref
        for copy in copies:
            copy.start()
        for copy in copies:
            copy.wait()
        drop = {i for g in fetch for i in g[1:]}
        ins = [ref for i, ref in enumerate(ins) if i not in drop]
        leaving = []
        for i, ref in zip(store, held_refs[len(fetch) :]):
            leaving.append(pltpu.make_async_copy(ref, out_refs[i], sems.at[k]))
            out_refs[i] = ref
            k += 1
        kernel(*ins, *out_refs, *own)
        for copy in leaving:
            copy.start()
        for copy in leaving:
            copy.wait()

    size = lambda shape, kind: math.prod(shape) * jnp.dtype(kind).itemsize
    used = sum(size(*b) for b in buffers)
    used += sum(size(b.shape, b.dtype) for b in scratch if hasattr(b, "shape") and b.memory_space == pltpu.VMEM)
    args = [
        pltpu.with_memory_space_constraint(a, pltpu.HBM) if i in far else a
        for i, a in enumerate(args)
    ]
    leave = lambda i: pltpu.HBM if raw_outs or i in store else jax.ShapeDtypeStruct
    return pl.pallas_call(
        body,
        out_shape=tuple(leave(i)(shape, kind) for i, (shape, kind) in enumerate(outs)),
        in_specs=specs,
        out_specs=tuple(hbm if raw_outs or i in store else vmem for i in range(n_out)),
        scratch_shapes=list(scratch) + held + [pltpu.SemaphoreType.DMA((moves,))],
        cost_estimate=pl.CostEstimate(flops=us * 10**9, bytes_accessed=us * 10**6, transcendentals=0),
        compiler_params=pltpu.CompilerParams(vmem_limit_bytes=used + room * MIB),
    )(*args, *after)


def hold_kernel(*refs):
    pass


def hold(values, *after):
    anywhere = pl.BlockSpec(memory_space=pl.ANY)
    return pl.pallas_call(
        hold_kernel,
        out_shape=jax.ShapeDtypeStruct(values.shape, values.dtype),
        in_specs=[anywhere] * (1 + len(after)),
        out_specs=anywhere,
        input_output_aliases={0: 0},
    )(values, *after)


def join_kernel(*refs):
    out_ref, row = refs[-1], 0
    for ref in refs[:-1]:
        out_ref[row : row + ref.shape[0], :] = ref[...]
        row += ref.shape[0]


def join(parts, after=()):
    rows = sum(p.shape[0] for p in parts)
    return call(join_kernel, [((rows, parts[0].shape[1]), bf16)], *parts, after=after)[0]


def sum_kernel(count, given, outs):
    groups = []
    for i in range(0, len(given), count):
        total = given[i][...].astype(f32)
        for ref in given[i + 1 : i + count]:
            total = total + ref[...].astype(f32)
        groups.append(total)
    rows, col = outs[0].shape[0], 0
    for total in groups:
        for i, ref in enumerate(outs):
            part = total[i * rows : (i + 1) * rows, :]
            ref[:, col : col + total.shape[1]] = part.astype(ref.dtype)
        col += total.shape[1]


def add_up(parts, pieces=1, count=None, after=()):
    count = count or len(parts)
    cols = sum(p.shape[1] for p in parts[::count])
    outs = [((parts[0].shape[0] // pieces, cols), bf16)] * pieces
    kernel = lambda *refs: sum_kernel(count, refs[: len(parts)], refs[len(parts) :])
    return call(kernel, outs, *parts, after=after)


def place(rows_ref, size, cols):
    row = lax.broadcasted_iota(jnp.int32, (size, cols.stop - cols.start), 0)
    return jnp.where(row == rows_ref[:1, cols], 1.0, 0.0).astype(bf16)


PIECES = [slice(i * PIECE, (i + 1) * PIECE) for i in range(4)]


def permute_kernel(rows_ref, *refs):
    out_ref = refs[-1]
    for cols in PIECES:
        here, row = place(rows_ref, D, cols), 0
        for ref in refs[:-1]:
            out_ref[row : row + ref.shape[0], cols] = dot(ref[...], here).astype(out_ref.dtype)
            row += ref.shape[0]


def unpermute_kernel(rows_ref, values_ref, out_ref):
    out = jnp.zeros(out_ref.shape, f32)
    for cols in PIECES:
        out += split_dot_nt(values_ref[:, cols], place(rows_ref, D, cols))
    out_ref[...] = out


def as_rows(rows):
    return jnp.broadcast_to(rows[None, :].astype(jnp.int32), (8, rows.shape[0]))


def rotary_tables(positions):
    half_dim = HD // 2
    freqs = rope_base ** (-jnp.arange(half_dim, dtype=f32) * 2.0 / HD)
    angles = positions.astype(f32)[:, None] * freqs[None, :]
    cos, sin = jnp.cos(angles), jnp.sin(angles)
    return jnp.concatenate([cos, cos], axis=1), jnp.concatenate([-sin, sin], axis=1)


def causal_mask(half):
    row = (lax.broadcasted_iota(jnp.int32, (LEN, LEN), 0) + half * TOK) % LEN
    col = (lax.broadcasted_iota(jnp.int32, (LEN, LEN), 1) + half * TOK) % LEN
    return row >= col


def norm_scale(values):
    return lax.rsqrt(jnp.mean(values * values, axis=-1, keepdims=True) + norm_eps)


def attend_kernel(
    half_ref, x_ref, gain_ref, w_ref, bias_ref, cos_ref, sin_ref,
    normed_ref, low_ref, out_ref, log_ref, qkv_ref,
):
    x = x_ref[...].astype(f32)
    normed_ref[...] = (x * norm_scale(x) * gain_ref[...]).astype(bf16)
    qkv_ref[...] = dot(normed_ref[...], w_ref[:, :COLS]) + bias_ref[...]
    cos, sin = cos_ref[...], sin_ref[...]
    mask = causal_mask(half_ref[0])

    def rotated(start):
        z = qkv_ref[:, start : start + HD]
        return (z * cos + pltpu.roll(z, HD // 2, 1) * sin).astype(bf16)

    key = rotated(QUERY)
    low_ref[:, QUERY : QUERY + HD] = key
    value = qkv_ref[:, QUERY + HD :].astype(bf16)
    low_ref[:, QUERY + HD :] = value
    for h in range(GROUP):
        query = rotated(h * HD)
        low_ref[:, h * HD : (h + 1) * HD] = query
        scores = jnp.where(mask, dot_nt(query, key) * score_scale, -1e30)
        top = jnp.max(scores, axis=-1, keepdims=True)
        total = top + jnp.log(jnp.sum(jnp.exp(scores - top), axis=-1, keepdims=True))
        log_ref[h] = jnp.broadcast_to(total, (LEN, HD))
        probs = jnp.exp(scores - total).astype(bf16)
        out_ref[:, h * HD : (h + 1) * HD] = dot(probs, value).astype(bf16)


def attend(half, x_rel, gain, proj, bias, cos, sin):
    outs = [((LEN, D), bf16), ((LEN, COLS), bf16), ((LEN, QUERY), bf16), ((GROUP, LEN, HD), f32)]
    return call(
        attend_kernel, outs, half, x_rel, gain, *proj, bias, cos, sin,
        us=6, smem=1, fetch=[1, (3, 4, 5, 6)], store=[0, 1, 3], scratch=[pltpu.VMEM((LEN, COLS), f32)],
    )


def branch_kernel(a_ref, rows_ref, w_ref, rel_ref, own_ref, give_ref):
    rel_ref[...] = dot(a_ref[...], place(rows_ref, HALF, slice(0, HALF))).astype(bf16)
    own_ref[...] = dot(rel_ref[:TOK, :], w_ref[...])
    give_ref[...] = dot(rel_ref[TOK:, :], w_ref[...]).astype(bf16)


def branch(a, rows, out_w):
    outs = [((LEN, HALF), bf16), ((TOK, D), f32), ((TOK, D), bf16)]
    return call(branch_kernel, outs, a, rows, *out_w, us=4, fetch=[(2, 3, 4, 5)], store=[0])


def second_kernel(x_ref, own_ref, got_ref, gain_ref, middle_ref, second_ref):
    middle = x_ref[...].astype(f32) + own_ref[...] + got_ref[...].astype(f32)
    middle_ref[...] = middle
    second_ref[...] = (middle * norm_scale(middle) * gain_ref[...]).astype(bf16)


def ff_kernel(*refs):
    h_parts, dy_parts, refs = refs[:8], refs[8:16], refs[16:]
    w_ref, hid_out, dgu_out, term_ref, h_all, dy_all, w, hid, dgu, in_sem, w_sem, out_sem, t_sem = refs
    tokens = []
    for k, (parts, whole) in enumerate(((h_parts, h_all), (dy_parts, dy_all))):
        for i, part in enumerate(parts):
            copy = pltpu.make_async_copy(part, whole.at[pl.ds(i * TOK, TOK), :], in_sem.at[k, i])
            copy.start()
            tokens.append(copy)
    loads = []
    for j in range(3):
        for k, (start, width) in enumerate(((2 * UNIT * j, 2 * UNIT), (2 * FFT + UNIT * j, UNIT))):
            for y in range(2):
                copy = pltpu.make_async_copy(
                    w_ref.at[:, :, y, :, pl.ds(start, width)],
                    w.at[:, y, :, :, pl.ds(start, width)],
                    w_sem.at[j * 4 + k * 2 + y],
                )
                copy.start()
                loads.append(copy)
    for copy in tokens:
        copy.wait()
    tile = 512
    for j in range(3):
        for copy in loads[4 * j : 4 * j + 4]:
            copy.wait()

        @pl.loop(0, 8 * TOK // tile)
        def _(m):
            rows = pl.ds(pl.multiple_of(m * tile, tile), tile)
            pair = slice(2 * UNIT * j, 2 * UNIT * (j + 1))
            last = slice(2 * FFT + UNIT * j, 2 * FFT + UNIT * (j + 1))
            gate_up = dot(h_all[rows, :], w[:, :, :, :, pair].reshape(D, 2 * UNIT))
            d_hidden = dot(dy_all[rows, :], w[:, :, :, :, last].reshape(D, UNIT))
            gate, up = gate_up[:, :UNIT], gate_up[:, UNIT:]
            sigmoid_gate = jax.nn.sigmoid(gate)
            act = gate * sigmoid_gate
            hid[rows, UNIT * j : UNIT * (j + 1)] = (act * up).astype(bf16)
            d_gate = d_hidden * up * (sigmoid_gate * (1.0 + gate * (1.0 - sigmoid_gate)))
            dgu[rows, 2 * UNIT * j : 2 * UNIT * j + UNIT] = d_gate.astype(bf16)
            dgu[rows, 2 * UNIT * j + UNIT : 2 * UNIT * (j + 1)] = (d_hidden * act).astype(bf16)

    outs = [
        pltpu.make_async_copy(hid, hid_out, out_sem.at[0]),
        pltpu.make_async_copy(dgu, dgu_out, out_sem.at[1]),
    ]
    for copy in outs:
        copy.start()
    for z in range(4):
        cols = slice(z * PIECE, (z + 1) * PIECE)
        for start in range(0, 3 * FFT, 2 * UNIT):
            width = min(2 * UNIT, 3 * FFT - start)
            if start < 2 * FFT:
                out = dot_tn(h_all[:, cols], dgu[:, start : start + width])
            else:
                out = dot_tn(dy_all[:, cols], hid[:, start - 2 * FFT : start - 2 * FFT + width])
            w[z, :, :, :, start : start + width] = out.astype(bf16).reshape(2, 4, 48, width)
        for y in range(2):
            copy = pltpu.make_async_copy(w.at[z, y], term_ref.at[z, :, y], t_sem.at[z, y])
            copy.start()
            outs.append(copy)
    for copy in outs:
        copy.wait()


def feed_forward(h_parts, dy_parts, w):
    tokens = 8 * TOK
    outs = [((tokens, FFT), bf16), ((tokens, 2 * FFT), bf16), ((4, 4, 2, 48, 3 * FFT), bf16)]
    scratch = [
        pltpu.VMEM((tokens, D), bf16),
        pltpu.VMEM((tokens, D), bf16),
        pltpu.VMEM((4, 2, 4, 48, 3 * FFT), bf16),
        pltpu.VMEM((tokens, FFT), bf16),
        pltpu.VMEM((tokens, 2 * FFT), bf16),
        pltpu.SemaphoreType.DMA((2, 8)),
        pltpu.SemaphoreType.DMA((12,)),
        pltpu.SemaphoreType.DMA((2,)),
        pltpu.SemaphoreType.DMA((4, 2)),
    ]
    return call(
        ff_kernel, outs, *h_parts, *dy_parts, w, us=30, raw=range(17), raw_outs=True, scratch=scratch
    )


def back_kernel(start, act_hbm, w_ref, put, act_ref, w, act_sem, w_sem):
    width = w.shape[-1]
    copy = pltpu.make_async_copy(act_hbm, act_ref, act_sem)
    copy.start()
    loads = []
    for z in range(4):
        for y in range(2):
            load = pltpu.make_async_copy(
                w_ref.at[z, :, y, :, pl.ds(start, width)], w.at[z, y], w_sem.at[z, y]
            )
            load.start()
            loads.append(load)
    copy.wait()
    for z in range(4):
        for load in loads[2 * z : 2 * z + 2]:
            load.wait()
        wz = w[z].reshape(PIECE, width)
        for m in range(4):
            put(z, m, dot_nt(act_ref[m * 2 * TOK : (m + 1) * 2 * TOK, :], wz))


def back_scratch(act):
    return [
        pltpu.VMEM(act.shape, bf16),
        pltpu.VMEM((4, 2, 4, 48, act.shape[1]), bf16),
        pltpu.SemaphoreType.DMA,
        pltpu.SemaphoreType.DMA((4, 2)),
    ]


def terms_kernel(start, act_hbm, w_ref, own_ref, give_ref, *scratch):
    def put(z, m, out):
        ref = own_ref if m < 2 else give_ref
        row = m % 2 * 2 * TOK
        ref[row : row + 2 * TOK, z * PIECE : (z + 1) * PIECE] = out.astype(ref.dtype)

    back_kernel(start, act_hbm, w_ref, put, *scratch)


def back_terms(start, act, w, us, after):
    outs = [((4 * TOK, D), f32), ((4 * TOK, D), bf16)]
    return call(
        lambda *refs: terms_kernel(start, *refs),
        outs, act, w, us=us, raw=(0, 1), scratch=back_scratch(act), after=after,
    )


def d_second_terms(d_gate_up, w):
    return back_terms(0, d_gate_up, w, 12, ())


def down_terms(hidden, w, after):
    return back_terms(2 * FFT, hidden, w, 8, after)


def add_kernel(own_ref, got_ref, keep_ref, g1_ref, g2_ref, g3_ref):
    for i, ref in enumerate((keep_ref, g1_ref, g2_ref, g3_ref)):
        rows = slice(i * TOK, (i + 1) * TOK)
        ref[...] = (own_ref[rows, :] + got_ref[rows, :].astype(f32)).astype(ref.dtype)


def reduce_tokens(own, give, after=()):
    outs = [((TOK, D), f32)] + [((TOK, D), bf16)] * 3
    return ring_collect(call(add_kernel, outs, own, core_send(give), after=after), y_send)


def d_middle_kernel(p0, p1, p2, p3, middle_ref, gain_ref, dy_ref, d_middle_ref, e_ref, d_gain_ref):
    d_second = p0[...] + p1[...].astype(f32) + p2[...].astype(f32) + p3[...].astype(f32)
    middle = middle_ref[...]
    inv = norm_scale(middle)
    unit = middle * inv
    scaled = d_second * gain_ref[...]
    d_gain_ref[...] = jnp.sum(d_second * unit, axis=0, keepdims=True)
    d_middle = dy_ref[...].astype(f32) + inv * (
        scaled - unit * jnp.mean(scaled * unit, axis=-1, keepdims=True)
    )
    d_middle_ref[...] = d_middle
    e_ref[...] = d_middle.astype(bf16)


def d_middle_of(parts, middle, gain, dy, after):
    outs = [((TOK, D), f32), ((TOK, D), bf16), ((1, D), f32)]
    return call(
        d_middle_kernel, outs, *parts, middle, gain, dy, us=2, fetch=[4, 6], store=[0], after=after
    )


def out_term_kernel(a_ref, e0_ref, e1_ref, t0, t1, t2, t3):
    total = dot_tn(a_ref[:TOK, :], e0_ref[...]) + dot_tn(a_ref[TOK:, :], e1_ref[...])
    for i, ref in enumerate((t0, t1, t2, t3)):
        ref[...] = total[i * LINE : (i + 1) * LINE, :].astype(bf16)


def out_terms(a_rel, e, e_other):
    outs = [((LINE, D), bf16)] * 4
    return call(out_term_kernel, outs, a_rel, e, e_other, us=2, fetch=[0], room=10)


def attend_back_kernel(
    half_ref, e0_ref, e1_ref, out_w_ref, rows_ref, low_ref, log_ref, cos_ref, sin_ref, normed_ref, x_ref, w_ref,
    t0, t1, t2, t3, sum_ref, own_ref, give_ref, d_gain_ref, grad_ref, out_ref, dh_ref,
):
    cos, sin = cos_ref[...], sin_ref[...]
    mask = causal_mask(half_ref[0])
    here = place(rows_ref, HALF, slice(0, HALF))
    for i, e_ref in enumerate((e0_ref, e1_ref)):
        rel = dot_nt(e_ref[...], out_w_ref[...]).astype(bf16)
        grad_ref[i * TOK : (i + 1) * TOK, :] = dot_nt(rel, here).astype(bf16)
    key = low_ref[:, QUERY : QUERY + HD]
    value = low_ref[:, QUERY + HD :]

    def unrotated(z):
        return (z * cos - pltpu.roll(z, HD // 2, 1) * sin).astype(bf16)

    def put(start, block):
        out_ref[:, start : start + HD] = block
        sum_ref[:, start : start + HD] = jnp.sum(block.astype(f32), axis=0, keepdims=True)

    d_key = jnp.zeros((LEN, HD), f32)
    d_value = jnp.zeros((LEN, HD), f32)
    for h in range(GROUP):
        query = low_ref[:, h * HD : (h + 1) * HD]
        grad = grad_ref[:, h * HD : (h + 1) * HD]
        scores = jnp.where(mask, dot_nt(query, key) * score_scale, -1e30)
        total = log_ref[h]
        probs = jnp.exp(scores - jnp.concatenate([total, total], axis=1))
        d_probs = dot_nt(grad, value)
        delta = jnp.sum(probs * d_probs, axis=-1, keepdims=True)
        d_scores = (probs * (d_probs - delta)).astype(bf16)
        put(h * HD, unrotated(dot(d_scores, key) * score_scale))
        d_key += dot_tn(d_scores, query)
        d_value += dot_tn(probs.astype(bf16), grad)
    put(QUERY, unrotated(d_key * score_scale))
    put(QUERY + HD, d_value.astype(bf16))
    for i, ref in enumerate((t0, t1, t2, t3)):
        ref[...] = dot_tn(normed_ref[:, i * PIECE : (i + 1) * PIECE], out_ref[...]).astype(bf16)
    dh_ref[...] = dot_nt(out_ref[...], w_ref[:, :COLS])
    own_ref[...] = dh_ref[:TOK, :]
    give_ref[...] = dh_ref[TOK:, :].astype(bf16)
    x = x_ref[...].astype(f32)
    d_gain_ref[...] = jnp.sum(dh_ref[...] * (x * norm_scale(x)), axis=0, keepdims=True)


def attend_back(half, e, e_other, out_w, rows, low, logs, cos, sin, normed, x_rel, proj, after):
    outs = [((PIECE, COLS), bf16)] * 4 + [
        ((1, COLS), f32),
        ((TOK, D), f32),
        ((TOK, D), bf16),
        ((1, D), f32),
    ]
    scratch = [
        pltpu.VMEM((LEN, QUERY), bf16),
        pltpu.VMEM((LEN, COLS), bf16),
        pltpu.VMEM((LEN, D), f32),
    ]
    return call(
        attend_back_kernel, outs, half, e, e_other, *out_w, rows, low, logs, cos, sin, normed, x_rel, *proj,
        us=9, smem=1, fetch=[(3, 4, 5, 6), 8, 9, 12, 13, (14, 15, 16, 17)], store=[5, 6], scratch=scratch,
        room=8, after=after,
    )


def input_grad_kernel(own_ref, got_ref, x_ref, gain_ref, d_middle_ref, rows_ref, out_ref):
    scaled = (own_ref[...] + got_ref[...].astype(f32)) * gain_ref[...]
    x = x_ref[:TOK, :].astype(f32)
    inv = norm_scale(x)
    unit = x * inv
    through = inv * (scaled - unit * jnp.mean(scaled * unit, axis=-1, keepdims=True))
    total = d_middle_ref[...]
    for cols in PIECES:
        total += split_dot_nt(through[:, cols], place(rows_ref, D, cols))
    out_ref[...] = total


def cut_kernel(rank_ref, weight_ref, keep_ref, send_ref, held_ref, sem):
    col = lax.broadcasted_iota(jnp.int32, (ROWS, UNIT), 1)
    ranks = [rank_ref[0] ^ flip for flip in (1, 7, 0, 6)]
    starts = [jnp.minimum(rank * FFT, FF - FFT) for rank in ranks]
    copies = []
    for n, start in enumerate(starts):
        for k in range(3):
            first = pl.multiple_of(k * FF + start, 128)
            copies.append(
                pltpu.make_async_copy(
                    weight_ref.at[:, pl.ds(first, FFT)], held_ref.at[n, k], sem.at[n, k]
                )
            )
            copies[-1].start()
    for n, (rank, start) in enumerate(zip(ranks, starts)):
        ref, i = (send_ref, n) if n < 2 else (keep_ref, n - 2)
        for copy in copies[3 * n : 3 * n + 3]:
            copy.wait()
        for j in range(3):
            inside = col >= rank * FFT - start - j * UNIT
            for k, to in enumerate((2 * UNIT * j, 2 * UNIT * j + UNIT, 2 * FFT + UNIT * j)):
                piece = held_ref[n, k, :, j * UNIT : (j + 1) * UNIT]
                ref[i, :, to : to + UNIT] = jnp.where(inside, piece, 0.0).astype(bf16)


def cut(rank, weight):
    scratch = [pltpu.VMEM((4, 3, ROWS, FFT), f32), pltpu.SemaphoreType.DMA((4, 3))]
    outs = [((2, ROWS, 3 * FFT), bf16)] * 2
    return call(cut_kernel, outs, rank, weight, us=2, smem=1, raw=(1,), scratch=scratch)


def near_kernel(flag_ref, own, before, after, across, proj_ref, out_ref):
    for i, ref in enumerate((own, before, after, across)):
        proj_ref[i * 4 * ROWS : (i + 1) * 4 * ROWS, :] = ref[:, : COLS + HD]
    rest = slice(COLS + HD, COLS + HD + D)
    first = jnp.where(flag_ref[0] == 1, own[:, rest], across[:, rest])
    second = jnp.where(flag_ref[1] == 1, after[:, rest], before[:, rest])
    out_ref[: 4 * ROWS, :] = first
    out_ref[4 * ROWS :, :] = second


def far_kernel(proj, proj_got, vec, out, out_got, o0, o1, o2, o3):
    total = proj[...].astype(f32) + proj_got[...].astype(f32)
    rest = out[...].astype(f32) + out_got[...].astype(f32)
    for i, ref in enumerate((o0, o1, o2, o3)):
        rows = slice(i * 4 * ROWS, (i + 1) * 4 * ROWS)
        ref[:, :COLS] = total[rows, :].astype(bf16)
        ref[:, COLS : COLS + HD] = vec[rows, :].astype(bf16)
        half = slice(0, 4 * ROWS) if i in (0, 3) else slice(4 * ROWS, 8 * ROWS)
        ref[:, COLS + HD :] = rest[half, :].astype(bf16)


def order_kernel(place_ref, keep_ref, got_ref, *outs):
    place = place_ref[0]
    for i, ref in enumerate(outs):
        ref[place] = keep_ref[i]
        ref[1 - place] = got_ref[i]


def attn_cut_kernel(side_ref, weight_ref, vec_ref, out_ref):
    side = side_ref[0]
    for start, width, to in ((0, QUERY, 0), (D, HD, QUERY), (D + KV * HD, HD, QUERY + HD)):
        first = pl.multiple_of(start + side * width, 128)
        out_ref[:, to : to + width] = weight_ref[:, pl.ds(first, width)].astype(bf16)
    out_ref[:, COLS : COLS + HD] = vec_ref[...]
    out_ref[:, COLS + HD :] = weight_ref[:, QKV:].astype(bf16)


def adam_update(weight, moment_one, moment_two, gradient, step_rate):
    moment_one = 0.9 * moment_one + 0.1 * gradient
    moment_two = 0.95 * moment_two + 0.05 * gradient * gradient
    first_hat = moment_one / (1.0 - 0.9**STEP)
    second_hat = moment_two / (1.0 - 0.95**STEP)
    updated = weight - step_rate * (first_hat / (jnp.sqrt(second_hat) + 1e-08) + 0.1 * weight)
    return (moment_one, moment_two, updated)


def ff_adam_kernel(rank_ref, g0, g1, g2, g3, w_ref, one_ref, two_ref, one_out, two_out, w_out):
    k = pl.program_id(0)

    def put(block, cols):
        results = adam_update(w_ref[:, cols], one_ref[:, cols], two_ref[:, cols], block.astype(f32), 0.02)
        for ref, value in zip((one_out, two_out, w_out), results):
            ref[:, cols] = value

    for flip in range(8):
        grad = (g0, g1, g2, g3)[flip // 2]
        rank = rank_ref[0] ^ flip
        for j in range(3):
            first = jnp.where(k == 2, 2 * FFT + UNIT * j, 2 * UNIT * j + UNIT * k)
            first = pl.multiple_of(first, 128)

            @pl.when(rank < 7)
            def _():
                block = grad[flip % 2, :, pl.ds(first, UNIT)]
                put(block, pl.ds(pl.multiple_of(rank * FFT + j * UNIT, 128), UNIT))

            skip = max(0, 8 * FFT - FF - j * UNIT)
            if skip < UNIT:

                @pl.when(rank == 7)
                def _():
                    block = grad[flip % 2, :, pl.ds(pl.multiple_of(first + skip, 128), UNIT - skip)]
                    start = FF - FFT + j * UNIT + skip
                    put(block, slice(start, start + UNIT - skip))


def ff_adam(rank, grads, weight, moment_one, moment_two):
    third = pl.BlockSpec((ROWS, FF), lambda k: (0, k))
    whole = pl.BlockSpec((2, ROWS, 3 * FFT), lambda k: (0, 0, 0))
    return pl.pallas_call(
        ff_adam_kernel,
        grid=(3,),
        out_shape=(jax.ShapeDtypeStruct((ROWS, 3 * FF), f32),) * 3,
        in_specs=[pl.BlockSpec(memory_space=pltpu.SMEM)] + [whole] * 4 + [third] * 3,
        out_specs=(third,) * 3,
        compiler_params=pltpu.CompilerParams(vmem_limit_bytes=32 * MIB),
    )(rank, *grads, *(pltpu.with_memory_space_constraint(a, pltpu.HBM) for a in (weight, moment_one, moment_two)))


def attn_adam_kernel(flag_ref, part_ref, other_ref, w_ref, one_ref, two_ref, one_out, two_out, w_out):
    def put(grad, start):
        cols = slice(start, start + grad.shape[1])
        results = adam_update(w_ref[:, cols], one_ref[:, cols], two_ref[:, cols], grad, 0.05)
        for ref, value in zip((one_out, two_out, w_out), results):
            ref[:, cols] = value

    part, other = part_ref[...].astype(f32), other_ref[...].astype(f32)
    own_first = flag_ref[0] == 0
    first = jnp.where(own_first, part[:, :COLS], other[:, :COLS])
    last = jnp.where(own_first, other[:, :COLS], part[:, :COLS])
    put(first[:, :QUERY], 0)
    put(last[:, :QUERY], QUERY)
    put(first[:, QUERY : QUERY + HD], D)
    put(last[:, QUERY : QUERY + HD], D + HD)
    put(first[:, QUERY + HD :], D + KV * HD)
    put(last[:, QUERY + HD :], D + KV * HD + HD)
    put(jnp.where(flag_ref[1] == 1, part[:, COLS + HD :], other[:, COLS + HD :]), QKV)


def shards(
    inputs,
    cotangent,
    attn_weight,
    attn_moment_one,
    attn_moment_two,
    mlp_weight,
    mlp_moment_one,
    mlp_moment_two,
    vectors,
    vector_moment_one,
    vector_moment_two,
):
    half = lax.axis_index("seq")
    yh, core = lax.axis_index("yh"), lax.axis_index("core")
    side = half ^ yh
    rank = half * 4 + yh * 2 + core
    scalar = lambda v: v.astype(jnp.int32).reshape(1)
    x_own, dy_own = inputs[0], cotangent[0]

    vec_own = jnp.pad(vectors.astype(bf16)[None, :], ((0, 15), (0, 48)))
    vec_pair = jnp.concatenate([vec_own[:1], cross_send(vec_own)[:1]])
    vec_block = jnp.concatenate([vec_pair, core_send(jnp.pad(vec_pair, ((0, 14), (0, 0))))[:2]])
    vec_block = jnp.pad(vec_block, ((0, ROWS - 4), (0, 0)))

    mlp_keep, mlp_give = cut(scalar(rank), mlp_weight)
    mlp_got = core_send(mlp_give)
    (attn_block,) = call(
        attn_cut_kernel, [((ROWS, COLS + HD + D), bf16)], scalar(side), attn_weight, vec_block, smem=1
    )
    block = ((2, ROWS, 3 * FFT), bf16)
    mlp_near, mlp_far = call(
        order_kernel, [block, block], scalar(core), mlp_keep, mlp_got, smem=1, after=[attn_block]
    )
    mlp_far = cross_send(mlp_far)
    attn_x = join(ring_parts(attn_block, x_send))
    (mlp_block,) = call(
        order_kernel, [((2,) + block[0], bf16)], scalar(yh), mlp_near[None], mlp_far[None], smem=1, after=[attn_x]
    )
    mlp_w = lax.all_gather(mlp_block.reshape(4 * ROWS, 3 * FFT), ("z", "x"), axis=0, tiled=True)
    mlp_w = mlp_w.reshape(4, 4, 2, 48, 3 * FFT)

    blocks = gathered_blocks(64)
    rows = as_rows((blocks[:, None] * ROWS + jnp.arange(ROWS, dtype=jnp.int32)[None, :]).reshape(D))
    z = lax.axis_index("z")
    inside = z // 2 == side
    first_z = jnp.where(inside, z, z ^ 2)
    j = jnp.arange(HALF, dtype=jnp.int32)
    r, xi, zi, yi, ci = j % 24, (j // 24) % 4, (j // 96) % 2, (j // 192) % 2, j // 384
    feature = ((first_z ^ zi) % 2) * 384 + (yh ^ yi) * 192 + (core ^ ci) * 24 + r
    features = as_rows(feature + (lax.axis_index("x") + near(xi) + 4) % 4 * 48)
    (x_rel,) = call(permute_kernel, [((LEN, D), bf16)], rows, x_own, seq_send(x_own), us=2, store=[0])
    dy_parts = gather_tokens(hold(dy_own, attn_x))

    flags = jnp.stack([inside, inside == (z % 2 == 0)]).astype(jnp.int32)
    proj_z, out_z = call(
        near_kernel, [((4 * 4 * ROWS, COLS + HD), bf16), ((2 * 4 * ROWS, D), bf16)], flags,
        *ring_parts(attn_x, z_send), smem=1, after=[x_rel] + dy_parts[1:4],
    )
    proj_y = cross_send(proj_z)
    out_y = cross_send(out_z)
    proj_w = [proj_z, proj_y, core_send(proj_z), core_send(proj_y)]

    place = jnp.arange(64, dtype=jnp.int32)
    by_vector = blocks[(place % 4) % 2 * 16 + (place % 4) // 2 * 32 + place // 4]
    pick = (place[:, None] == by_vector[None, :]).astype(bf16)
    vec_rel = proj_z[:, COLS:].reshape(16, ROWS, HD)[:, :4].reshape(64, HD)
    vec_all = dot(pick, vec_rel)[:, :80].reshape(1, 5120)
    gain_rows = jnp.broadcast_to(vec_all[:, :D].astype(bf16), (16, D))
    gain_one = call(permute_kernel, [((16, D), f32)], rows, gain_rows, us=1)[0][:1]
    gain_two = vec_all[:, D : 2 * D]
    bias_all = vec_all[:, 2 * D :]
    own_cols = lambda a, start, width: lax.dynamic_slice_in_dim(a, start + side * width, width, 1)
    bias = jnp.concatenate(
        [
            own_cols(bias_all, 0, QUERY),
            own_cols(bias_all, D, HD),
            own_cols(bias_all, D + KV * HD, HD),
        ],
        axis=1,
    )

    cos, sin = rotary_tables((jnp.arange(LEN) + half * TOK) % LEN)
    normed, low, heads_out, logs = attend(
        scalar(half), x_rel, gain_one, proj_w, bias, cos, sin
    )
    out_y = hold(out_y, heads_out)
    out_w = [out_z, out_y, core_send(out_z), core_send(out_y)]
    a_rel, branch_own, branch_give = branch(heads_out, features, out_w)
    middle, second = call(
        second_kernel, [((TOK, D), f32), ((TOK, D), bf16)], x_own, branch_own, seq_send(branch_give), gain_two,
        us=2, store=[0],
    )

    hidden, d_gate_up, mlp_term = feed_forward(gather_tokens(second), dy_parts, mlp_w)
    mlp_part = lax.psum_scatter(
        mlp_term.reshape(D, 3 * FFT), ("z", "x"), scatter_dimension=0, tiled=True
    )
    d_second = reduce_tokens(*d_second_terms(d_gate_up, mlp_w))
    down_own, down_give = down_terms(hidden, mlp_w, [d_second[0]])
    d_middle, e, d_gain_two = d_middle_of(d_second, middle, gain_two, dy_own, [down_give])

    e_other = seq_send(e)
    out_term = out_terms(a_rel, e, e_other)
    (out_far,) = add_up([out_term[1], core_send(out_term[3])])
    (out_near,) = add_up([out_term[0], core_send(out_term[2])])
    out_got = cross_send(out_far)
    *proj_term, d_bias_own, dh_own, dh_give, d_gain_one = attend_back(
        scalar(half), e, e_other, out_w, features, low, logs, cos, sin, normed, x_rel, proj_w, [out_far]
    )
    proj_term[3] = hold(proj_term[3], out_got)

    by_core = mlp_part.reshape(2, 2, ROWS, 3 * FFT)
    of_core = lambda c: lax.dynamic_index_in_dim(by_core, c, 1, keepdims=False)
    pair = jnp.stack([of_core(core), core_send(of_core(1 - core))], axis=1)
    near_rows = lax.dynamic_index_in_dim(pair, yh, 0, keepdims=False)
    far_rows = lax.dynamic_index_in_dim(pair, 1 - yh, 0, keepdims=False)
    grads = [near_rows, ring_send(far_rows, "yh", 1), seq_send(near_rows), cross_send(far_rows)]

    (proj_far,) = add_up([proj_term[1], core_send(proj_term[3])])
    (proj_near,) = add_up([proj_term[0], core_send(proj_term[2])])
    bias_zero = jnp.zeros((1, QKV), f32)
    put = lambda a, v, start, width: lax.dynamic_update_slice_in_dim(a, v, start + side * width, 1)
    d_bias = put(bias_zero, d_bias_own[:, :QUERY], 0, QUERY)
    d_bias = put(d_bias, d_bias_own[:, QUERY : QUERY + HD], D, HD)
    d_bias = put(d_bias, d_bias_own[:, QUERY + HD :], D + KV * HD, HD)
    d_gain_rows = jnp.broadcast_to(d_gain_one, (8, D))
    d_gain_one = call(unpermute_kernel, [((8, D), f32)], rows, d_gain_rows, us=2)[0][:1]
    vec_term = jnp.concatenate([d_gain_one, d_gain_two, d_bias], axis=1)
    vec_term = jnp.pad(vec_term.reshape(64, 80), ((0, 0), (0, 48))).astype(bf16)
    pick_rel = (place[:, None] == blocks[None, :]).astype(bf16)
    vec_term = dot_tn(pick_rel, vec_term)
    vec_term = pair_reduce(vec_term, core_send)
    vec_term = pair_reduce(vec_term, cross_send)
    vec_term = jnp.pad(vec_term[:, None, :], ((0, 0), (0, ROWS - 1), (0, 0))).reshape(PIECE, HD)
    attn_parts = call(
        far_kernel, [((4 * ROWS, COLS + HD + D), bf16)] * 4,
        proj_near, cross_send(proj_far), vec_term, out_near, out_got,
    )
    down = reduce_tokens(down_own, hold(down_give, proj_far))
    attn_parts = add_up(
        ring_collect(attn_parts, z_send), pieces=4, after=list(down[1:]) + grads[1:]
    )
    (attn_part,) = add_up(ring_collect(attn_parts, x_send))
    attn_other = seq_send(attn_part)
    vec_cols = slice(COLS, COLS + 80)
    vec_grad = attn_part[0, vec_cols].astype(f32) + attn_other[0, vec_cols].astype(f32)

    mlp_one, mlp_two, mlp_new = ff_adam(
        scalar(rank), grads, mlp_weight, mlp_moment_one, mlp_moment_two
    )
    attn_one, attn_two, attn_new = call(
        attn_adam_kernel,
        [((ROWS, QKV + D), f32)] * 3,
        jnp.stack([side, inside.astype(side.dtype)]).astype(jnp.int32),
        attn_part,
        attn_other,
        attn_weight,
        attn_moment_one,
        attn_moment_two,
        smem=1,
    )

    total = down[0] + down[1].astype(f32) + down[2].astype(f32) + down[3].astype(f32)
    output = (middle + total).astype(bf16)[None]
    (input_grad,) = call(
        input_grad_kernel, [((TOK, D), f32)], dh_own, seq_send(dh_give), x_rel, gain_one, d_middle, rows,
        us=5, fetch=[0, 2, 4], after=[proj_far],
    )
    vec_one, vec_two, vec_new = adam_update(
        vectors, vector_moment_one, vector_moment_two, vec_grad, 0.5
    )
    return (
        output,
        input_grad[None],
        attn_one,
        attn_two,
        attn_new,
        mlp_one,
        mlp_two,
        mlp_new,
        vec_one,
        vec_two,
        vec_new,
    )


def solution(mesh):
    grid = Mesh(mesh.devices.reshape(2, 4, 2, 4, 2), ("seq",) + FSDP)
    tokens, rows, vector = P(FSDP, "seq", None), P(FSDP, None), P(FSDP)
    return jax.shard_map(
        shards,
        mesh=grid,
        in_specs=(tokens, tokens) + (rows,) * 6 + (vector,) * 3,
        out_specs=(tokens, tokens) + (rows,) * 6 + (vector,) * 3,
        check_vma=False,
    )
```

```python
import math

import jax
import jax.numpy as jnp
from jax import lax
from jax.experimental import pallas as pl
from jax.experimental.pallas import tpu as pltpu
from jax.sharding import Mesh
from jax.sharding import PartitionSpec as P

D = 1536
H = 12
KV = 2
HD = 128
FF = 8960
STEP = 10
QKV = 2048
ROWS = 24
TOK = 128
LEN = 256
HALF = D // 2
GROUP = H // KV
QUERY = GROUP * HD
COLS = QUERY + 2 * HD
FFT = 1152
UNIT = FFT // 3
PIECE = D // 4
LINE = HALF // 4
MIB = 1024 * 1024

norm_eps = 1e-06
rope_base = 1000000.0
f32 = jnp.float32
bf16 = jnp.bfloat16
contract_rows = (((0,), (0,)), ((), ()))
contract_cols = (((1,), (1,)), ((), ()))
score_scale = HD ** (-0.5)
FSDP = ("z", "yh", "x", "core")
SIZES = {"seq": 2, "z": 4, "yh": 2, "x": 4, "core": 2}


def dot(a, b):
    return jnp.dot(a, b, preferred_element_type=f32)


def dot_tn(a, b):
    return lax.dot_general(a, b, contract_rows, preferred_element_type=f32)


def dot_nt(a, b):
    return lax.dot_general(a, b, contract_cols, preferred_element_type=f32)


def split_dot_nt(a, b):
    high = a.astype(bf16)
    low = (a - high.astype(f32)).astype(bf16)
    return dot_nt(high, b) + dot_nt(low, b)


def ring_send(values, axis, shift):
    size = SIZES[axis]
    return lax.ppermute(values, axis, [(i, (i + shift) % size) for i in range(size)])


def x_send(values, shift):
    return ring_send(values, "x", shift)


def z_send(values, shift):
    return ring_send(values, "z", shift)


def y_send(values, shift):
    place = lambda y: (y % 2) * 2 + y // 2
    return lax.ppermute(
        values, ("seq", "yh"), [(place(i), place((i + shift) % 4)) for i in range(4)]
    )


def cross_send(values):
    return lax.ppermute(values, ("seq", "yh"), [(i, 3 - i) for i in range(4)])


def core_send(values):
    return ring_send(values, "core", 1)


def seq_send(values):
    return ring_send(values, "seq", 1)


def ring_parts(values, send):
    return [values, send(values, 1), send(values, -1), send(values, 2)]


def pair_reduce(values, send):
    rows = values.shape[0] // 2
    return values[:rows] + send(values[rows:].astype(bf16)).astype(f32)


def ring_collect(parts, send):
    return [parts[0], send(parts[1], -1), send(parts[2], 1), send(parts[3], 2)]


def gather_tokens(values):
    parts = ring_parts(values, y_send)
    return parts + [core_send(p) for p in parts]


def near(index):
    return jnp.where(index == 1, -1, jnp.where(index == 0, 0, index - 1))


def gathered_blocks(count):
    j = jnp.arange(count, dtype=jnp.int32)
    xi, zi, yi, ci = j % 4, (j // 4) % 4, (j // 16) % 2, j // 32
    z = (lax.axis_index("z") + near(zi) + 4) % 4
    x = (lax.axis_index("x") + near(xi) + 4) % 4
    yh = (lax.axis_index("yh") + yi) % 2
    core = (lax.axis_index("core") + ci) % 2
    return z * 16 + yh * 8 + x * 2 + core


def call(
    kernel, outs, *args, us=1, smem=0, fetch=(), raw=(), store=(), raw_outs=(), scratch=(), room=6, after=(), behind=(), late=()
):
    vmem, hbm = pl.BlockSpec(memory_space=pltpu.VMEM), pl.BlockSpec(memory_space=pltpu.HBM)
    fetch = [g if isinstance(g, tuple) else (g,) for g in fetch]
    far = set(raw) | {i for g in fetch for i in g}
    specs = [
        pl.BlockSpec(memory_space=pltpu.SMEM) if i < smem else hbm if i in far else vmem
        for i in range(len(args))
    ] + [pl.BlockSpec(memory_space=pl.ANY)] * len(after) + [hbm] * len(behind)
    after = list(after) + [pltpu.with_memory_space_constraint(a, pltpu.HBM) for a in behind]
    buffers = []
    for g in fetch:
        rows = sum(args[i].shape[0] for i in g)
        buffers.append(((rows,) + args[g[0]].shape[1:], args[g[0]].dtype))
    buffers += [outs[i] for i in store]
    held = [pltpu.VMEM(shape, kind) for shape, kind in buffers]
    moves = max(1, sum(len(g) for g in fetch) + len(store))
    n_in, n_out, n_own = len(args), len(outs), len(scratch)

    def body(*refs):
        ins, refs = list(refs[:n_in]), refs[n_in + len(after) :]
        out_refs, own = list(refs[:n_out]), refs[n_out : n_out + n_own]
        held_refs, sems = refs[n_out + n_own : -1], refs[-1]
        copies, last, k = [], [], 0
        for n, (g, ref) in enumerate(zip(fetch, held_refs)):
            row = 0
            for i in g:
                rows = args[i].shape[0]
                copy = pltpu.make_async_copy(ins[i], ref.at[pl.ds(row, rows)], sems.at[k])
                (last if n in late else copies).append(copy)
                row, k = row + rows, k + 1
            ins[g[0]] = ref
        for copy in copies + last:
            copy.start()
        for copy in copies:
            copy.wait()

        def wait_late():
            for copy in last:
                copy.wait()

        drop = {i for g in fetch for i in g[1:]}
        ins = [ref for i, ref in enumerate(ins) if i not in drop]
        leaving = []
        for i, ref in zip(store, held_refs[len(fetch) :]):
            leaving.append(pltpu.make_async_copy(ref, out_refs[i], sems.at[k]))
            out_refs[i] = ref
            k += 1
        kernel(*([wait_late] if late else []), *ins, *out_refs, *own)
        for copy in leaving:
            copy.start()
        for copy in leaving:
            copy.wait()

    size = lambda shape, kind: math.prod(shape) * jnp.dtype(kind).itemsize
    used = sum(size(*b) for b in buffers)
    used += sum(size(b.shape, b.dtype) for b in scratch if hasattr(b, "shape") and b.memory_space == pltpu.VMEM)
    args = [
        pltpu.with_memory_space_constraint(a, pltpu.HBM) if i in far else a
        for i, a in enumerate(args)
    ]
    leave = lambda i: pltpu.HBM if i in raw_outs or i in store else jax.ShapeDtypeStruct
    return pl.pallas_call(
        body,
        out_shape=tuple(leave(i)(shape, kind) for i, (shape, kind) in enumerate(outs)),
        in_specs=specs,
        out_specs=tuple(hbm if i in raw_outs or i in store else vmem for i in range(n_out)),
        scratch_shapes=list(scratch) + held + [pltpu.SemaphoreType.DMA((moves,))],
        cost_estimate=pl.CostEstimate(flops=us * 10**7, bytes_accessed=us * 10**4, transcendentals=0),
        compiler_params=pltpu.CompilerParams(vmem_limit_bytes=used + room * MIB),
    )(*args, *after)


def hold_kernel(*refs):
    pass


def hold(values, *after):
    anywhere = pl.BlockSpec(memory_space=pl.ANY)
    return pl.pallas_call(
        hold_kernel,
        out_shape=jax.ShapeDtypeStruct(values.shape, values.dtype),
        in_specs=[anywhere] * (1 + len(after)),
        out_specs=anywhere,
        input_output_aliases={0: 0},
    )(values, *after)


def join_kernel(*refs):
    out_ref, row = refs[-1], 0
    for ref in refs[:-1]:
        out_ref[row : row + ref.shape[0], :] = ref[...]
        row += ref.shape[0]


def join(parts, after=()):
    rows = sum(p.shape[0] for p in parts)
    return call(join_kernel, [((rows, parts[0].shape[1]), bf16)], *parts, after=after)[0]


def sum_kernel(count, given, outs):
    groups = []
    for i in range(0, len(given), count):
        total = given[i][...].astype(f32)
        for ref in given[i + 1 : i + count]:
            total = total + ref[...].astype(f32)
        groups.append(total)
    rows, col = outs[0].shape[0], 0
    for total in groups:
        for i, ref in enumerate(outs):
            part = total[i * rows : (i + 1) * rows, :]
            ref[:, col : col + total.shape[1]] = part.astype(ref.dtype)
        col += total.shape[1]


def add_up(parts, pieces=1, count=None, after=(), behind=()):
    count = count or len(parts)
    cols = sum(p.shape[1] for p in parts[::count])
    outs = [((parts[0].shape[0] // pieces, cols), bf16)] * pieces
    kernel = lambda *refs: sum_kernel(count, refs[: len(parts)], refs[len(parts) :])
    return call(kernel, outs, *parts, after=after, behind=behind)


def place(rows_ref, size, cols):
    row = lax.broadcasted_iota(jnp.int32, (size, cols.stop - cols.start), 0)
    return jnp.where(row == rows_ref[:1, cols], 1.0, 0.0).astype(bf16)


PIECES = [slice(i * PIECE, (i + 1) * PIECE) for i in range(4)]


def permute_kernel(rows_ref, *refs):
    out_ref = refs[-1]
    for cols in PIECES:
        here, row = place(rows_ref, D, cols), 0
        for ref in refs[:-1]:
            out_ref[row : row + ref.shape[0], cols] = dot(ref[...], here).astype(out_ref.dtype)
            row += ref.shape[0]


def unpermute_kernel(rows_ref, values_ref, out_ref):
    out = jnp.zeros(out_ref.shape, f32)
    for cols in PIECES:
        out += split_dot_nt(values_ref[:, cols], place(rows_ref, D, cols))
    out_ref[...] = out


def as_rows(rows):
    return jnp.broadcast_to(rows[None, :].astype(jnp.int32), (8, rows.shape[0]))


def rotary_tables(positions):
    half_dim = HD // 2
    freqs = rope_base ** (-jnp.arange(half_dim, dtype=f32) * 2.0 / HD)
    angles = positions.astype(f32)[:, None] * freqs[None, :]
    cos, sin = jnp.cos(angles), jnp.sin(angles)
    return jnp.concatenate([cos, cos], axis=1), jnp.concatenate([-sin, sin], axis=1)


def causal_mask(half):
    row = (lax.broadcasted_iota(jnp.int32, (LEN, LEN), 0) + half * TOK) % LEN
    col = (lax.broadcasted_iota(jnp.int32, (LEN, LEN), 1) + half * TOK) % LEN
    return row >= col


def norm_scale(values):
    return lax.rsqrt(jnp.mean(values * values, axis=-1, keepdims=True) + norm_eps)


def attend_kernel(
    wait_weights, half_ref, x_ref, gain_ref, w_ref, bias_ref, cos_ref, sin_ref,
    normed_ref, low_ref, out_ref, log_ref, qkv_ref,
):
    x = x_ref[...].astype(f32)
    normed_ref[...] = (x * norm_scale(x) * gain_ref[...]).astype(bf16)
    wait_weights()
    qkv_ref[...] = dot(normed_ref[...], w_ref[:, :COLS]) + bias_ref[...]
    cos, sin = cos_ref[...], sin_ref[...]
    mask = causal_mask(half_ref[0])

    def rotated(start):
        z = qkv_ref[:, start : start + HD]
        return (z * cos + pltpu.roll(z, HD // 2, 1) * sin).astype(bf16)

    key = rotated(QUERY)
    low_ref[:, QUERY : QUERY + HD] = key
    value = qkv_ref[:, QUERY + HD :].astype(bf16)
    low_ref[:, QUERY + HD :] = value
    for h in range(GROUP):
        query = rotated(h * HD)
        low_ref[:, h * HD : (h + 1) * HD] = query
        scores = jnp.where(mask, dot_nt(query, key) * score_scale, -1e30)
        top = jnp.max(scores, axis=-1, keepdims=True)
        total = top + jnp.log(jnp.sum(jnp.exp(scores - top), axis=-1, keepdims=True))
        log_ref[h] = jnp.broadcast_to(total, (LEN, HD))
        probs = jnp.exp(scores - total).astype(bf16)
        out_ref[:, h * HD : (h + 1) * HD] = dot(probs, value).astype(bf16)


def attend(half, x_rel, gain, proj, bias, cos, sin):
    outs = [((LEN, D), bf16), ((LEN, COLS), bf16), ((LEN, QUERY), bf16), ((GROUP, LEN, HD), f32)]
    return call(
        attend_kernel, outs, half, x_rel, gain, *proj, bias, cos, sin,
        us=6, smem=1, fetch=[1, (3, 4, 5, 6)], late=[1], store=[0, 1, 3], scratch=[pltpu.VMEM((LEN, COLS), f32)],
    )


def branch_kernel(a_ref, rows_ref, w_ref, rel_ref, own_ref, give_ref):
    rel_ref[...] = dot(a_ref[...], place(rows_ref, HALF, slice(0, HALF))).astype(bf16)
    own_ref[...] = dot(rel_ref[:TOK, :], w_ref[...])
    give_ref[...] = dot(rel_ref[TOK:, :], w_ref[...]).astype(bf16)


def branch(a, rows, out_w):
    outs = [((LEN, HALF), bf16), ((TOK, D), f32), ((TOK, D), bf16)]
    return call(branch_kernel, outs, a, rows, *out_w, us=4, fetch=[(2, 3, 4, 5)], store=[0])


def second_kernel(x_ref, own_ref, got_ref, gain_ref, middle_ref, second_ref):
    middle = x_ref[...].astype(f32) + own_ref[...] + got_ref[...].astype(f32)
    middle_ref[...] = middle
    second_ref[...] = (middle * norm_scale(middle) * gain_ref[...]).astype(bf16)


def load_tokens(parts, whole, sems):
    copies = []
    for i, part in enumerate(parts):
        copies.append(pltpu.make_async_copy(part, whole.at[pl.ds(i * TOK, TOK), :], sems.at[i]))
        copies[-1].start()
    return copies


def ff_kernel(*refs):
    h_parts, dy_parts, refs = refs[:8], refs[8:16], refs[16:]
    w_ref, hid_out, dgu_out, own_ref, give_ref, h_all, dy_all, w, hid, dgu, h_sem, dy_sem, w_sem, out_sem = refs
    tokens = load_tokens(h_parts, h_all, h_sem) + load_tokens(dy_parts, dy_all, dy_sem)
    loads = []
    for j in range(3):
        for k, (start, width) in enumerate(((2 * UNIT * j, 2 * UNIT), (2 * FFT + UNIT * j, UNIT))):
            for y in range(2):
                copy = pltpu.make_async_copy(
                    w_ref.at[:, :, y, :, pl.ds(start, width)],
                    w.at[:, y, :, :, pl.ds(start, width)],
                    w_sem.at[j * 4 + k * 2 + y],
                )
                copy.start()
                loads.append(copy)
    for copy in tokens:
        copy.wait()
    tile = 512
    for j in range(3):
        for copy in loads[4 * j : 4 * j + 4]:
            copy.wait()

        @pl.loop(0, 8 * TOK // tile)
        def _(m):
            rows = pl.ds(pl.multiple_of(m * tile, tile), tile)
            pair = slice(2 * UNIT * j, 2 * UNIT * (j + 1))
            last = slice(2 * FFT + UNIT * j, 2 * FFT + UNIT * (j + 1))
            gate_up = dot(h_all[rows, :], w[:, :, :, :, pair].reshape(D, 2 * UNIT))
            d_hidden = dot(dy_all[rows, :], w[:, :, :, :, last].reshape(D, UNIT))
            gate, up = gate_up[:, :UNIT], gate_up[:, UNIT:]
            sigmoid_gate = jax.nn.sigmoid(gate)
            act = gate * sigmoid_gate
            hid[rows, UNIT * j : UNIT * (j + 1)] = (act * up).astype(bf16)
            d_gate = d_hidden * up * (sigmoid_gate * (1.0 + gate * (1.0 - sigmoid_gate)))
            dgu[rows, 2 * UNIT * j : 2 * UNIT * j + UNIT] = d_gate.astype(bf16)
            dgu[rows, 2 * UNIT * j + UNIT : 2 * UNIT * (j + 1)] = (d_hidden * act).astype(bf16)

    outs = [
        pltpu.make_async_copy(hid, hid_out, out_sem.at[0]),
        pltpu.make_async_copy(dgu, dgu_out, out_sem.at[1]),
    ]
    for copy in outs:
        copy.start()
    for z in range(4):
        wz = w[z, :, :, :, : 2 * FFT].reshape(PIECE, 2 * FFT)
        for i, ref in enumerate((own_ref, give_ref)):
            rows = slice(i * 4 * TOK, (i + 1) * 4 * TOK)
            ref[:, z * PIECE : (z + 1) * PIECE] = dot_nt(dgu[rows, :], wz).astype(ref.dtype)
    for copy in outs:
        copy.wait()


def feed_forward(h_parts, dy_parts, w):
    tokens = 8 * TOK
    outs = [
        ((tokens, FFT), bf16),
        ((tokens, 2 * FFT), bf16),
        ((4 * TOK, D), f32),
        ((4 * TOK, D), bf16),
    ]
    scratch = [
        pltpu.VMEM((tokens, D), bf16),
        pltpu.VMEM((tokens, D), bf16),
        pltpu.VMEM((4, 2, 4, 48, 3 * FFT), bf16),
        pltpu.VMEM((tokens, FFT), bf16),
        pltpu.VMEM((tokens, 2 * FFT), bf16),
        pltpu.SemaphoreType.DMA((8,)),
        pltpu.SemaphoreType.DMA((8,)),
        pltpu.SemaphoreType.DMA((12,)),
        pltpu.SemaphoreType.DMA((2,)),
    ]
    return call(
        ff_kernel, outs, *h_parts, *dy_parts, w, us=25, raw=range(17), raw_outs=(0, 1), scratch=scratch
    )


def ff_grad_kernel(*refs):
    h_parts, dy_parts, refs = refs[:8], refs[8:16], refs[16:]
    hid_ref, dgu_ref, term_ref, h_all, dy_all, hid, dgu, term, h_sem, dy_sem, in_sem, t_sem = refs
    first = load_tokens(h_parts, h_all, h_sem) + [pltpu.make_async_copy(dgu_ref, dgu, in_sem.at[0])]
    first[-1].start()
    last = load_tokens(dy_parts, dy_all, dy_sem) + [pltpu.make_async_copy(hid_ref, hid, in_sem.at[1])]
    last[-1].start()
    for copy in first:
        copy.wait()
    outs = []
    for z in range(4):
        cols = slice(z * PIECE, (z + 1) * PIECE)
        for start in range(0, 3 * FFT, 2 * UNIT):
            width = min(2 * UNIT, 3 * FFT - start)
            if start < 2 * FFT:
                out = dot_tn(h_all[:, cols], dgu[:, start : start + width])
            else:
                if z == 0 and start == 2 * FFT:
                    for copy in last:
                        copy.wait()
                out = dot_tn(dy_all[:, cols], hid[:, start - 2 * FFT : start - 2 * FFT + width])
            term[z, :, :, :, start : start + width] = out.astype(bf16).reshape(2, 4, 48, width)
        for y in range(2):
            copy = pltpu.make_async_copy(term.at[z, y], term_ref.at[z, :, y], t_sem.at[z, y])
            copy.start()
            outs.append(copy)
    for copy in outs:
        copy.wait()


def ff_grad(h_parts, dy_parts, hid, dgu, after):
    tokens = 8 * TOK
    scratch = [
        pltpu.VMEM((tokens, D), bf16),
        pltpu.VMEM((tokens, D), bf16),
        pltpu.VMEM((tokens, FFT), bf16),
        pltpu.VMEM((tokens, 2 * FFT), bf16),
        pltpu.VMEM((4, 2, 4, 48, 3 * FFT), bf16),
        pltpu.SemaphoreType.DMA((8,)),
        pltpu.SemaphoreType.DMA((8,)),
        pltpu.SemaphoreType.DMA((2,)),
        pltpu.SemaphoreType.DMA((4, 2)),
    ]
    return call(
        ff_grad_kernel, [((4, 4, 2, 48, 3 * FFT), bf16)], *h_parts, *dy_parts, hid, dgu,
        us=17, raw=range(18), raw_outs=(0,), scratch=scratch, after=after,
    )[0]


def down_kernel(hid_ref, w_ref, own_ref, give_ref, w, w_sem):
    loads = []
    for z in range(4):
        for y in range(2):
            load = pltpu.make_async_copy(
                w_ref.at[z, :, y, :, pl.ds(2 * FFT, FFT)], w.at[z, y], w_sem.at[z, y]
            )
            load.start()
            loads.append(load)
    for z in range(4):
        for load in loads[2 * z : 2 * z + 2]:
            load.wait()
        wz = w[z].reshape(PIECE, FFT)
        for i, ref in enumerate((own_ref, give_ref)):
            rows = slice(i * 4 * TOK, (i + 1) * 4 * TOK)
            ref[:, z * PIECE : (z + 1) * PIECE] = dot_nt(hid_ref[rows, :], wz).astype(ref.dtype)


def down_terms(hidden, w, after):
    outs = [((4 * TOK, D), f32), ((4 * TOK, D), bf16)]
    scratch = [pltpu.VMEM((4, 2, 4, 48, FFT), bf16), pltpu.SemaphoreType.DMA((4, 2))]
    return call(
        down_kernel, outs, hidden, w, us=8, fetch=[0], raw=(1,), store=[0], scratch=scratch, after=after
    )


def add_kernel(own_ref, got_ref, keep_ref, g1_ref, g2_ref, g3_ref):
    for i, ref in enumerate((keep_ref, g1_ref, g2_ref, g3_ref)):
        rows = slice(i * TOK, (i + 1) * TOK)
        ref[...] = (own_ref[rows, :] + got_ref[rows, :].astype(f32)).astype(ref.dtype)


def d_middle_kernel(p0, p1, p2, p3, middle_ref, gain_ref, dy_ref, d_middle_ref, e_ref, d_gain_ref):
    d_second = p0[...] + p1[...].astype(f32) + p2[...].astype(f32) + p3[...].astype(f32)
    middle = middle_ref[...]
    inv = norm_scale(middle)
    unit = middle * inv
    scaled = d_second * gain_ref[...]
    d_gain_ref[...] = jnp.sum(d_second * unit, axis=0, keepdims=True)
    d_middle = dy_ref[...].astype(f32) + inv * (
        scaled - unit * jnp.mean(scaled * unit, axis=-1, keepdims=True)
    )
    d_middle_ref[...] = d_middle
    e_ref[...] = d_middle.astype(bf16)


def d_middle_of(parts, middle, gain, dy, behind):
    outs = [((TOK, D), f32), ((TOK, D), bf16), ((1, D), f32)]
    return call(
        d_middle_kernel, outs, *parts, middle, gain, dy, us=2, fetch=[4, 6], store=[0], behind=behind
    )


def out_term_kernel(a_ref, e0_ref, e1_ref, t0, t1, t2, t3):
    total = dot_tn(a_ref[:TOK, :], e0_ref[...]) + dot_tn(a_ref[TOK:, :], e1_ref[...])
    for i, ref in enumerate((t0, t1, t2, t3)):
        ref[...] = total[i * LINE : (i + 1) * LINE, :].astype(bf16)


def out_terms(a_rel, e, e_other, after):
    outs = [((LINE, D), bf16)] * 4
    return call(out_term_kernel, outs, a_rel, e, e_other, us=20000, fetch=[0], room=10, after=after)


def attend_back_kernel(
    wait_normed, half_ref, e0_ref, e1_ref, out_w_ref, rows_ref, low_ref, log_ref, cos_ref, sin_ref, normed_ref,
    t0, t1, t2, t3, out_ref, sum_ref, grad_ref,
):
    cos, sin = cos_ref[...], sin_ref[...]
    mask = causal_mask(half_ref[0])
    here = place(rows_ref, HALF, slice(0, HALF))
    for i, e_ref in enumerate((e0_ref, e1_ref)):
        rel = dot_nt(e_ref[...], out_w_ref[...]).astype(bf16)
        grad_ref[i * TOK : (i + 1) * TOK, :] = dot_nt(rel, here).astype(bf16)
    key = low_ref[:, QUERY : QUERY + HD]
    value = low_ref[:, QUERY + HD :]

    def unrotated(z):
        return (z * cos - pltpu.roll(z, HD // 2, 1) * sin).astype(bf16)

    def put(start, block):
        out_ref[:, start : start + HD] = block
        sum_ref[:, start : start + HD] = jnp.sum(block.astype(f32), axis=0, keepdims=True)

    d_key = jnp.zeros((LEN, HD), f32)
    d_value = jnp.zeros((LEN, HD), f32)
    for h in range(GROUP):
        query = low_ref[:, h * HD : (h + 1) * HD]
        grad = grad_ref[:, h * HD : (h + 1) * HD]
        scores = jnp.where(mask, dot_nt(query, key) * score_scale, -1e30)
        total = log_ref[h]
        probs = jnp.exp(scores - jnp.concatenate([total, total], axis=1))
        d_probs = dot_nt(grad, value)
        delta = jnp.sum(probs * d_probs, axis=-1, keepdims=True)
        d_scores = (probs * (d_probs - delta)).astype(bf16)
        put(h * HD, unrotated(dot(d_scores, key) * score_scale))
        d_key += dot_tn(d_scores, query)
        d_value += dot_tn(probs.astype(bf16), grad)
    put(QUERY, unrotated(d_key * score_scale))
    put(QUERY + HD, d_value.astype(bf16))
    wait_normed()
    for i, ref in enumerate((t0, t1, t2, t3)):
        ref[...] = dot_tn(normed_ref[:, i * PIECE : (i + 1) * PIECE], out_ref[...]).astype(bf16)


def attend_back(half, e, e_other, out_w, rows, low, logs, cos, sin, normed, after):
    outs = [((PIECE, COLS), bf16)] * 4 + [((LEN, COLS), bf16), ((1, COLS), f32)]
    return call(
        attend_back_kernel, outs, half, e, e_other, *out_w, rows, low, logs, cos, sin, normed,
        us=9, smem=1, fetch=[(3, 4, 5, 6), 8, 9, 12], late=[3], scratch=[pltpu.VMEM((LEN, QUERY), bf16)],
        room=8, after=after,
    )


def d_normed_kernel(d_ref, x_ref, w_ref, own_ref, give_ref, d_gain_ref):
    x = x_ref[...].astype(f32)
    d_normed = dot_nt(d_ref[...], w_ref[:, :COLS])
    own_ref[...] = d_normed[:TOK, :]
    give_ref[...] = d_normed[TOK:, :].astype(bf16)
    d_gain_ref[...] = jnp.sum(d_normed * (x * norm_scale(x)), axis=0, keepdims=True)


def d_normed_of(d_proj, x_rel, proj, after):
    outs = [((TOK, D), f32), ((TOK, D), bf16), ((1, D), f32)]
    return call(
        d_normed_kernel, outs, d_proj, x_rel, *proj, us=3, fetch=[1, (2, 3, 4, 5)], store=[0, 1], room=8, after=after
    )


def input_grad_kernel(own_ref, got_ref, x_ref, gain_ref, d_middle_ref, rows_ref, out_ref):
    scaled = (own_ref[...] + got_ref[...].astype(f32)) * gain_ref[...]
    x = x_ref[:TOK, :].astype(f32)
    inv = norm_scale(x)
    unit = x * inv
    through = inv * (scaled - unit * jnp.mean(scaled * unit, axis=-1, keepdims=True))
    total = d_middle_ref[...]
    for cols in PIECES:
        total += split_dot_nt(through[:, cols], place(rows_ref, D, cols))
    out_ref[...] = total


def cut_kernel(rank_ref, weight_ref, keep_ref, send_ref, held_ref, sem):
    col = lax.broadcasted_iota(jnp.int32, (ROWS, UNIT), 1)
    ranks = [rank_ref[0] ^ flip for flip in (1, 7, 0, 6)]
    starts = [jnp.minimum(rank * FFT, FF - FFT) for rank in ranks]
    copies = []
    for n, start in enumerate(starts):
        for k in range(3):
            first = pl.multiple_of(k * FF + start, 128)
            copies.append(
                pltpu.make_async_copy(
                    weight_ref.at[:, pl.ds(first, FFT)], held_ref.at[n, k], sem.at[n, k]
                )
            )
            copies[-1].start()
    for n, (rank, start) in enumerate(zip(ranks, starts)):
        ref, i = (send_ref, n) if n < 2 else (keep_ref, n - 2)
        for copy in copies[3 * n : 3 * n + 3]:
            copy.wait()
        for j in range(3):
            inside = col >= rank * FFT - start - j * UNIT
            for k, to in enumerate((2 * UNIT * j, 2 * UNIT * j + UNIT, 2 * FFT + UNIT * j)):
                piece = held_ref[n, k, :, j * UNIT : (j + 1) * UNIT]
                ref[i, :, to : to + UNIT] = jnp.where(inside, piece, 0.0).astype(bf16)


def cut(rank, weight):
    scratch = [pltpu.VMEM((4, 3, ROWS, FFT), f32), pltpu.SemaphoreType.DMA((4, 3))]
    outs = [((2, ROWS, 3 * FFT), bf16)] * 2
    return call(cut_kernel, outs, rank, weight, us=2, smem=1, raw=(1,), scratch=scratch)


def near_kernel(flag_ref, own, before, after, across, proj_ref, out_ref):
    for i, ref in enumerate((own, before, after, across)):
        proj_ref[i * 4 * ROWS : (i + 1) * 4 * ROWS, :] = ref[:, : COLS + HD]
    rest = slice(COLS + HD, COLS + HD + D)
    first = jnp.where(flag_ref[0] == 1, own[:, rest], across[:, rest])
    second = jnp.where(flag_ref[1] == 1, after[:, rest], before[:, rest])
    out_ref[: 4 * ROWS, :] = first
    out_ref[4 * ROWS :, :] = second


def far_kernel(proj, proj_got, vec, out, out_got, o0, o1, o2, o3):
    total = proj[...].astype(f32) + proj_got[...].astype(f32)
    rest = out[...].astype(f32) + out_got[...].astype(f32)
    for i, ref in enumerate((o0, o1, o2, o3)):
        rows = slice(i * 4 * ROWS, (i + 1) * 4 * ROWS)
        ref[:, :COLS] = total[rows, :].astype(bf16)
        ref[:, COLS : COLS + HD] = vec[rows, :].astype(bf16)
        half = slice(0, 4 * ROWS) if i in (0, 3) else slice(4 * ROWS, 8 * ROWS)
        ref[:, COLS + HD :] = rest[half, :].astype(bf16)


def order_kernel(place_ref, keep_ref, got_ref, *outs):
    place = place_ref[0]
    for i, ref in enumerate(outs):
        ref[place] = keep_ref[i]
        ref[1 - place] = got_ref[i]


def attn_cut_kernel(side_ref, weight_ref, vec_ref, out_ref):
    side = side_ref[0]
    for start, width, to in ((0, QUERY, 0), (D, HD, QUERY), (D + KV * HD, HD, QUERY + HD)):
        first = pl.multiple_of(start + side * width, 128)
        out_ref[:, to : to + width] = weight_ref[:, pl.ds(first, width)].astype(bf16)
    out_ref[:, COLS : COLS + HD] = vec_ref[...]
    out_ref[:, COLS + HD :] = weight_ref[:, QKV:].astype(bf16)


def adam_update(weight, moment_one, moment_two, gradient, step_rate):
    moment_one = 0.9 * moment_one + 0.1 * gradient
    moment_two = 0.95 * moment_two + 0.05 * gradient * gradient
    first_hat = moment_one / (1.0 - 0.9**STEP)
    second_hat = moment_two / (1.0 - 0.95**STEP)
    updated = weight - step_rate * (first_hat / (jnp.sqrt(second_hat) + 1e-08) + 0.1 * weight)
    return (moment_one, moment_two, updated)


def ff_adam_kernel(rank_ref, g0, g1, g2, g3, w_ref, one_ref, two_ref, one_out, two_out, w_out):
    k = pl.program_id(0)

    def put(block, cols):
        results = adam_update(w_ref[:, cols], one_ref[:, cols], two_ref[:, cols], block.astype(f32), 0.02)
        for ref, value in zip((one_out, two_out, w_out), results):
            ref[:, cols] = value

    for flip in range(8):
        grad = (g0, g1, g2, g3)[flip // 2]
        rank = rank_ref[0] ^ flip
        for j in range(3):
            first = jnp.where(k == 2, 2 * FFT + UNIT * j, 2 * UNIT * j + UNIT * k)
            first = pl.multiple_of(first, 128)

            @pl.when(rank < 7)
            def _():
                block = grad[flip % 2, :, pl.ds(first, UNIT)]
                put(block, pl.ds(pl.multiple_of(rank * FFT + j * UNIT, 128), UNIT))

            skip = max(0, 8 * FFT - FF - j * UNIT)
            if skip < UNIT:

                @pl.when(rank == 7)
                def _():
                    block = grad[flip % 2, :, pl.ds(pl.multiple_of(first + skip, 128), UNIT - skip)]
                    start = FF - FFT + j * UNIT + skip
                    put(block, slice(start, start + UNIT - skip))


def ff_adam(rank, grads, weight, moment_one, moment_two):
    third = pl.BlockSpec((ROWS, FF), lambda k: (0, k))
    whole = pl.BlockSpec((2, ROWS, 3 * FFT), lambda k: (0, 0, 0))
    return pl.pallas_call(
        ff_adam_kernel,
        grid=(3,),
        out_shape=(jax.ShapeDtypeStruct((ROWS, 3 * FF), f32),) * 3,
        in_specs=[pl.BlockSpec(memory_space=pltpu.SMEM)] + [whole] * 4 + [third] * 3,
        out_specs=(third,) * 3,
        compiler_params=pltpu.CompilerParams(vmem_limit_bytes=32 * MIB),
    )(rank, *grads, *(pltpu.with_memory_space_constraint(a, pltpu.HBM) for a in (weight, moment_one, moment_two)))


def attn_adam_kernel(flag_ref, part_ref, other_ref, w_ref, one_ref, two_ref, one_out, two_out, w_out):
    def put(grad, start):
        cols = slice(start, start + grad.shape[1])
        results = adam_update(w_ref[:, cols], one_ref[:, cols], two_ref[:, cols], grad, 0.05)
        for ref, value in zip((one_out, two_out, w_out), results):
            ref[:, cols] = value

    part, other = part_ref[...].astype(f32), other_ref[...].astype(f32)
    own_first = flag_ref[0] == 0
    first = jnp.where(own_first, part[:, :COLS], other[:, :COLS])
    last = jnp.where(own_first, other[:, :COLS], part[:, :COLS])
    put(first[:, :QUERY], 0)
    put(last[:, :QUERY], QUERY)
    put(first[:, QUERY : QUERY + HD], D)
    put(last[:, QUERY : QUERY + HD], D + HD)
    put(first[:, QUERY + HD :], D + KV * HD)
    put(last[:, QUERY + HD :], D + KV * HD + HD)
    put(jnp.where(flag_ref[1] == 1, part[:, COLS + HD :], other[:, COLS + HD :]), QKV)


def shards(
    inputs,
    cotangent,
    attn_weight,
    attn_moment_one,
    attn_moment_two,
    mlp_weight,
    mlp_moment_one,
    mlp_moment_two,
    vectors,
    vector_moment_one,
    vector_moment_two,
):
    half = lax.axis_index("seq")
    yh, core = lax.axis_index("yh"), lax.axis_index("core")
    side = half ^ yh
    rank = half * 4 + yh * 2 + core
    scalar = lambda v: v.astype(jnp.int32).reshape(1)
    x_own, dy_own = inputs[0], cotangent[0]

    vec_own = jnp.pad(vectors.astype(bf16)[None, :], ((0, 15), (0, 48)))
    vec_pair = jnp.concatenate([vec_own[:1], cross_send(vec_own)[:1]])
    vec_block = jnp.concatenate([vec_pair, core_send(jnp.pad(vec_pair, ((0, 14), (0, 0))))[:2]])
    vec_block = jnp.pad(vec_block, ((0, ROWS - 4), (0, 0)))

    mlp_keep, mlp_give = cut(scalar(rank), mlp_weight)
    mlp_got = core_send(mlp_give)
    (attn_block,) = call(
        attn_cut_kernel, [((ROWS, COLS + HD + D), bf16)], scalar(side), attn_weight, vec_block, smem=1
    )
    block = ((2, ROWS, 3 * FFT), bf16)
    mlp_near, mlp_far = call(
        order_kernel, [block, block], scalar(core), mlp_keep, mlp_got, smem=1, after=[attn_block]
    )
    mlp_far = cross_send(mlp_far)
    attn_x = join(ring_parts(attn_block, x_send))
    blocks = gathered_blocks(64)
    rows = as_rows((blocks[:, None] * ROWS + jnp.arange(ROWS, dtype=jnp.int32)[None, :]).reshape(D))
    z = lax.axis_index("z")
    inside = z // 2 == side
    first_z = jnp.where(inside, z, z ^ 2)
    j = jnp.arange(HALF, dtype=jnp.int32)
    r, xi, zi, yi, ci = j % 24, (j // 24) % 4, (j // 96) % 2, (j // 192) % 2, j // 384
    feature = ((first_z ^ zi) % 2) * 384 + (yh ^ yi) * 192 + (core ^ ci) * 24 + r
    features = as_rows(feature + (lax.axis_index("x") + near(xi) + 4) % 4 * 48)
    (x_rel,) = call(permute_kernel, [((LEN, D), bf16)], rows, x_own, seq_send(x_own), us=2, store=[0])
    dy_parts = gather_tokens(hold(dy_own, attn_x))

    flags = jnp.stack([inside, inside == (z % 2 == 0)]).astype(jnp.int32)
    proj_z, out_z = call(
        near_kernel, [((4 * 4 * ROWS, COLS + HD), bf16), ((2 * 4 * ROWS, D), bf16)], flags,
        *ring_parts(attn_x, z_send), smem=1, after=dy_parts[1:4], behind=[x_rel],
    )

    (mlp_block,) = call(
        order_kernel, [((2,) + block[0], bf16)], scalar(yh), mlp_near[None], mlp_far[None], smem=1, after=[proj_z]
    )
    mlp_w = lax.all_gather(mlp_block.reshape(4 * ROWS, 3 * FFT), ("z", "x"), axis=0, tiled=True)
    mlp_w = mlp_w.reshape(4, 4, 2, 48, 3 * FFT)

    proj_y = cross_send(proj_z)
    out_y = cross_send(out_z)
    proj_w = [proj_z, proj_y, core_send(proj_z), core_send(proj_y)]

    place = jnp.arange(64, dtype=jnp.int32)
    by_vector = blocks[(place % 4) % 2 * 16 + (place % 4) // 2 * 32 + place // 4]
    pick = (place[:, None] == by_vector[None, :]).astype(bf16)
    vec_rel = proj_z[:, COLS:].reshape(16, ROWS, HD)[:, :4].reshape(64, HD)
    vec_all = dot(pick, vec_rel)[:, :80].reshape(1, 5120)
    gain_rows = jnp.broadcast_to(vec_all[:, :D].astype(bf16), (16, D))
    gain_one = call(permute_kernel, [((16, D), f32)], rows, gain_rows, us=1)[0][:1]
    gain_two = vec_all[:, D : 2 * D]
    bias_all = vec_all[:, 2 * D :]
    own_cols = lambda a, start, width: lax.dynamic_slice_in_dim(a, start + side * width, width, 1)
    bias = jnp.concatenate(
        [
            own_cols(bias_all, 0, QUERY),
            own_cols(bias_all, D, HD),
            own_cols(bias_all, D + KV * HD, HD),
        ],
        axis=1,
    )

    cos, sin = rotary_tables((jnp.arange(LEN) + half * TOK) % LEN)
    normed, low, heads_out, logs = attend(
        scalar(half), x_rel, gain_one, proj_w, bias, cos, sin
    )
    out_y = hold(out_y, heads_out)
    out_w = [out_z, out_y, core_send(out_z), core_send(out_y)]
    a_rel, branch_own, branch_give = branch(heads_out, features, out_w)
    middle, second = call(
        second_kernel, [((TOK, D), f32), ((TOK, D), bf16)], x_own, branch_own, seq_send(branch_give), gain_two,
        us=2, store=[0],
    )

    second_parts = gather_tokens(second)
    hidden, d_gate_up, d_second_own, d_second_give = feed_forward(second_parts, dy_parts, mlp_w)
    d_second = call(
        add_kernel, [((TOK, D), f32)] + [((TOK, D), bf16)] * 3, d_second_own, core_send(d_second_give)
    )
    mlp_term = ff_grad(second_parts, dy_parts, hidden, d_gate_up, [d_second[0]])
    mlp_part = lax.psum_scatter(
        mlp_term.reshape(D, 3 * FFT), ("z", "x"), scatter_dimension=0, tiled=True
    )
    d_middle, e, d_gain_two = d_middle_of(
        ring_collect(d_second, y_send), middle, gain_two, dy_own, [mlp_term]
    )
    down_own, down_give = down_terms(hidden, mlp_w, [e])

    e_other = seq_send(e)
    out_term = out_terms(a_rel, e, e_other, [down_give])
    (out_far,) = add_up([out_term[1], core_send(out_term[3])])
    (out_near,) = add_up([out_term[0], core_send(out_term[2])])
    out_got = cross_send(out_far)
    *proj_term, d_proj, d_bias_own = attend_back(
        scalar(half), e, e_other, out_w, features, low, logs, cos, sin, normed, [out_far]
    )

    by_core = mlp_part.reshape(2, 2, ROWS, 3 * FFT)
    of_core = lambda c: lax.dynamic_index_in_dim(by_core, c, 1, keepdims=False)
    pair = jnp.stack([of_core(core), core_send(of_core(1 - core))], axis=1)
    near_rows = lax.dynamic_index_in_dim(pair, yh, 0, keepdims=False)
    far_rows = lax.dynamic_index_in_dim(pair, 1 - yh, 0, keepdims=False)
    grads = [near_rows, ring_send(far_rows, "yh", 1), seq_send(near_rows), cross_send(far_rows)]

    (proj_far,) = add_up([proj_term[1], core_send(proj_term[3])])
    (proj_near,) = add_up([proj_term[0], core_send(proj_term[2])])
    dh_own, dh_give, d_gain_one = d_normed_of(hold(d_proj, out_got), x_rel, proj_w, [proj_far])
    bias_zero = jnp.zeros((1, QKV), f32)
    put = lambda a, v, start, width: lax.dynamic_update_slice_in_dim(a, v, start + side * width, 1)
    d_bias = put(bias_zero, d_bias_own[:, :QUERY], 0, QUERY)
    d_bias = put(d_bias, d_bias_own[:, QUERY : QUERY + HD], D, HD)
    d_bias = put(d_bias, d_bias_own[:, QUERY + HD :], D + KV * HD, HD)
    d_gain_rows = jnp.broadcast_to(d_gain_one, (8, D))
    d_gain_one = call(unpermute_kernel, [((8, D), f32)], rows, d_gain_rows, us=2)[0][:1]
    vec_term = jnp.concatenate([d_gain_one, d_gain_two, d_bias], axis=1)
    vec_term = jnp.pad(vec_term.reshape(64, 80), ((0, 0), (0, 48))).astype(bf16)
    pick_rel = (place[:, None] == blocks[None, :]).astype(bf16)
    vec_term = dot_tn(pick_rel, vec_term)
    vec_term = pair_reduce(vec_term, core_send)
    vec_term = pair_reduce(vec_term, cross_send)
    vec_term = jnp.pad(vec_term[:, None, :], ((0, 0), (0, ROWS - 1), (0, 0))).reshape(PIECE, HD)
    down = call(
        add_kernel, [((TOK, D), f32)] + [((TOK, D), bf16)] * 3, down_own, core_send(hold(down_give, proj_far))
    )
    dh_got = seq_send(dh_give)
    attn_parts = call(
        far_kernel, [((4 * ROWS, COLS + HD + D), bf16)] * 4,
        proj_near, cross_send(proj_far), vec_term, out_near, out_got, after=[down[1], dh_got],
    )
    down = ring_collect(down, y_send)
    (input_grad,) = call(
        input_grad_kernel, [((TOK, D), f32)], dh_own, dh_got, x_rel, gain_one, d_middle, rows,
        us=5, fetch=[0, 2, 4], store=[0], after=[attn_parts[0]],
    )
    attn_parts = add_up(ring_collect(attn_parts, z_send), pieces=4, after=down[1:], behind=[input_grad])
    (attn_part,) = add_up(ring_collect(attn_parts, x_send), after=[near_rows, far_rows])
    mlp_one, mlp_two, mlp_new = ff_adam(
        scalar(rank), grads, mlp_weight, mlp_moment_one, mlp_moment_two
    )
    attn_other = seq_send(attn_part)
    vec_cols = slice(COLS, COLS + 80)
    vec_grad = attn_part[0, vec_cols].astype(f32) + attn_other[0, vec_cols].astype(f32)

    attn_one, attn_two, attn_new = call(
        attn_adam_kernel,
        [((ROWS, QKV + D), f32)] * 3,
        jnp.stack([side, inside.astype(side.dtype)]).astype(jnp.int32),
        attn_part,
        attn_other,
        attn_weight,
        attn_moment_one,
        attn_moment_two,
        smem=1,
        behind=[mlp_one],
    )

    total = down[0] + down[1].astype(f32) + down[2].astype(f32) + down[3].astype(f32)
    output = (middle + total).astype(bf16)[None]
    vec_one, vec_two, vec_new = adam_update(
        vectors, vector_moment_one, vector_moment_two, vec_grad, 0.5
    )
    return (
        output,
        input_grad[None],
        attn_one,
        attn_two,
        attn_new,
        mlp_one,
        mlp_two,
        mlp_new,
        vec_one,
        vec_two,
        vec_new,
    )


def solution(mesh):
    grid = Mesh(mesh.devices.reshape(2, 4, 2, 4, 2), ("seq",) + FSDP)
    tokens, rows, vector = P(FSDP, "seq", None), P(FSDP, None), P(FSDP)
    return jax.shard_map(
        shards,
        mesh=grid,
        in_specs=(tokens, tokens) + (rows,) * 6 + (vector,) * 3,
        out_specs=(tokens, tokens) + (rows,) * 6 + (vector,) * 3,
        check_vma=False,
    )
```

```python
import math

import jax
import jax.numpy as jnp
from jax import lax
from jax.experimental import pallas as pl
from jax.experimental.pallas import tpu as pltpu
from jax.sharding import Mesh
from jax.sharding import PartitionSpec as P

D = 1536
H = 12
KV = 2
HD = 128
FF = 8960
STEP = 10
QKV = 2048
ROWS = 24
TOK = 128
LEN = 256
HALF = D // 2
GROUP = H // KV
QUERY = GROUP * HD
COLS = QUERY + 2 * HD
FFT = 1152
UNIT = FFT // 3
PIECE = D // 4
LINE = HALF // 4
MIB = 1024 * 1024

norm_eps = 1e-06
rope_base = 1000000.0
f32 = jnp.float32
bf16 = jnp.bfloat16
contract_rows = (((0,), (0,)), ((), ()))
contract_cols = (((1,), (1,)), ((), ()))
score_scale = HD ** (-0.5)
FSDP = ("z", "yh", "x", "core")
SIZES = {"seq": 2, "z": 4, "yh": 2, "x": 4, "core": 2}


def dot(a, b):
    return jnp.dot(a, b, preferred_element_type=f32)


def dot_tn(a, b):
    return lax.dot_general(a, b, contract_rows, preferred_element_type=f32)


def dot_nt(a, b):
    return lax.dot_general(a, b, contract_cols, preferred_element_type=f32)


def split_dot_nt(a, b):
    high = a.astype(bf16)
    low = (a - high.astype(f32)).astype(bf16)
    return dot_nt(high, b) + dot_nt(low, b)


def ring_send(values, axis, shift):
    size = SIZES[axis]
    return lax.ppermute(values, axis, [(i, (i + shift) % size) for i in range(size)])


def x_send(values, shift):
    return ring_send(values, "x", shift)


def z_send(values, shift):
    return ring_send(values, "z", shift)


def y_send(values, shift):
    place = lambda y: (y % 2) * 2 + y // 2
    return lax.ppermute(
        values, ("seq", "yh"), [(place(i), place((i + shift) % 4)) for i in range(4)]
    )


def cross_send(values):
    return lax.ppermute(values, ("seq", "yh"), [(i, 3 - i) for i in range(4)])


def core_send(values):
    return ring_send(values, "core", 1)


def seq_send(values):
    return ring_send(values, "seq", 1)


def ring_parts(values, send):
    return [values, send(values, 1), send(values, -1), send(values, 2)]


def pair_reduce(values, send):
    rows = values.shape[0] // 2
    return values[:rows] + send(values[rows:].astype(bf16)).astype(f32)


def ring_collect(parts, send):
    return [parts[0], send(parts[1], -1), send(parts[2], 1), send(parts[3], 2)]


def gather_tokens(values):
    parts = ring_parts(values, y_send)
    return parts + [core_send(p) for p in parts]


def near(index):
    return jnp.where(index == 1, -1, jnp.where(index == 0, 0, index - 1))


def gathered_blocks(count):
    j = jnp.arange(count, dtype=jnp.int32)
    xi, zi, yi, ci = j % 4, (j // 4) % 4, (j // 16) % 2, j // 32
    z = (lax.axis_index("z") + near(zi) + 4) % 4
    x = (lax.axis_index("x") + near(xi) + 4) % 4
    yh = (lax.axis_index("yh") + yi) % 2
    core = (lax.axis_index("core") + ci) % 2
    return z * 16 + yh * 8 + x * 2 + core


def call(
    kernel, outs, *args, us=1, smem=0, fetch=(), raw=(), store=(), raw_outs=(), scratch=(), room=6, after=(), behind=(), late=()
):
    vmem, hbm = pl.BlockSpec(memory_space=pltpu.VMEM), pl.BlockSpec(memory_space=pltpu.HBM)
    fetch = [g if isinstance(g, tuple) else (g,) for g in fetch]
    far = set(raw) | {i for g in fetch for i in g}
    specs = [
        pl.BlockSpec(memory_space=pltpu.SMEM) if i < smem else hbm if i in far else vmem
        for i in range(len(args))
    ] + [pl.BlockSpec(memory_space=pl.ANY)] * len(after) + [hbm] * len(behind)
    after = list(after) + [in_hbm(a) for a in behind]
    buffers = []
    for g in fetch:
        rows = sum(args[i].shape[0] for i in g)
        buffers.append(((rows,) + args[g[0]].shape[1:], args[g[0]].dtype))
    buffers += [outs[i] for i in store]
    held = [pltpu.VMEM(shape, kind) for shape, kind in buffers]
    moves = max(1, sum(len(g) for g in fetch) + len(store))
    n_in, n_out, n_own = len(args), len(outs), len(scratch)

    def body(*refs):
        ins, refs = list(refs[:n_in]), refs[n_in + len(after) :]
        out_refs, own = list(refs[:n_out]), refs[n_out : n_out + n_own]
        held_refs, sems = refs[n_out + n_own : -1], refs[-1]
        copies, last, k = [], [], 0
        for n, (g, ref) in enumerate(zip(fetch, held_refs)):
            row = 0
            for i in g:
                rows = args[i].shape[0]
                copy = pltpu.make_async_copy(ins[i], ref.at[pl.ds(row, rows)], sems.at[k])
                (last if n in late else copies).append(copy)
                row, k = row + rows, k + 1
            ins[g[0]] = ref
        for copy in copies + last:
            copy.start()
        for copy in copies:
            copy.wait()

        def wait_late():
            for copy in last:
                copy.wait()

        drop = {i for g in fetch for i in g[1:]}
        ins = [ref for i, ref in enumerate(ins) if i not in drop]
        leaving = []
        for i, ref in zip(store, held_refs[len(fetch) :]):
            leaving.append(pltpu.make_async_copy(ref, out_refs[i], sems.at[k]))
            out_refs[i] = ref
            k += 1
        kernel(*([wait_late] if late else []), *ins, *out_refs, *own)
        for copy in leaving:
            copy.start()
        for copy in leaving:
            copy.wait()

    size = lambda shape, kind: math.prod(shape) * jnp.dtype(kind).itemsize
    used = sum(size(*b) for b in buffers)
    used += sum(size(b.shape, b.dtype) for b in scratch if hasattr(b, "shape") and b.memory_space == pltpu.VMEM)
    args = [
        in_hbm(a) if i in far else a
        for i, a in enumerate(args)
    ]
    leave = lambda i: pltpu.HBM if i in raw_outs or i in store else jax.ShapeDtypeStruct
    return pl.pallas_call(
        body,
        out_shape=tuple(leave(i)(shape, kind) for i, (shape, kind) in enumerate(outs)),
        in_specs=specs,
        out_specs=tuple(hbm if i in raw_outs or i in store else vmem for i in range(n_out)),
        scratch_shapes=list(scratch) + held + [pltpu.SemaphoreType.DMA((moves,))],
        cost_estimate=pl.CostEstimate(flops=us * 10**7, bytes_accessed=us * 10**4, transcendentals=0),
        compiler_params=pltpu.CompilerParams(vmem_limit_bytes=used + room * MIB),
    )(*args, *after)


def hold_kernel(*refs):
    pass


def in_hbm(values):
    return pltpu.with_memory_space_constraint(values, pltpu.HBM)


def hold(values, *after, behind=()):
    anywhere, hbm = pl.BlockSpec(memory_space=pl.ANY), pl.BlockSpec(memory_space=pltpu.HBM)
    return pl.pallas_call(
        hold_kernel,
        out_shape=jax.ShapeDtypeStruct(values.shape, values.dtype),
        in_specs=[anywhere] * (1 + len(after)) + [hbm] * len(behind),
        out_specs=anywhere,
        input_output_aliases={0: 0},
    )(values, *after, *(in_hbm(a) for a in behind))


def join_kernel(*refs):
    out_ref, row = refs[-1], 0
    for ref in refs[:-1]:
        out_ref[row : row + ref.shape[0], :] = ref[...]
        row += ref.shape[0]


def join(parts):
    rows = sum(p.shape[0] for p in parts)
    return call(join_kernel, [((rows, parts[0].shape[1]), bf16)], *parts)[0]


def sum_kernel(count, given, outs):
    groups = []
    for i in range(0, len(given), count):
        total = given[i][...].astype(f32)
        for ref in given[i + 1 : i + count]:
            total = total + ref[...].astype(f32)
        groups.append(total)
    rows, col = outs[0].shape[0], 0
    for total in groups:
        for i, ref in enumerate(outs):
            part = total[i * rows : (i + 1) * rows, :]
            ref[:, col : col + total.shape[1]] = part.astype(ref.dtype)
        col += total.shape[1]


def add_up(parts, pieces=1, count=None, after=(), behind=(), fetch=False):
    count = count or len(parts)
    cols = sum(p.shape[1] for p in parts[::count])
    outs = [((parts[0].shape[0] // pieces, cols), bf16)] * pieces
    kernel = lambda *refs: sum_kernel(count, refs[: len(parts)], refs[len(parts) :])
    fetch = range(len(parts)) if fetch else ()
    return call(kernel, outs, *parts, after=after, behind=behind, fetch=fetch)


def place(rows_ref, size, cols):
    row = lax.broadcasted_iota(jnp.int32, (size, cols.stop - cols.start), 0)
    return jnp.where(row == rows_ref[:1, cols], 1.0, 0.0).astype(bf16)


PIECES = [slice(i * PIECE, (i + 1) * PIECE) for i in range(4)]


def permute_kernel(rows_ref, *refs):
    out_ref = refs[-1]
    for cols in PIECES:
        here, row = place(rows_ref, D, cols), 0
        for ref in refs[:-1]:
            out_ref[row : row + ref.shape[0], cols] = dot(ref[...], here).astype(out_ref.dtype)
            row += ref.shape[0]


def unpermute_kernel(rows_ref, values_ref, out_ref):
    out = jnp.zeros(out_ref.shape, f32)
    for cols in PIECES:
        out += split_dot_nt(values_ref[:, cols], place(rows_ref, D, cols))
    out_ref[...] = out


def as_rows(rows):
    return jnp.broadcast_to(rows[None, :].astype(jnp.int32), (8, rows.shape[0]))


def rotary_tables(positions):
    half_dim = HD // 2
    freqs = rope_base ** (-jnp.arange(half_dim, dtype=f32) * 2.0 / HD)
    angles = positions.astype(f32)[:, None] * freqs[None, :]
    cos, sin = jnp.cos(angles), jnp.sin(angles)
    return jnp.concatenate([cos, cos], axis=1), jnp.concatenate([-sin, sin], axis=1)


def causal_mask(half):
    row = (lax.broadcasted_iota(jnp.int32, (LEN, LEN), 0) + half * TOK) % LEN
    col = (lax.broadcasted_iota(jnp.int32, (LEN, LEN), 1) + half * TOK) % LEN
    return row >= col


def norm_scale(values):
    return lax.rsqrt(jnp.mean(values * values, axis=-1, keepdims=True) + norm_eps)


def attend_kernel(
    wait_weights, half_ref, x_ref, gain_ref, w_ref, bias_ref, cos_ref, sin_ref,
    normed_ref, low_ref, out_ref, log_ref, qkv_ref,
):
    x = x_ref[...].astype(f32)
    normed_ref[...] = (x * norm_scale(x) * gain_ref[...]).astype(bf16)
    wait_weights()
    qkv_ref[...] = dot(normed_ref[...], w_ref[...]) + bias_ref[...]
    cos, sin = cos_ref[...], sin_ref[...]
    mask = causal_mask(half_ref[0])

    def rotated(start):
        z = qkv_ref[:, start : start + HD]
        return (z * cos + pltpu.roll(z, HD // 2, 1) * sin).astype(bf16)

    key = rotated(QUERY)
    low_ref[:, QUERY : QUERY + HD] = key
    value = qkv_ref[:, QUERY + HD :].astype(bf16)
    low_ref[:, QUERY + HD :] = value
    for h in range(GROUP):
        query = rotated(h * HD)
        low_ref[:, h * HD : (h + 1) * HD] = query
        scores = jnp.where(mask, dot_nt(query, key) * score_scale, -1e30)
        top = jnp.max(scores, axis=-1, keepdims=True)
        total = top + jnp.log(jnp.sum(jnp.exp(scores - top), axis=-1, keepdims=True))
        log_ref[h] = jnp.broadcast_to(total, (LEN, HD))
        probs = jnp.exp(scores - total).astype(bf16)
        out_ref[:, h * HD : (h + 1) * HD] = dot(probs, value).astype(bf16)


def attend(half, x_rel, gain, proj, bias, cos, sin):
    outs = [((LEN, D), bf16), ((LEN, COLS), bf16), ((LEN, QUERY), bf16), ((GROUP, LEN, HD), f32)]
    return call(
        attend_kernel, outs, half, x_rel, gain, *proj, bias, cos, sin,
        us=6, smem=1, fetch=[1, (3, 4, 5, 6)], late=[1], store=[0, 1, 3], scratch=[pltpu.VMEM((LEN, COLS), f32)],
    )


def branch_kernel(a_ref, rows_ref, w_ref, rel_ref, own_ref, give_ref):
    rel_ref[...] = dot(a_ref[...], place(rows_ref, HALF, slice(0, HALF))).astype(bf16)
    own_ref[...] = dot(rel_ref[:TOK, :], w_ref[...])
    give_ref[...] = dot(rel_ref[TOK:, :], w_ref[...]).astype(bf16)


def branch(a, rows, out_w):
    outs = [((LEN, HALF), bf16), ((TOK, D), f32), ((TOK, D), bf16)]
    return call(branch_kernel, outs, a, rows, *out_w, us=4, fetch=[(2, 3, 4, 5)], store=[0])


def second_kernel(x_ref, own_ref, got_ref, gain_ref, middle_ref, second_ref):
    middle = x_ref[...].astype(f32) + own_ref[...] + got_ref[...].astype(f32)
    middle_ref[...] = middle
    second_ref[...] = (middle * norm_scale(middle) * gain_ref[...]).astype(bf16)


def load_tokens(parts, whole, sems):
    copies = []
    for i, part in enumerate(parts):
        copies.append(pltpu.make_async_copy(part, whole.at[pl.ds(i * TOK, TOK), :], sems.at[i]))
        copies[-1].start()
    return copies


def ff_kernel(*refs):
    h_parts, dy_parts, refs = refs[:8], refs[8:16], refs[16:]
    w_ref, hid_out, dgu_out, own_ref, give_ref, h_all, dy_all, w, hid, dgu, h_sem, dy_sem, w_sem, out_sem = refs
    tokens = load_tokens(h_parts, h_all, h_sem) + load_tokens(dy_parts, dy_all, dy_sem)
    loads = []
    for j in range(3):
        for k, (start, width) in enumerate(((2 * UNIT * j, 2 * UNIT), (2 * FFT + UNIT * j, UNIT))):
            for y in range(2):
                copy = pltpu.make_async_copy(
                    w_ref.at[:, :, y, :, pl.ds(start, width)],
                    w.at[:, y, :, :, pl.ds(start, width)],
                    w_sem.at[j * 4 + k * 2 + y],
                )
                copy.start()
                loads.append(copy)
    for copy in tokens:
        copy.wait()
    tile = 512
    for j in range(3):
        for copy in loads[4 * j : 4 * j + 4]:
            copy.wait()

        @pl.loop(0, 8 * TOK // tile)
        def _(m):
            rows = pl.ds(pl.multiple_of(m * tile, tile), tile)
            pair = slice(2 * UNIT * j, 2 * UNIT * (j + 1))
            last = slice(2 * FFT + UNIT * j, 2 * FFT + UNIT * (j + 1))
            gate_up = dot(h_all[rows, :], w[:, :, :, :, pair].reshape(D, 2 * UNIT))
            d_hidden = dot(dy_all[rows, :], w[:, :, :, :, last].reshape(D, UNIT))
            gate, up = gate_up[:, :UNIT], gate_up[:, UNIT:]
            sigmoid_gate = jax.nn.sigmoid(gate)
            act = gate * sigmoid_gate
            hid[rows, UNIT * j : UNIT * (j + 1)] = (act * up).astype(bf16)
            d_gate = d_hidden * up * (sigmoid_gate * (1.0 + gate * (1.0 - sigmoid_gate)))
            dgu[rows, 2 * UNIT * j : 2 * UNIT * j + UNIT] = d_gate.astype(bf16)
            dgu[rows, 2 * UNIT * j + UNIT : 2 * UNIT * (j + 1)] = (d_hidden * act).astype(bf16)

    outs = [
        pltpu.make_async_copy(hid, hid_out, out_sem.at[0]),
        pltpu.make_async_copy(dgu, dgu_out, out_sem.at[1]),
    ]
    for copy in outs:
        copy.start()
    for z in range(4):
        wz = w[z, :, :, :, : 2 * FFT].reshape(PIECE, 2 * FFT)
        for i, ref in enumerate((own_ref, give_ref)):
            rows = slice(i * 4 * TOK, (i + 1) * 4 * TOK)
            ref[:, z * PIECE : (z + 1) * PIECE] = dot_nt(dgu[rows, :], wz).astype(ref.dtype)
    for copy in outs:
        copy.wait()


def feed_forward(h_parts, dy_parts, w):
    tokens = 8 * TOK
    outs = [
        ((tokens, FFT), bf16),
        ((tokens, 2 * FFT), bf16),
        ((4 * TOK, D), f32),
        ((4 * TOK, D), bf16),
    ]
    scratch = [
        pltpu.VMEM((tokens, D), bf16),
        pltpu.VMEM((tokens, D), bf16),
        pltpu.VMEM((4, 2, 4, 48, 3 * FFT), bf16),
        pltpu.VMEM((tokens, FFT), bf16),
        pltpu.VMEM((tokens, 2 * FFT), bf16),
        pltpu.SemaphoreType.DMA((8,)),
        pltpu.SemaphoreType.DMA((8,)),
        pltpu.SemaphoreType.DMA((12,)),
        pltpu.SemaphoreType.DMA((2,)),
    ]
    return call(
        ff_kernel, outs, *h_parts, *dy_parts, w, us=25, raw=range(17), raw_outs=(0, 1), scratch=scratch
    )


def ff_grad_kernel(*refs):
    h_parts, dy_parts, refs = refs[:8], refs[8:16], refs[16:]
    hid_ref, dgu_ref, term_ref, h_all, dy_all, hid, dgu, term, h_sem, dy_sem, in_sem, t_sem = refs
    last = load_tokens(dy_parts, dy_all, dy_sem) + [pltpu.make_async_copy(hid_ref, hid, in_sem.at[1])]
    last[-1].start()
    first = load_tokens(h_parts, h_all, h_sem) + [pltpu.make_async_copy(dgu_ref, dgu, in_sem.at[0])]
    first[-1].start()
    for copy in last:
        copy.wait()
    outs = []
    for z in range(4):
        cols = slice(z * PIECE, (z + 1) * PIECE)
        for start in (2 * FFT, 2 * FFT + 2 * UNIT, 0, 2 * UNIT, 4 * UNIT):
            width = min(2 * UNIT, 3 * FFT - start)
            if start >= 2 * FFT:
                out = dot_tn(dy_all[:, cols], hid[:, start - 2 * FFT : start - 2 * FFT + width])
            else:
                if z == 0 and start == 0:
                    for copy in first:
                        copy.wait()
                out = dot_tn(h_all[:, cols], dgu[:, start : start + width])
            term[z, :, :, :, start : start + width] = out.astype(bf16).reshape(2, 4, 48, width)
        for y in range(2):
            copy = pltpu.make_async_copy(term.at[z, y], term_ref.at[z, :, y], t_sem.at[z, y])
            copy.start()
            outs.append(copy)
    for copy in outs:
        copy.wait()


def ff_grad(h_parts, dy_parts, hid, dgu, after):
    tokens = 8 * TOK
    scratch = [
        pltpu.VMEM((tokens, D), bf16),
        pltpu.VMEM((tokens, D), bf16),
        pltpu.VMEM((tokens, FFT), bf16),
        pltpu.VMEM((tokens, 2 * FFT), bf16),
        pltpu.VMEM((4, 2, 4, 48, 3 * FFT), bf16),
        pltpu.SemaphoreType.DMA((8,)),
        pltpu.SemaphoreType.DMA((8,)),
        pltpu.SemaphoreType.DMA((2,)),
        pltpu.SemaphoreType.DMA((4, 2)),
    ]
    return call(
        ff_grad_kernel, [((4, 4, 2, 48, 3 * FFT), bf16)], *h_parts, *dy_parts, hid, dgu,
        us=17, raw=range(18), raw_outs=(0,), scratch=scratch, after=after,
    )[0]


def down_kernel(hid_ref, w_ref, own_ref, give_ref, w, w_sem):
    loads = []
    for z in range(4):
        for y in range(2):
            load = pltpu.make_async_copy(
                w_ref.at[z, :, y, :, pl.ds(2 * FFT, FFT)], w.at[z, y], w_sem.at[z, y]
            )
            load.start()
            loads.append(load)
    for z in range(4):
        for load in loads[2 * z : 2 * z + 2]:
            load.wait()
        wz = w[z].reshape(PIECE, FFT)
        for i, ref in enumerate((own_ref, give_ref)):
            rows = slice(i * 4 * TOK, (i + 1) * 4 * TOK)
            ref[:, z * PIECE : (z + 1) * PIECE] = dot_nt(hid_ref[rows, :], wz).astype(ref.dtype)


def down_terms(hidden, w, after):
    outs = [((4 * TOK, D), f32), ((4 * TOK, D), bf16)]
    scratch = [pltpu.VMEM((4, 2, 4, 48, FFT), bf16), pltpu.SemaphoreType.DMA((4, 2))]
    return call(
        down_kernel, outs, hidden, w, us=8, fetch=[0], raw=(1,), store=[0], scratch=scratch, after=after
    )


def add_kernel(own_ref, got_ref, keep_ref, g1_ref, g2_ref, g3_ref):
    for i, ref in enumerate((keep_ref, g1_ref, g2_ref, g3_ref)):
        rows = slice(i * TOK, (i + 1) * TOK)
        ref[...] = (own_ref[rows, :] + got_ref[rows, :].astype(f32)).astype(ref.dtype)


def d_middle_kernel(p0, p1, p2, p3, middle_ref, gain_ref, dy_ref, d_middle_ref, e_ref, d_gain_ref):
    d_second = p0[...] + p1[...].astype(f32) + p2[...].astype(f32) + p3[...].astype(f32)
    middle = middle_ref[...]
    inv = norm_scale(middle)
    unit = middle * inv
    scaled = d_second * gain_ref[...]
    d_gain_ref[...] = jnp.sum(d_second * unit, axis=0, keepdims=True)
    d_middle = dy_ref[...].astype(f32) + inv * (
        scaled - unit * jnp.mean(scaled * unit, axis=-1, keepdims=True)
    )
    d_middle_ref[...] = d_middle
    e_ref[...] = d_middle.astype(bf16)


def d_middle_of(parts, middle, gain, dy, behind):
    outs = [((TOK, D), f32), ((TOK, D), bf16), ((1, D), f32)]
    return call(
        d_middle_kernel, outs, *parts, middle, gain, dy, us=20000, fetch=[4, 6], store=[0], behind=behind
    )


def out_term_kernel(a_ref, e0_ref, e1_ref, t0, t1, t2, t3):
    total = dot_tn(a_ref[:TOK, :], e0_ref[...]) + dot_tn(a_ref[TOK:, :], e1_ref[...])
    for i, ref in enumerate((t0, t1, t2, t3)):
        ref[...] = total[i * LINE : (i + 1) * LINE, :].astype(bf16)


def out_terms(a_rel, e, e_other, after):
    outs = [((LINE, D), bf16)] * 4
    return call(out_term_kernel, outs, a_rel, e, e_other, us=2, fetch=[0], store=range(4), room=10, after=after)


def attend_back_kernel(
    wait_normed, half_ref, e0_ref, e1_ref, out_w_ref, rows_ref, low_ref, log_ref, cos_ref, sin_ref, normed_ref,
    t0, t1, t2, t3, t4, out_ref, sum_ref, grad_ref,
):
    cos, sin = cos_ref[...], sin_ref[...]
    mask = causal_mask(half_ref[0])
    here = place(rows_ref, HALF, slice(0, HALF))
    for i, e_ref in enumerate((e0_ref, e1_ref)):
        rel = dot_nt(e_ref[...], out_w_ref[...]).astype(bf16)
        grad_ref[i * TOK : (i + 1) * TOK, :] = dot_nt(rel, here).astype(bf16)
    key = low_ref[:, QUERY : QUERY + HD]
    value = low_ref[:, QUERY + HD :]

    def unrotated(z):
        return (z * cos - pltpu.roll(z, HD // 2, 1) * sin).astype(bf16)

    def put(start, block):
        out_ref[:, start : start + HD] = block
        sum_ref[:, start : start + HD] = jnp.sum(block.astype(f32), axis=0, keepdims=True)

    d_key = jnp.zeros((LEN, HD), f32)
    d_value = jnp.zeros((LEN, HD), f32)
    for h in range(GROUP):
        query = low_ref[:, h * HD : (h + 1) * HD]
        grad = grad_ref[:, h * HD : (h + 1) * HD]
        scores = jnp.where(mask, dot_nt(query, key) * score_scale, -1e30)
        total = log_ref[h]
        probs = jnp.exp(scores - jnp.concatenate([total, total], axis=1))
        d_probs = dot_nt(grad, value)
        delta = jnp.sum(probs * d_probs, axis=-1, keepdims=True)
        d_scores = (probs * (d_probs - delta)).astype(bf16)
        put(h * HD, unrotated(dot(d_scores, key) * score_scale))
        d_key += dot_tn(d_scores, query)
        d_value += dot_tn(probs.astype(bf16), grad)
    put(QUERY, unrotated(d_key * score_scale))
    put(QUERY + HD, d_value.astype(bf16))
    wait_normed()
    for i, ref in enumerate((t0, t1, t2)):
        ref[...] = dot_tn(normed_ref[:, i * PIECE : (i + 1) * PIECE], out_ref[...]).astype(bf16)
    last = dot_tn(normed_ref[:, 3 * PIECE :], out_ref[...]).astype(bf16)
    t3[...] = last[:LINE, :]
    t4[...] = last[LINE:, :]


def attend_back(half, e, e_other, out_w, rows, low, logs, cos, sin, normed, after):
    outs = [((PIECE, COLS), bf16)] * 3 + [((LINE, COLS), bf16)] * 2
    outs += [((LEN, COLS), bf16), ((1, COLS), f32)]
    return call(
        attend_back_kernel, outs, half, e, e_other, *out_w, rows, low, logs, cos, sin, normed,
        us=9, smem=1, fetch=[(3, 4, 5, 6), 8, 9, 12], late=[3], store=range(6),
        scratch=[pltpu.VMEM((LEN, QUERY), bf16)],
        room=8, after=after,
    )


def d_normed_kernel(d_ref, x_ref, w_ref, own_ref, give_ref, d_gain_ref):
    x = x_ref[...].astype(f32)
    d_normed = dot_nt(d_ref[...], w_ref[...])
    own_ref[...] = d_normed[:TOK, :]
    give_ref[...] = d_normed[TOK:, :].astype(bf16)
    d_gain_ref[...] = jnp.sum(d_normed * (x * norm_scale(x)), axis=0, keepdims=True)


def d_normed_of(d_proj, x_rel, proj):
    outs = [((TOK, D), f32), ((TOK, D), bf16), ((1, D), f32)]
    return call(
        d_normed_kernel, outs, d_proj, x_rel, *proj, us=3, fetch=[0, 1, (2, 3, 4, 5)], store=[0, 1], room=8
    )


def input_grad_kernel(own_ref, got_ref, x_ref, gain_ref, d_middle_ref, rows_ref, out_ref):
    scaled = (own_ref[...] + got_ref[...].astype(f32)) * gain_ref[...]
    x = x_ref[:TOK, :].astype(f32)
    inv = norm_scale(x)
    unit = x * inv
    through = inv * (scaled - unit * jnp.mean(scaled * unit, axis=-1, keepdims=True))
    total = d_middle_ref[...]
    for cols in PIECES:
        total += split_dot_nt(through[:, cols], place(rows_ref, D, cols))
    out_ref[...] = total


def cut_kernel(rank_ref, weight_ref, keep_ref, send_ref, held_ref, sem):
    col = lax.broadcasted_iota(jnp.int32, (ROWS, UNIT), 1)
    ranks = [rank_ref[0] ^ flip for flip in (1, 7, 0, 6)]
    starts = [jnp.minimum(rank * FFT, FF - FFT) for rank in ranks]
    copies = []
    for n, start in enumerate(starts):
        for k in range(3):
            first = pl.multiple_of(k * FF + start, 128)
            copies.append(
                pltpu.make_async_copy(
                    weight_ref.at[:, pl.ds(first, FFT)], held_ref.at[n, k], sem.at[n, k]
                )
            )
            copies[-1].start()
    for n, (rank, start) in enumerate(zip(ranks, starts)):
        ref, i = (send_ref, n) if n < 2 else (keep_ref, n - 2)
        for copy in copies[3 * n : 3 * n + 3]:
            copy.wait()
        for j in range(3):
            inside = col >= rank * FFT - start - j * UNIT
            for k, to in enumerate((2 * UNIT * j, 2 * UNIT * j + UNIT, 2 * FFT + UNIT * j)):
                piece = held_ref[n, k, :, j * UNIT : (j + 1) * UNIT]
                ref[i, :, to : to + UNIT] = jnp.where(inside, piece, 0.0).astype(bf16)


def cut(rank, weight):
    scratch = [pltpu.VMEM((4, 3, ROWS, FFT), f32), pltpu.SemaphoreType.DMA((4, 3))]
    outs = [((2, ROWS, 3 * FFT), bf16)] * 2
    return call(cut_kernel, outs, rank, weight, us=2, smem=1, raw=(1,), scratch=scratch)


def near_kernel(flag_ref, own, before, after, across, proj_ref, vec_ref, out_ref):
    for i, ref in enumerate((own, before, after, across)):
        rows = slice(i * 4 * ROWS, (i + 1) * 4 * ROWS)
        proj_ref[rows, :] = ref[:, :COLS]
        vec_ref[rows, :] = ref[:, COLS : COLS + HD]
    rest = slice(COLS + HD, COLS + HD + D)
    first = jnp.where(flag_ref[0] == 1, own[:, rest], across[:, rest])
    second = jnp.where(flag_ref[1] == 1, after[:, rest], before[:, rest])
    out_ref[: 4 * ROWS, :] = first
    out_ref[4 * ROWS :, :] = second


def far_add_kernel(own, low, high, out_ref):
    out_ref[:LINE, :] = (own[:LINE, :].astype(f32) + low[...].astype(f32)).astype(bf16)
    out_ref[LINE:, :] = (own[LINE:, :].astype(f32) + high[...].astype(f32)).astype(bf16)


def far_kernel(proj, proj_got, vec, out, out_got, o0, o1, o2, o3):
    total = proj[...].astype(f32) + proj_got[...].astype(f32)
    rest = out[...].astype(f32) + out_got[...].astype(f32)
    for i, ref in enumerate((o0, o1, o2, o3)):
        rows = slice(i * 4 * ROWS, (i + 1) * 4 * ROWS)
        ref[:, :COLS] = total[rows, :].astype(bf16)
        ref[:, COLS : COLS + HD] = vec[rows, :].astype(bf16)
        half = slice(0, 4 * ROWS) if i in (0, 3) else slice(4 * ROWS, 8 * ROWS)
        ref[:, COLS + HD :] = rest[half, :].astype(bf16)


def order_kernel(place_ref, keep_ref, got_ref, *outs):
    place = place_ref[0]
    for i, ref in enumerate(outs):
        ref[place] = keep_ref[i]
        ref[1 - place] = got_ref[i]


def attn_cut_kernel(side_ref, weight_ref, vec_ref, out_ref):
    side = side_ref[0]
    for start, width, to in ((0, QUERY, 0), (D, HD, QUERY), (D + KV * HD, HD, QUERY + HD)):
        first = pl.multiple_of(start + side * width, 128)
        out_ref[:, to : to + width] = weight_ref[:, pl.ds(first, width)].astype(bf16)
    out_ref[:, COLS : COLS + HD] = vec_ref[...]
    out_ref[:, COLS + HD :] = weight_ref[:, QKV:].astype(bf16)


def adam_update(weight, moment_one, moment_two, gradient, step_rate):
    moment_one = 0.9 * moment_one + 0.1 * gradient
    moment_two = 0.95 * moment_two + 0.05 * gradient * gradient
    first_hat = moment_one / (1.0 - 0.9**STEP)
    second_hat = moment_two / (1.0 - 0.95**STEP)
    updated = weight - step_rate * (first_hat / (jnp.sqrt(second_hat) + 1e-08) + 0.1 * weight)
    return (moment_one, moment_two, updated)


def core_kernel(core_ref, p0, p1, p2, p3, keep_ref, give_ref):
    core = core_ref[0]
    for i, part in enumerate((p0, p1, p2, p3)):
        keep_ref[i] = part[core]
        give_ref[i] = part[1 - core]


def ff_adam_kernel(rank_ref, keep_ref, got_ref, *refs):
    given, results, held, sems = refs[:3], refs[3:6], refs[6:9], refs[9]
    third = lambda ref, k: ref.at[:, pl.ds(k * FF, FF)]
    loads = [[pltpu.make_async_copy(third(a, k), third(b, k), sems.at[i, k]) for i, (a, b) in enumerate(zip(given, held))] for k in range(3)]
    stores = [[pltpu.make_async_copy(third(a, k), third(b, k), sems.at[3 + i, k]) for i, (a, b) in enumerate(zip(held, results))] for k in range(3)]
    for group in loads:
        for copy in group:
            copy.start()

    def put(block, cols):
        weight, one, two = (ref[:, cols] for ref in held)
        one, two, weight = adam_update(weight, one, two, block.astype(f32), 0.02)
        for ref, value in zip(held, (weight, one, two)):
            ref[:, cols] = value

    for k in range(3):
        for copy in loads[k]:
            copy.wait()
        for flip in range(8):
            grad = (keep_ref, got_ref)[flip % 2]
            rank = rank_ref[0] ^ flip
            for j in range(3):
                first = 2 * FFT + UNIT * j if k == 2 else 2 * UNIT * j + UNIT * k

                @pl.when(rank < 7)
                def _():
                    start = pl.multiple_of(k * FF + rank * FFT + j * UNIT, 128)
                    put(grad[flip // 2, :, first : first + UNIT], pl.ds(start, UNIT))

                skip = max(0, 8 * FFT - FF - j * UNIT)
                if skip < UNIT:

                    @pl.when(rank == 7)
                    def _():
                        start = k * FF + FF - FFT + j * UNIT + skip
                        put(grad[flip // 2, :, first + skip : first + UNIT], slice(start, start + UNIT - skip))

        for copy in stores[k]:
            copy.start()
    for group in stores:
        for copy in group:
            copy.wait()


def ff_adam(rank, keep, got, weight, moment_one, moment_two):
    shape = (ROWS, 3 * FF)
    scratch = [pltpu.VMEM(shape, f32)] * 3 + [pltpu.SemaphoreType.DMA((6, 3))]
    weight, one, two = call(
        ff_adam_kernel, [(shape, f32)] * 3, rank, keep, got, weight, moment_one, moment_two,
        smem=1, raw=(3, 4, 5), raw_outs=(0, 1, 2), scratch=scratch,
    )
    return one, two, weight


def attn_adam_kernel(flag_ref, part_ref, other_ref, w_ref, one_ref, two_ref, one_out, two_out, w_out):
    def put(grad, start):
        cols = slice(start, start + grad.shape[1])
        results = adam_update(w_ref[:, cols], one_ref[:, cols], two_ref[:, cols], grad, 0.05)
        for ref, value in zip((one_out, two_out, w_out), results):
            ref[:, cols] = value

    part, other = part_ref[...].astype(f32), other_ref[...].astype(f32)
    own_first = flag_ref[0] == 0
    first = jnp.where(own_first, part[:, :COLS], other[:, :COLS])
    last = jnp.where(own_first, other[:, :COLS], part[:, :COLS])
    put(first[:, :QUERY], 0)
    put(last[:, :QUERY], QUERY)
    put(first[:, QUERY : QUERY + HD], D)
    put(last[:, QUERY : QUERY + HD], D + HD)
    put(first[:, QUERY + HD :], D + KV * HD)
    put(last[:, QUERY + HD :], D + KV * HD + HD)
    put(jnp.where(flag_ref[1] == 1, part[:, COLS + HD :], other[:, COLS + HD :]), QKV)


def shards(
    inputs,
    cotangent,
    attn_weight,
    attn_moment_one,
    attn_moment_two,
    mlp_weight,
    mlp_moment_one,
    mlp_moment_two,
    vectors,
    vector_moment_one,
    vector_moment_two,
):
    half = lax.axis_index("seq")
    yh, core = lax.axis_index("yh"), lax.axis_index("core")
    side = half ^ yh
    rank = half * 4 + yh * 2 + core
    scalar = lambda v: v.astype(jnp.int32).reshape(1)
    x_own, dy_own = inputs[0], cotangent[0]

    vec_own = jnp.pad(vectors.astype(bf16)[None, :], ((0, 15), (0, 48)))
    vec_pair = jnp.concatenate([vec_own[:1], cross_send(vec_own)[:1]])
    vec_block = jnp.concatenate([vec_pair, core_send(jnp.pad(vec_pair, ((0, 14), (0, 0))))[:2]])
    vec_block = jnp.pad(vec_block, ((0, ROWS - 4), (0, 0)))

    mlp_keep, mlp_give = cut(scalar(rank), mlp_weight)
    mlp_got = core_send(mlp_give)
    (attn_block,) = call(
        attn_cut_kernel, [((ROWS, COLS + HD + D), bf16)], scalar(side), attn_weight, vec_block, smem=1, fetch=[1]
    )
    block = ((2, ROWS, 3 * FFT), bf16)
    mlp_near, mlp_far = call(
        order_kernel, [block, block], scalar(core), mlp_keep, mlp_got, smem=1, after=[attn_block]
    )
    mlp_far = cross_send(mlp_far)
    attn_x = join(ring_parts(attn_block, x_send))

    blocks = gathered_blocks(64)
    rows = as_rows((blocks[:, None] * ROWS + jnp.arange(ROWS, dtype=jnp.int32)[None, :]).reshape(D))
    z = lax.axis_index("z")
    inside = z // 2 == side
    first_z = jnp.where(inside, z, z ^ 2)
    j = jnp.arange(HALF, dtype=jnp.int32)
    r, xi, zi, yi, ci = j % 24, (j // 24) % 4, (j // 96) % 2, (j // 192) % 2, j // 384
    feature = ((first_z ^ zi) % 2) * 384 + (yh ^ yi) * 192 + (core ^ ci) * 24 + r
    features = as_rows(feature + (lax.axis_index("x") + near(xi) + 4) % 4 * 48)
    (x_rel,) = call(permute_kernel, [((LEN, D), bf16)], rows, x_own, seq_send(x_own), us=2, store=[0])
    dy_parts = gather_tokens(hold(dy_own, attn_x))

    flags = jnp.stack([inside, inside == (z % 2 == 0)]).astype(jnp.int32)
    proj_z, vec_z, out_z = call(
        near_kernel,
        [((4 * 4 * ROWS, COLS), bf16), ((4 * 4 * ROWS, HD), bf16), ((2 * 4 * ROWS, D), bf16)], flags,
        *ring_parts(attn_x, z_send), smem=1, after=dy_parts[1:4], behind=[x_rel],
    )

    (mlp_block,) = call(
        order_kernel, [((2,) + block[0], bf16)], scalar(yh), mlp_near[None], mlp_far[None], smem=1, after=[proj_z]
    )
    mlp_w = lax.all_gather(mlp_block.reshape(4 * ROWS, 3 * FFT), ("z", "x"), axis=0, tiled=True)
    mlp_w = mlp_w.reshape(4, 4, 2, 48, 3 * FFT)

    proj_y = cross_send(proj_z)
    out_y = cross_send(out_z)
    proj_w = [proj_z, proj_y, core_send(proj_z), core_send(proj_y)]

    place = jnp.arange(64, dtype=jnp.int32)
    by_vector = blocks[(place % 4) % 2 * 16 + (place % 4) // 2 * 32 + place // 4]
    pick = (place[:, None] == by_vector[None, :]).astype(bf16)
    vec_rel = vec_z.reshape(16, ROWS, HD)[:, :4].reshape(64, HD)
    vec_all = dot(pick, vec_rel)[:, :80].reshape(1, 5120)
    gain_rows = jnp.broadcast_to(vec_all[:, :D].astype(bf16), (16, D))
    gain_one = call(permute_kernel, [((16, D), f32)], rows, gain_rows, us=1)[0][:1]
    gain_two = vec_all[:, D : 2 * D]
    bias_all = vec_all[:, 2 * D :]
    own_cols = lambda a, start, width: lax.dynamic_slice_in_dim(a, start + side * width, width, 1)
    bias = jnp.concatenate(
        [
            own_cols(bias_all, 0, QUERY),
            own_cols(bias_all, D, HD),
            own_cols(bias_all, D + KV * HD, HD),
        ],
        axis=1,
    )

    cos, sin = rotary_tables((jnp.arange(LEN) + half * TOK) % LEN)
    normed, low, heads_out, logs = attend(
        scalar(half), x_rel, gain_one, proj_w, bias, cos, sin
    )
    out_y = hold(out_y, behind=[normed])
    out_w = [out_z, out_y, core_send(out_z), core_send(out_y)]
    a_rel, branch_own, branch_give = branch(heads_out, features, out_w)
    middle, second = call(
        second_kernel, [((TOK, D), f32), ((TOK, D), bf16)], x_own, branch_own, seq_send(branch_give), gain_two,
        us=2, store=[0, 1],
    )

    second_parts = gather_tokens(second)
    hidden, d_gate_up, d_second_own, d_second_give = feed_forward(second_parts, dy_parts, mlp_w)
    d_second = call(
        add_kernel, [((TOK, D), f32)] + [((TOK, D), bf16)] * 3, d_second_own, core_send(d_second_give)
    )
    mlp_term = ff_grad(second_parts, dy_parts, hidden, d_gate_up, [d_second[0]])
    mlp_part = lax.psum_scatter(
        mlp_term.reshape(D, 3 * FFT), ("z", "x"), scatter_dimension=0, tiled=True
    )
    d_middle, e, d_gain_two = d_middle_of(
        ring_collect(d_second, y_send), middle, gain_two, dy_own, [mlp_term]
    )
    down_own, down_give = down_terms(hidden, mlp_w, [e])

    e_other = seq_send(e)
    out_term = out_terms(a_rel, e, e_other, [down_give])
    (out_far,) = add_up([out_term[1], core_send(out_term[3])], fetch=True)
    (out_near,) = add_up([out_term[0], core_send(out_term[2])], fetch=True)
    out_got = cross_send(out_far)
    *proj_term, d_proj, d_bias_own = attend_back(
        scalar(half), e, e_other, out_w, features, low, logs, cos, sin, normed, [out_far]
    )
    dh_own, dh_give, d_gain_one = d_normed_of(d_proj, x_rel, proj_w)

    (proj_far,) = call(
        far_add_kernel, [((PIECE, COLS), bf16)], proj_term[1], core_send(proj_term[3]), core_send(proj_term[4]),
        fetch=range(3), after=[out_got],
    )
    (proj_near,) = add_up([proj_term[0], core_send(proj_term[2])], fetch=True)
    bias_zero = jnp.zeros((1, QKV), f32)
    put = lambda a, v, start, width: lax.dynamic_update_slice_in_dim(a, v, start + side * width, 1)
    d_bias = put(bias_zero, d_bias_own[:, :QUERY], 0, QUERY)
    d_bias = put(d_bias, d_bias_own[:, QUERY : QUERY + HD], D, HD)
    d_bias = put(d_bias, d_bias_own[:, QUERY + HD :], D + KV * HD, HD)
    d_gain_rows = jnp.broadcast_to(d_gain_one, (8, D))
    d_gain_one = call(unpermute_kernel, [((8, D), f32)], rows, d_gain_rows, us=2)[0][:1]
    vec_term = jnp.concatenate([d_gain_one, d_gain_two, d_bias], axis=1)
    vec_term = jnp.pad(vec_term.reshape(64, 80), ((0, 0), (0, 48))).astype(bf16)
    pick_rel = (place[:, None] == blocks[None, :]).astype(bf16)
    vec_term = dot_tn(pick_rel, vec_term)
    vec_term = pair_reduce(vec_term, core_send)
    vec_term = pair_reduce(vec_term, cross_send)
    vec_term = jnp.pad(vec_term[:, None, :], ((0, 0), (0, ROWS - 1), (0, 0))).reshape(PIECE, HD)
    down = call(
        add_kernel, [((TOK, D), f32)] + [((TOK, D), bf16)] * 3, down_own, core_send(hold(down_give, proj_far))
    )
    dh_got = seq_send(dh_give)
    attn_parts = call(
        far_kernel, [((4 * ROWS, COLS + HD + D), bf16)] * 4,
        proj_near, cross_send(proj_far), vec_term, out_near, out_got, after=[down[1], dh_got],
    )
    attn_near = ring_collect(attn_parts, z_send)
    down = ring_collect(down, y_send)
    (input_grad,) = call(
        input_grad_kernel, [((TOK, D), f32)], dh_own, dh_got, x_rel, gain_one, d_middle, rows,
        us=5, fetch=[0, 2, 4], store=[0], after=[attn_parts[0]],
    )
    attn_parts = add_up(attn_near, pieces=4, after=down[1:], behind=[input_grad])

    by_y = hold(mlp_part, behind=[input_grad]).reshape(2, 2, ROWS, 3 * FFT)
    near_rows = lax.dynamic_index_in_dim(by_y, yh, 0, keepdims=False)
    far_rows = lax.dynamic_index_in_dim(by_y, 1 - yh, 0, keepdims=False)
    block = ((4, ROWS, 3 * FFT), bf16)
    grads_keep, grads_give = call(
        core_kernel, [block, block], scalar(core),
        near_rows, ring_send(far_rows, "yh", 1), seq_send(near_rows), cross_send(far_rows), smem=1,
    )
    mlp_one, mlp_two, mlp_new = ff_adam(
        scalar(rank), grads_keep, core_send(grads_give), mlp_weight, mlp_moment_one, mlp_moment_two
    )
    (attn_part,) = add_up(ring_collect(attn_parts, x_send))
    attn_other = hold(seq_send(attn_part), behind=[mlp_one])
    vec_cols = slice(COLS, COLS + 80)
    vec_grad = attn_part[0, vec_cols].astype(f32) + attn_other[0, vec_cols].astype(f32)

    attn_one, attn_two, attn_new = call(
        attn_adam_kernel,
        [((ROWS, QKV + D), f32)] * 3,
        jnp.stack([side, inside.astype(side.dtype)]).astype(jnp.int32),
        attn_part,
        attn_other,
        attn_weight,
        attn_moment_one,
        attn_moment_two,
        smem=1,
    )

    total = down[0] + down[1].astype(f32) + down[2].astype(f32) + down[3].astype(f32)
    output = (middle + total).astype(bf16)[None]
    vec_one, vec_two, vec_new = adam_update(
        vectors, vector_moment_one, vector_moment_two, vec_grad, 0.5
    )
    return (
        output,
        input_grad[None],
        attn_one,
        attn_two,
        attn_new,
        mlp_one,
        mlp_two,
        mlp_new,
        vec_one,
        vec_two,
        vec_new,
    )


def solution(mesh):
    grid = Mesh(mesh.devices.reshape(2, 4, 2, 4, 2), ("seq",) + FSDP)
    tokens, rows, vector = P(FSDP, "seq", None), P(FSDP, None), P(FSDP)
    return jax.shard_map(
        shards,
        mesh=grid,
        in_specs=(tokens, tokens) + (rows,) * 6 + (vector,) * 3,
        out_specs=(tokens, tokens) + (rows,) * 6 + (vector,) * 3,
        check_vma=False,
    )
```

```python
import math

import jax
import jax.numpy as jnp
from jax import lax
from jax.experimental import pallas as pl
from jax.experimental.pallas import tpu as pltpu
from jax.sharding import Mesh
from jax.sharding import PartitionSpec as P

D = 1536
H = 12
KV = 2
HD = 128
FF = 8960
STEP = 10
QKV = 2048
ROWS = 24
TOK = 128
LEN = 256
HALF = D // 2
GROUP = H // KV
QUERY = GROUP * HD
COLS = QUERY + 2 * HD
FFT = 1152
UNIT = FFT // 3
PIECE = D // 4
LINE = HALF // 4
MIB = 1024 * 1024

norm_eps = 1e-06
rope_base = 1000000.0
f32 = jnp.float32
bf16 = jnp.bfloat16
contract_rows = (((0,), (0,)), ((), ()))
contract_cols = (((1,), (1,)), ((), ()))
score_scale = HD ** (-0.5)
FSDP = ("z", "yh", "x", "core")
SIZES = {"seq": 2, "z": 4, "yh": 2, "x": 4, "core": 2}


def dot(a, b):
    return jnp.dot(a, b, preferred_element_type=f32)


def dot_tn(a, b):
    return lax.dot_general(a, b, contract_rows, preferred_element_type=f32)


def dot_nt(a, b):
    return lax.dot_general(a, b, contract_cols, preferred_element_type=f32)


def split_dot_nt(a, b):
    high = a.astype(bf16)
    low = (a - high.astype(f32)).astype(bf16)
    return dot_nt(high, b) + dot_nt(low, b)


def ring_send(values, axis, shift):
    size = SIZES[axis]
    return lax.ppermute(values, axis, [(i, (i + shift) % size) for i in range(size)])


def x_send(values, shift):
    return ring_send(values, "x", shift)


def z_send(values, shift):
    return ring_send(values, "z", shift)


def y_send(values, shift):
    place = lambda y: (y % 2) * 2 + y // 2
    return lax.ppermute(
        values, ("seq", "yh"), [(place(i), place((i + shift) % 4)) for i in range(4)]
    )


def cross_send(values):
    return lax.ppermute(values, ("seq", "yh"), [(i, 3 - i) for i in range(4)])


def core_send(values):
    return ring_send(values, "core", 1)


def seq_send(values):
    return ring_send(values, "seq", 1)


def ring_parts(values, send):
    return [values, send(values, 1), send(values, -1), send(values, 2)]


def pair_reduce(values, send):
    rows = values.shape[0] // 2
    return values[:rows] + send(values[rows:].astype(bf16)).astype(f32)


def ring_collect(parts, send):
    return [parts[0], send(parts[1], -1), send(parts[2], 1), send(parts[3], 2)]


def gather_tokens(values):
    parts = ring_parts(values, y_send)
    return parts + [core_send(p) for p in parts]


def near(index):
    return jnp.where(index == 1, -1, jnp.where(index == 0, 0, index - 1))


def gathered_blocks(count):
    j = jnp.arange(count, dtype=jnp.int32)
    xi, zi, yi, ci = j % 4, (j // 4) % 4, (j // 16) % 2, j // 32
    z = (lax.axis_index("z") + near(zi) + 4) % 4
    x = (lax.axis_index("x") + near(xi) + 4) % 4
    yh = (lax.axis_index("yh") + yi) % 2
    core = (lax.axis_index("core") + ci) % 2
    return z * 16 + yh * 8 + x * 2 + core


def call(
    kernel, outs, *args, us=1, smem=0, fetch=(), raw=(), store=(), raw_outs=(), scratch=(), room=6, after=(), behind=(), late=()
):
    vmem, hbm = pl.BlockSpec(memory_space=pltpu.VMEM), pl.BlockSpec(memory_space=pltpu.HBM)
    fetch = [g if isinstance(g, tuple) else (g,) for g in fetch]
    far = set(raw) | {i for g in fetch for i in g}
    specs = [
        pl.BlockSpec(memory_space=pltpu.SMEM) if i < smem else hbm if i in far else vmem
        for i in range(len(args))
    ] + [pl.BlockSpec(memory_space=pl.ANY)] * len(after) + [hbm] * len(behind)
    after = list(after) + [in_hbm(a) for a in behind]
    buffers = []
    for g in fetch:
        rows = sum(args[i].shape[0] for i in g)
        buffers.append(((rows,) + args[g[0]].shape[1:], args[g[0]].dtype))
    buffers += [outs[i] for i in store]
    held = [pltpu.VMEM(shape, kind) for shape, kind in buffers]
    moves = max(1, sum(len(g) for g in fetch) + len(store))
    n_in, n_out, n_own = len(args), len(outs), len(scratch)

    def body(*refs):
        ins, refs = list(refs[:n_in]), refs[n_in + len(after) :]
        out_refs, own = list(refs[:n_out]), refs[n_out : n_out + n_own]
        held_refs, sems = refs[n_out + n_own : -1], refs[-1]
        copies, last, k = [], [], 0
        for n, (g, ref) in enumerate(zip(fetch, held_refs)):
            row = 0
            for i in g:
                rows = args[i].shape[0]
                copy = pltpu.make_async_copy(ins[i], ref.at[pl.ds(row, rows)], sems.at[k])
                (last if n in late else copies).append(copy)
                row, k = row + rows, k + 1
            ins[g[0]] = ref
        for copy in copies + last:
            copy.start()
        for copy in copies:
            copy.wait()

        def wait_late():
            for copy in last:
                copy.wait()

        drop = {i for g in fetch for i in g[1:]}
        ins = [ref for i, ref in enumerate(ins) if i not in drop]
        leaving = []
        for i, ref in zip(store, held_refs[len(fetch) :]):
            leaving.append(pltpu.make_async_copy(ref, out_refs[i], sems.at[k]))
            out_refs[i] = ref
            k += 1
        kernel(*([wait_late] if late else []), *ins, *out_refs, *own)
        for copy in leaving:
            copy.start()
        for copy in leaving:
            copy.wait()

    size = lambda shape, kind: math.prod(shape) * jnp.dtype(kind).itemsize
    used = sum(size(*b) for b in buffers)
    used += sum(size(b.shape, b.dtype) for b in scratch if hasattr(b, "shape") and b.memory_space == pltpu.VMEM)
    args = [
        in_hbm(a) if i in far else a
        for i, a in enumerate(args)
    ]
    leave = lambda i: pltpu.HBM if i in raw_outs or i in store else jax.ShapeDtypeStruct
    return pl.pallas_call(
        body,
        out_shape=tuple(leave(i)(shape, kind) for i, (shape, kind) in enumerate(outs)),
        in_specs=specs,
        out_specs=tuple(hbm if i in raw_outs or i in store else vmem for i in range(n_out)),
        scratch_shapes=list(scratch) + held + [pltpu.SemaphoreType.DMA((moves,))],
        cost_estimate=pl.CostEstimate(flops=us * 10**7, bytes_accessed=us * 10**4, transcendentals=0),
        compiler_params=pltpu.CompilerParams(vmem_limit_bytes=used + room * MIB),
    )(*args, *after)


def hold_kernel(*refs):
    pass


def in_hbm(values):
    return pltpu.with_memory_space_constraint(values, pltpu.HBM)


def hold(values, *after, behind=()):
    anywhere, hbm = pl.BlockSpec(memory_space=pl.ANY), pl.BlockSpec(memory_space=pltpu.HBM)
    return pl.pallas_call(
        hold_kernel,
        out_shape=jax.ShapeDtypeStruct(values.shape, values.dtype),
        in_specs=[anywhere] * (1 + len(after)) + [hbm] * len(behind),
        out_specs=anywhere,
        input_output_aliases={0: 0},
    )(values, *after, *(in_hbm(a) for a in behind))


def join_kernel(*refs):
    out_ref, row = refs[-1], 0
    for ref in refs[:-1]:
        out_ref[row : row + ref.shape[0], :] = ref[...]
        row += ref.shape[0]


def join(parts):
    rows = sum(p.shape[0] for p in parts)
    return call(join_kernel, [((rows, parts[0].shape[1]), bf16)], *parts)[0]


def sum_kernel(count, given, outs):
    groups = []
    for i in range(0, len(given), count):
        total = given[i][...].astype(f32)
        for ref in given[i + 1 : i + count]:
            total = total + ref[...].astype(f32)
        groups.append(total)
    rows, col = outs[0].shape[0], 0
    for total in groups:
        for i, ref in enumerate(outs):
            part = total[i * rows : (i + 1) * rows, :]
            ref[:, col : col + total.shape[1]] = part.astype(ref.dtype)
        col += total.shape[1]


def add_up(parts, pieces=1, count=None, after=(), behind=(), fetch=False):
    count = count or len(parts)
    cols = sum(p.shape[1] for p in parts[::count])
    outs = [((parts[0].shape[0] // pieces, cols), bf16)] * pieces
    kernel = lambda *refs: sum_kernel(count, refs[: len(parts)], refs[len(parts) :])
    fetch = range(len(parts)) if fetch else ()
    return call(kernel, outs, *parts, after=after, behind=behind, fetch=fetch)


def place(rows_ref, size, cols):
    row = lax.broadcasted_iota(jnp.int32, (size, cols.stop - cols.start), 0)
    return jnp.where(row == rows_ref[:1, cols], 1.0, 0.0).astype(bf16)


PIECES = [slice(i * PIECE, (i + 1) * PIECE) for i in range(4)]


def permute_kernel(rows_ref, *refs):
    out_ref = refs[-1]
    for cols in PIECES:
        here, row = place(rows_ref, D, cols), 0
        for ref in refs[:-1]:
            out_ref[row : row + ref.shape[0], cols] = dot(ref[...], here).astype(out_ref.dtype)
            row += ref.shape[0]


def unpermute_kernel(rows_ref, values_ref, out_ref):
    out = jnp.zeros(out_ref.shape, f32)
    for cols in PIECES:
        out += split_dot_nt(values_ref[:, cols], place(rows_ref, D, cols))
    out_ref[...] = out


def as_rows(rows):
    return jnp.broadcast_to(rows[None, :].astype(jnp.int32), (8, rows.shape[0]))


def rotary_tables(positions):
    half_dim = HD // 2
    freqs = rope_base ** (-jnp.arange(half_dim, dtype=f32) * 2.0 / HD)
    angles = positions.astype(f32)[:, None] * freqs[None, :]
    cos, sin = jnp.cos(angles), jnp.sin(angles)
    return jnp.concatenate([cos, cos], axis=1), jnp.concatenate([-sin, sin], axis=1)


def causal_mask(half):
    row = (lax.broadcasted_iota(jnp.int32, (LEN, LEN), 0) + half * TOK) % LEN
    col = (lax.broadcasted_iota(jnp.int32, (LEN, LEN), 1) + half * TOK) % LEN
    return row >= col


def norm_scale(values):
    return lax.rsqrt(jnp.mean(values * values, axis=-1, keepdims=True) + norm_eps)


def attend_kernel(
    wait_weights, half_ref, x_ref, gain_ref, w_ref, bias_ref, cos_ref, sin_ref,
    normed_ref, low_ref, out_ref, log_ref, qkv_ref,
):
    x = x_ref[...].astype(f32)
    normed_ref[...] = (x * norm_scale(x) * gain_ref[...]).astype(bf16)
    wait_weights()
    qkv_ref[...] = dot(normed_ref[...], w_ref[...]) + bias_ref[...]
    cos, sin = cos_ref[...], sin_ref[...]
    mask = causal_mask(half_ref[0])

    def rotated(start):
        z = qkv_ref[:, start : start + HD]
        return (z * cos + pltpu.roll(z, HD // 2, 1) * sin).astype(bf16)

    key = rotated(QUERY)
    low_ref[:, QUERY : QUERY + HD] = key
    value = qkv_ref[:, QUERY + HD :].astype(bf16)
    low_ref[:, QUERY + HD :] = value
    for h in range(GROUP):
        query = rotated(h * HD)
        low_ref[:, h * HD : (h + 1) * HD] = query
        scores = jnp.where(mask, dot_nt(query, key) * score_scale, -1e30)
        top = jnp.max(scores, axis=-1, keepdims=True)
        total = top + jnp.log(jnp.sum(jnp.exp(scores - top), axis=-1, keepdims=True))
        log_ref[h] = jnp.broadcast_to(total, (LEN, HD))
        probs = jnp.exp(scores - total).astype(bf16)
        out_ref[:, h * HD : (h + 1) * HD] = dot(probs, value).astype(bf16)


def attend(half, x_rel, gain, proj, bias, cos, sin):
    outs = [((LEN, D), bf16), ((LEN, COLS), bf16), ((LEN, QUERY), bf16), ((GROUP, LEN, HD), f32)]
    return call(
        attend_kernel, outs, half, x_rel, gain, *proj, bias, cos, sin,
        us=6, smem=1, fetch=[1, tuple(range(3, 11))], late=[1], store=[0, 1, 3], scratch=[pltpu.VMEM((LEN, COLS), f32)],
    )


def branch_kernel(a_ref, rows_ref, w_ref, rel_ref, own_ref, give_ref):
    rel_ref[...] = dot(a_ref[...], place(rows_ref, HALF, slice(0, HALF))).astype(bf16)
    own_ref[...] = dot(rel_ref[:TOK, :], w_ref[...])
    give_ref[...] = dot(rel_ref[TOK:, :], w_ref[...]).astype(bf16)


def branch(a, rows, out_w):
    outs = [((LEN, HALF), bf16), ((TOK, D), f32), ((TOK, D), bf16)]
    return call(branch_kernel, outs, a, rows, *out_w, us=4, fetch=[(2, 3, 4, 5)], store=[0])


def second_kernel(x_ref, own_ref, got_ref, gain_ref, middle_ref, second_ref):
    middle = x_ref[...].astype(f32) + own_ref[...] + got_ref[...].astype(f32)
    middle_ref[...] = middle
    second_ref[...] = (middle * norm_scale(middle) * gain_ref[...]).astype(bf16)


def load_tokens(parts, whole, sems):
    copies = []
    for i, part in enumerate(parts):
        copies.append(pltpu.make_async_copy(part, whole.at[pl.ds(i * TOK, TOK), :], sems.at[i]))
        copies[-1].start()
    return copies


def ff_kernel(*refs):
    h_parts, dy_parts, refs = refs[:8], refs[8:16], refs[16:]
    w_ref, hid_out, dgu_out, own_ref, give_ref, h_all, dy_all, w, hid, dgu, h_sem, dy_sem, w_sem, out_sem = refs
    tokens = load_tokens(h_parts, h_all, h_sem) + load_tokens(dy_parts, dy_all, dy_sem)
    loads = []
    for j in range(3):
        for k, (start, width) in enumerate(((2 * UNIT * j, 2 * UNIT), (2 * FFT + UNIT * j, UNIT))):
            for y in range(2):
                copy = pltpu.make_async_copy(
                    w_ref.at[:, :, y, :, pl.ds(start, width)],
                    w.at[:, y, :, :, pl.ds(start, width)],
                    w_sem.at[j * 4 + k * 2 + y],
                )
                copy.start()
                loads.append(copy)
    for copy in tokens:
        copy.wait()
    tile = 512
    for j in range(3):
        for copy in loads[4 * j : 4 * j + 4]:
            copy.wait()

        @pl.loop(0, 8 * TOK // tile)
        def _(m):
            rows = pl.ds(pl.multiple_of(m * tile, tile), tile)
            pair = slice(2 * UNIT * j, 2 * UNIT * (j + 1))
            last = slice(2 * FFT + UNIT * j, 2 * FFT + UNIT * (j + 1))
            gate_up = dot(h_all[rows, :], w[:, :, :, :, pair].reshape(D, 2 * UNIT))
            d_hidden = dot(dy_all[rows, :], w[:, :, :, :, last].reshape(D, UNIT))
            gate, up = gate_up[:, :UNIT], gate_up[:, UNIT:]
            sigmoid_gate = jax.nn.sigmoid(gate)
            act = gate * sigmoid_gate
            hid[rows, UNIT * j : UNIT * (j + 1)] = (act * up).astype(bf16)
            d_gate = d_hidden * up * (sigmoid_gate * (1.0 + gate * (1.0 - sigmoid_gate)))
            dgu[rows, 2 * UNIT * j : 2 * UNIT * j + UNIT] = d_gate.astype(bf16)
            dgu[rows, 2 * UNIT * j + UNIT : 2 * UNIT * (j + 1)] = (d_hidden * act).astype(bf16)

    outs = [
        pltpu.make_async_copy(hid, hid_out, out_sem.at[0]),
        pltpu.make_async_copy(dgu, dgu_out, out_sem.at[1]),
    ]
    for copy in outs:
        copy.start()
    for z in range(2):
        cols = slice(2 * z * PIECE, 2 * (z + 1) * PIECE)
        wz = w[2 * z : 2 * (z + 1), :, :, :, : 2 * FFT].reshape(2 * PIECE, 2 * FFT)
        for i, ref in enumerate((own_ref, give_ref)):
            rows = slice(i * 4 * TOK, (i + 1) * 4 * TOK)
            ref[:, cols] = dot_nt(dgu[rows, :], wz).astype(ref.dtype)
    for copy in outs:
        copy.wait()


def feed_forward(h_parts, dy_parts, w):
    tokens = 8 * TOK
    outs = [
        ((tokens, FFT), bf16),
        ((tokens, 2 * FFT), bf16),
        ((4 * TOK, D), f32),
        ((4 * TOK, D), bf16),
    ]
    scratch = [
        pltpu.VMEM((tokens, D), bf16),
        pltpu.VMEM((tokens, D), bf16),
        pltpu.VMEM((4, 2, 4, 48, 3 * FFT), bf16),
        pltpu.VMEM((tokens, FFT), bf16),
        pltpu.VMEM((tokens, 2 * FFT), bf16),
        pltpu.SemaphoreType.DMA((8,)),
        pltpu.SemaphoreType.DMA((8,)),
        pltpu.SemaphoreType.DMA((12,)),
        pltpu.SemaphoreType.DMA((2,)),
    ]
    return call(
        ff_kernel, outs, *h_parts, *dy_parts, w, us=25, raw=range(17), raw_outs=(0, 1), scratch=scratch
    )


def ff_grad_kernel(*refs):
    h_parts, dy_parts, refs = refs[:8], refs[8:16], refs[16:]
    hid_ref, dgu_ref, term_ref, h_all, dy_all, hid, dgu, term, h_sem, dy_sem, in_sem, t_sem = refs
    last = load_tokens(dy_parts, dy_all, dy_sem) + [pltpu.make_async_copy(hid_ref, hid, in_sem.at[1])]
    last[-1].start()
    first = load_tokens(h_parts, h_all, h_sem) + [pltpu.make_async_copy(dgu_ref, dgu, in_sem.at[0])]
    first[-1].start()
    for copy in last:
        copy.wait()
    outs = []
    for z in range(4):
        cols = slice(z * PIECE, (z + 1) * PIECE)
        for start in (2 * FFT, 2 * FFT + 2 * UNIT, 0, 2 * UNIT, 4 * UNIT):
            width = min(2 * UNIT, 3 * FFT - start)
            if start >= 2 * FFT:
                out = dot_tn(dy_all[:, cols], hid[:, start - 2 * FFT : start - 2 * FFT + width])
            else:
                if z == 0 and start == 0:
                    for copy in first:
                        copy.wait()
                out = dot_tn(h_all[:, cols], dgu[:, start : start + width])
            term[z, :, :, :, start : start + width] = out.astype(bf16).reshape(2, 4, 48, width)
        for y in range(2):
            copy = pltpu.make_async_copy(term.at[z, y], term_ref.at[z, :, y], t_sem.at[z, y])
            copy.start()
            outs.append(copy)
    for copy in outs:
        copy.wait()


def ff_grad(h_parts, dy_parts, hid, dgu, after):
    tokens = 8 * TOK
    scratch = [
        pltpu.VMEM((tokens, D), bf16),
        pltpu.VMEM((tokens, D), bf16),
        pltpu.VMEM((tokens, FFT), bf16),
        pltpu.VMEM((tokens, 2 * FFT), bf16),
        pltpu.VMEM((4, 2, 4, 48, 3 * FFT), bf16),
        pltpu.SemaphoreType.DMA((8,)),
        pltpu.SemaphoreType.DMA((8,)),
        pltpu.SemaphoreType.DMA((2,)),
        pltpu.SemaphoreType.DMA((4, 2)),
    ]
    return call(
        ff_grad_kernel, [((4, 4, 2, 48, 3 * FFT), bf16)], *h_parts, *dy_parts, hid, dgu,
        us=17, raw=range(18), raw_outs=(0,), scratch=scratch, after=after,
    )[0]


def down_kernel(hid_ref, w_ref, own_ref, give_ref, w, w_sem):
    loads = []
    for z in range(4):
        for y in range(2):
            load = pltpu.make_async_copy(
                w_ref.at[z, :, y, :, pl.ds(2 * FFT, FFT)], w.at[z, y], w_sem.at[z, y]
            )
            load.start()
            loads.append(load)
    for z in range(2):
        for load in loads[4 * z : 4 * z + 4]:
            load.wait()
        cols = slice(2 * z * PIECE, 2 * (z + 1) * PIECE)
        wz = w[2 * z : 2 * (z + 1)].reshape(2 * PIECE, FFT)
        for i, ref in enumerate((own_ref, give_ref)):
            rows = slice(i * 4 * TOK, (i + 1) * 4 * TOK)
            ref[:, cols] = dot_nt(hid_ref[rows, :], wz).astype(ref.dtype)


def down_terms(hidden, w, after):
    outs = [((4 * TOK, D), f32), ((4 * TOK, D), bf16)]
    scratch = [pltpu.VMEM((4, 2, 4, 48, FFT), bf16), pltpu.SemaphoreType.DMA((4, 2))]
    return call(
        down_kernel, outs, hidden, w, us=8, fetch=[0], raw=(1,), store=[0], scratch=scratch, after=after
    )


def add_kernel(own_ref, got_ref, keep_ref, g1_ref, g2_ref, g3_ref):
    for i, ref in enumerate((keep_ref, g1_ref, g2_ref, g3_ref)):
        rows = slice(i * TOK, (i + 1) * TOK)
        ref[...] = (own_ref[rows, :] + got_ref[rows, :].astype(f32)).astype(ref.dtype)


def d_middle_kernel(p0, p1, p2, p3, middle_ref, gain_ref, dy_ref, d_middle_ref, e_ref, d_gain_ref):
    d_second = p0[...] + p1[...].astype(f32) + p2[...].astype(f32) + p3[...].astype(f32)
    middle = middle_ref[...]
    inv = norm_scale(middle)
    unit = middle * inv
    scaled = d_second * gain_ref[...]
    d_gain_ref[...] = jnp.sum(d_second * unit, axis=0, keepdims=True)
    d_middle = dy_ref[...].astype(f32) + inv * (
        scaled - unit * jnp.mean(scaled * unit, axis=-1, keepdims=True)
    )
    d_middle_ref[...] = d_middle
    e_ref[...] = d_middle.astype(bf16)


def d_middle_of(parts, middle, gain, dy, behind):
    outs = [((TOK, D), f32), ((TOK, D), bf16), ((1, D), f32)]
    return call(
        d_middle_kernel, outs, *parts, middle, gain, dy, us=20000, fetch=[4, 6], store=[0], behind=behind
    )


def out_term_kernel(a_ref, e0_ref, e1_ref, t0, t1, t2, t3):
    total = dot_tn(a_ref[:TOK, :], e0_ref[...]) + dot_tn(a_ref[TOK:, :], e1_ref[...])
    for i, ref in enumerate((t0, t1, t2, t3)):
        ref[...] = total[i * LINE : (i + 1) * LINE, :].astype(bf16)


def out_terms(a_rel, e, e_other, after):
    outs = [((LINE, D), bf16)] * 4
    return call(out_term_kernel, outs, a_rel, e, e_other, us=2, fetch=[0], store=range(4), room=10, after=after)


def attend_back_kernel(
    wait_normed, half_ref, e0_ref, e1_ref, out_w_ref, rows_ref, low_ref, log_ref, cos_ref, sin_ref, normed_ref,
    t0, t1, t2, t3, t4, out_ref, sum_ref, grad_ref,
):
    cos, sin = cos_ref[...], sin_ref[...]
    mask = causal_mask(half_ref[0])
    here = place(rows_ref, HALF, slice(0, HALF))
    for i, e_ref in enumerate((e0_ref, e1_ref)):
        rel = dot_nt(e_ref[...], out_w_ref[...]).astype(bf16)
        grad_ref[i * TOK : (i + 1) * TOK, :] = dot_nt(rel, here).astype(bf16)
    key = low_ref[:, QUERY : QUERY + HD]
    value = low_ref[:, QUERY + HD :]

    def unrotated(z):
        return (z * cos - pltpu.roll(z, HD // 2, 1) * sin).astype(bf16)

    def put(start, block):
        out_ref[:, start : start + HD] = block
        sum_ref[:, start : start + HD] = jnp.sum(block.astype(f32), axis=0, keepdims=True)

    d_key = jnp.zeros((LEN, HD), f32)
    d_value = jnp.zeros((LEN, HD), f32)
    for h in range(GROUP):
        query = low_ref[:, h * HD : (h + 1) * HD]
        grad = grad_ref[:, h * HD : (h + 1) * HD]
        scores = jnp.where(mask, dot_nt(query, key) * score_scale, -1e30)
        total = log_ref[h]
        probs = jnp.exp(scores - jnp.concatenate([total, total], axis=1))
        d_probs = dot_nt(grad, value)
        delta = jnp.sum(probs * d_probs, axis=-1, keepdims=True)
        d_scores = (probs * (d_probs - delta)).astype(bf16)
        put(h * HD, unrotated(dot(d_scores, key) * score_scale))
        d_key += dot_tn(d_scores, query)
        d_value += dot_tn(probs.astype(bf16), grad)
    put(QUERY, unrotated(d_key * score_scale))
    put(QUERY + HD, d_value.astype(bf16))
    wait_normed()
    for i, ref in enumerate((t0, t1, t2)):
        ref[...] = dot_tn(normed_ref[:, i * PIECE : (i + 1) * PIECE], out_ref[...]).astype(bf16)
    last = dot_tn(normed_ref[:, 3 * PIECE :], out_ref[...]).astype(bf16)
    t3[...] = last[:LINE, :]
    t4[...] = last[LINE:, :]


def attend_back(half, e, e_other, out_w, rows, low, logs, cos, sin, normed, after):
    outs = [((PIECE, COLS), bf16)] * 3 + [((LINE, COLS), bf16)] * 2
    outs += [((LEN, COLS), bf16), ((1, COLS), f32)]
    return call(
        attend_back_kernel, outs, half, e, e_other, *out_w, rows, low, logs, cos, sin, normed,
        us=9, smem=1, fetch=[(3, 4, 5, 6), 8, 9, 12], late=[3], store=range(6),
        scratch=[pltpu.VMEM((LEN, QUERY), bf16)],
        room=8, after=after,
    )


def d_normed_kernel(d_ref, x_ref, w_ref, own_ref, give_ref, d_gain_ref):
    x = x_ref[...].astype(f32)
    d_normed = dot_nt(d_ref[...], w_ref[...])
    own_ref[...] = d_normed[:TOK, :]
    give_ref[...] = d_normed[TOK:, :].astype(bf16)
    d_gain_ref[...] = jnp.sum(d_normed * (x * norm_scale(x)), axis=0, keepdims=True)


def d_normed_of(d_proj, x_rel, proj):
    outs = [((TOK, D), f32), ((TOK, D), bf16), ((1, D), f32)]
    return call(
        d_normed_kernel, outs, d_proj, x_rel, *proj, us=3, fetch=[0, 1, tuple(range(2, 10))], store=[0, 1], room=8
    )


def input_grad_kernel(own_ref, got_ref, x_ref, gain_ref, d_middle_ref, rows_ref, out_ref):
    scaled = (own_ref[...] + got_ref[...].astype(f32)) * gain_ref[...]
    x = x_ref[:TOK, :].astype(f32)
    inv = norm_scale(x)
    unit = x * inv
    through = inv * (scaled - unit * jnp.mean(scaled * unit, axis=-1, keepdims=True))
    total = d_middle_ref[...]
    for cols in PIECES:
        total += split_dot_nt(through[:, cols], place(rows_ref, D, cols))
    out_ref[...] = total


def cut_kernel(rank_ref, weight_ref, keep_ref, send_ref, held_ref, sem):
    col = lax.broadcasted_iota(jnp.int32, (ROWS, UNIT), 1)
    ranks = [rank_ref[0] ^ flip for flip in (1, 7, 0, 6)]
    starts = [jnp.minimum(rank * FFT, FF - FFT) for rank in ranks]
    copies = []
    for n, start in enumerate(starts):
        for k in range(3):
            first = pl.multiple_of(k * FF + start, 128)
            copies.append(
                pltpu.make_async_copy(
                    weight_ref.at[:, pl.ds(first, FFT)], held_ref.at[n, k], sem.at[n, k]
                )
            )
            copies[-1].start()
    for n, (rank, start) in enumerate(zip(ranks, starts)):
        ref, i = (send_ref, n) if n < 2 else (keep_ref, n - 2)
        for copy in copies[3 * n : 3 * n + 3]:
            copy.wait()
        for j in range(3):
            inside = col >= rank * FFT - start - j * UNIT
            for k, to in enumerate((2 * UNIT * j, 2 * UNIT * j + UNIT, 2 * FFT + UNIT * j)):
                piece = held_ref[n, k, :, j * UNIT : (j + 1) * UNIT]
                ref[i, :, to : to + UNIT] = jnp.where(inside, piece, 0.0).astype(bf16)


def cut(rank, weight):
    scratch = [pltpu.VMEM((4, 3, ROWS, FFT), f32), pltpu.SemaphoreType.DMA((4, 3))]
    outs = [((2, ROWS, 3 * FFT), bf16)] * 2
    return call(cut_kernel, outs, rank, weight, us=2, smem=1, raw=(1,), scratch=scratch)


def near_kernel(flag_ref, own, before, after, across, low_ref, high_ref, vec_ref, out_ref):
    for i, ref in enumerate((own, before, after, across)):
        rows = slice(i * 4 * ROWS, (i + 1) * 4 * ROWS)
        half = slice(i % 2 * 4 * ROWS, (i % 2 + 1) * 4 * ROWS)
        (low_ref if i < 2 else high_ref)[half, :] = ref[:, :COLS]
        vec_ref[rows, :] = ref[:, COLS : COLS + HD]
    rest = slice(COLS + HD, COLS + HD + D)
    first = jnp.where(flag_ref[0] == 1, own[:, rest], across[:, rest])
    second = jnp.where(flag_ref[1] == 1, after[:, rest], before[:, rest])
    out_ref[: 4 * ROWS, :] = first
    out_ref[4 * ROWS :, :] = second


def far_add_kernel(own, low, high, out_ref):
    out_ref[:LINE, :] = (own[:LINE, :].astype(f32) + low[...].astype(f32)).astype(bf16)
    out_ref[LINE:, :] = (own[LINE:, :].astype(f32) + high[...].astype(f32)).astype(bf16)


def far_kernel(proj, proj_got, vec, out, out_got, o0, o1, o2, o3):
    total = proj[...].astype(f32) + proj_got[...].astype(f32)
    rest = out[...].astype(f32) + out_got[...].astype(f32)
    for i, ref in enumerate((o0, o1, o2, o3)):
        rows = slice(i * 4 * ROWS, (i + 1) * 4 * ROWS)
        ref[:, :COLS] = total[rows, :].astype(bf16)
        ref[:, COLS : COLS + HD] = vec[rows, :].astype(bf16)
        half = slice(0, 4 * ROWS) if i in (0, 3) else slice(4 * ROWS, 8 * ROWS)
        ref[:, COLS + HD :] = rest[half, :].astype(bf16)


def order_kernel(place_ref, keep_ref, got_ref, *outs):
    place = place_ref[0]
    for i, ref in enumerate(outs):
        ref[place] = keep_ref[i]
        ref[1 - place] = got_ref[i]


def attn_cut_kernel(side_ref, weight_ref, vec_ref, out_ref):
    side = side_ref[0]
    for start, width, to in ((0, QUERY, 0), (D, HD, QUERY), (D + KV * HD, HD, QUERY + HD)):
        first = pl.multiple_of(start + side * width, 128)
        out_ref[:, to : to + width] = weight_ref[:, pl.ds(first, width)].astype(bf16)
    out_ref[:, COLS : COLS + HD] = vec_ref[...]
    out_ref[:, COLS + HD :] = weight_ref[:, QKV:].astype(bf16)


def adam_update(weight, moment_one, moment_two, gradient, step_rate):
    moment_one = 0.9 * moment_one + 0.1 * gradient
    moment_two = 0.95 * moment_two + 0.05 * gradient * gradient
    first_hat = moment_one / (1.0 - 0.9**STEP)
    second_hat = moment_two / (1.0 - 0.95**STEP)
    updated = weight - step_rate * (first_hat / (jnp.sqrt(second_hat) + 1e-08) + 0.1 * weight)
    return (moment_one, moment_two, updated)


def core_kernel(core_ref, p0, p1, p2, p3, keep_ref, give_ref):
    core = core_ref[0]
    for i, part in enumerate((p0, p1, p2, p3)):
        keep_ref[i] = part[core]
        give_ref[i] = part[1 - core]


def ff_adam_kernel(rank_ref, keep_ref, got_ref, *refs):
    given, results, held, sems = refs[:3], refs[3:6], refs[6:9], refs[9]
    third = lambda ref, k: ref.at[:, pl.ds(k * FF, FF)]
    loads = [[pltpu.make_async_copy(third(a, k), third(b, k), sems.at[i, k]) for i, (a, b) in enumerate(zip(given, held))] for k in range(3)]
    stores = [[pltpu.make_async_copy(third(a, k), third(b, k), sems.at[3 + i, k]) for i, (a, b) in enumerate(zip(held, results))] for k in range(3)]
    for group in loads:
        for copy in group:
            copy.start()

    def put(block, cols):
        weight, one, two = (ref[:, cols] for ref in held)
        one, two, weight = adam_update(weight, one, two, block.astype(f32), 0.02)
        for ref, value in zip(held, (weight, one, two)):
            ref[:, cols] = value

    for k in range(3):
        for copy in loads[k]:
            copy.wait()
        for flip in range(8):
            grad = (keep_ref, got_ref)[flip % 2]
            rank = rank_ref[0] ^ flip
            for j in range(3):
                first = 2 * FFT + UNIT * j if k == 2 else 2 * UNIT * j + UNIT * k

                @pl.when(rank < 7)
                def _():
                    start = pl.multiple_of(k * FF + rank * FFT + j * UNIT, 128)
                    put(grad[flip // 2, :, first : first + UNIT], pl.ds(start, UNIT))

                skip = max(0, 8 * FFT - FF - j * UNIT)
                if skip < UNIT:

                    @pl.when(rank == 7)
                    def _():
                        start = k * FF + FF - FFT + j * UNIT + skip
                        put(grad[flip // 2, :, first + skip : first + UNIT], slice(start, start + UNIT - skip))

        for copy in stores[k]:
            copy.start()
    for group in stores:
        for copy in group:
            copy.wait()


def ff_adam(rank, keep, got, weight, moment_one, moment_two):
    shape = (ROWS, 3 * FF)
    scratch = [pltpu.VMEM(shape, f32)] * 3 + [pltpu.SemaphoreType.DMA((6, 3))]
    weight, one, two = call(
        ff_adam_kernel, [(shape, f32)] * 3, rank, keep, got, weight, moment_one, moment_two,
        smem=1, raw=(3, 4, 5), raw_outs=(0, 1, 2), scratch=scratch,
    )
    return one, two, weight


def attn_adam_kernel(flag_ref, part_ref, other_ref, w_ref, one_ref, two_ref, one_out, two_out, w_out):
    def put(grad, start):
        cols = slice(start, start + grad.shape[1])
        results = adam_update(w_ref[:, cols], one_ref[:, cols], two_ref[:, cols], grad, 0.05)
        for ref, value in zip((one_out, two_out, w_out), results):
            ref[:, cols] = value

    part, other = part_ref[...].astype(f32), other_ref[...].astype(f32)
    own_first = flag_ref[0] == 0
    first = jnp.where(own_first, part[:, :COLS], other[:, :COLS])
    last = jnp.where(own_first, other[:, :COLS], part[:, :COLS])
    put(first[:, :QUERY], 0)
    put(last[:, :QUERY], QUERY)
    put(first[:, QUERY : QUERY + HD], D)
    put(last[:, QUERY : QUERY + HD], D + HD)
    put(first[:, QUERY + HD :], D + KV * HD)
    put(last[:, QUERY + HD :], D + KV * HD + HD)
    put(jnp.where(flag_ref[1] == 1, part[:, COLS + HD :], other[:, COLS + HD :]), QKV)


def shards(
    inputs,
    cotangent,
    attn_weight,
    attn_moment_one,
    attn_moment_two,
    mlp_weight,
    mlp_moment_one,
    mlp_moment_two,
    vectors,
    vector_moment_one,
    vector_moment_two,
):
    half = lax.axis_index("seq")
    yh, core = lax.axis_index("yh"), lax.axis_index("core")
    side = half ^ yh
    rank = half * 4 + yh * 2 + core
    scalar = lambda v: v.astype(jnp.int32).reshape(1)
    x_own, dy_own = inputs[0], cotangent[0]

    vec_own = jnp.pad(vectors.astype(bf16)[None, :], ((0, 15), (0, 48)))
    vec_pair = jnp.concatenate([vec_own[:1], cross_send(vec_own)[:1]])
    vec_block = jnp.concatenate([vec_pair, core_send(jnp.pad(vec_pair, ((0, 14), (0, 0))))[:2]])
    vec_block = jnp.pad(vec_block, ((0, ROWS - 4), (0, 0)))

    mlp_keep, mlp_give = cut(scalar(rank), mlp_weight)
    mlp_got = core_send(mlp_give)
    (attn_block,) = call(
        attn_cut_kernel, [((ROWS, COLS + HD + D), bf16)], scalar(side), attn_weight, vec_block, smem=1, fetch=[1]
    )
    block = ((2, ROWS, 3 * FFT), bf16)
    mlp_near, mlp_far = call(
        order_kernel, [block, block], scalar(core), mlp_keep, mlp_got, smem=1, after=[attn_block]
    )
    mlp_far = cross_send(mlp_far)
    attn_x = join(ring_parts(attn_block, x_send))

    blocks = gathered_blocks(64)
    rows = as_rows((blocks[:, None] * ROWS + jnp.arange(ROWS, dtype=jnp.int32)[None, :]).reshape(D))
    z = lax.axis_index("z")
    inside = z // 2 == side
    first_z = jnp.where(inside, z, z ^ 2)
    j = jnp.arange(HALF, dtype=jnp.int32)
    r, xi, zi, yi, ci = j % 24, (j // 24) % 4, (j // 96) % 2, (j // 192) % 2, j // 384
    feature = ((first_z ^ zi) % 2) * 384 + (yh ^ yi) * 192 + (core ^ ci) * 24 + r
    features = as_rows(feature + (lax.axis_index("x") + near(xi) + 4) % 4 * 48)
    (x_rel,) = call(permute_kernel, [((LEN, D), bf16)], rows, x_own, seq_send(x_own), us=2, store=[0])
    dy_parts = gather_tokens(hold(dy_own, attn_x))

    flags = jnp.stack([inside, inside == (z % 2 == 0)]).astype(jnp.int32)
    part = ((2 * 4 * ROWS, COLS), bf16)
    *proj_z, vec_z, out_z = call(
        near_kernel, [part, part, ((4 * 4 * ROWS, HD), bf16), ((2 * 4 * ROWS, D), bf16)], flags,
        *ring_parts(attn_x, z_send), smem=1, after=dy_parts[1:4], behind=[x_rel],
    )

    (mlp_block,) = call(
        order_kernel, [((2,) + block[0], bf16)], scalar(yh), mlp_near[None], mlp_far[None], smem=1, after=[vec_z]
    )
    mlp_w = lax.all_gather(mlp_block.reshape(4 * ROWS, 3 * FFT), ("z", "x"), axis=0, tiled=True)
    mlp_w = mlp_w.reshape(4, 4, 2, 48, 3 * FFT)

    proj_y = [cross_send(p) for p in proj_z]
    out_y = cross_send(out_z)
    proj_w = proj_z + proj_y
    proj_w = proj_w + [core_send(p) for p in proj_w]

    place = jnp.arange(64, dtype=jnp.int32)
    by_vector = blocks[(place % 4) % 2 * 16 + (place % 4) // 2 * 32 + place // 4]
    pick = (place[:, None] == by_vector[None, :]).astype(bf16)
    vec_rel = vec_z.reshape(16, ROWS, HD)[:, :4].reshape(64, HD)
    vec_all = dot(pick, vec_rel)[:, :80].reshape(1, 5120)
    gain_rows = jnp.broadcast_to(vec_all[:, :D].astype(bf16), (16, D))
    gain_one = call(permute_kernel, [((16, D), f32)], rows, gain_rows, us=1)[0][:1]
    gain_two = vec_all[:, D : 2 * D]
    bias_all = vec_all[:, 2 * D :]
    own_cols = lambda a, start, width: lax.dynamic_slice_in_dim(a, start + side * width, width, 1)
    bias = jnp.concatenate(
        [
            own_cols(bias_all, 0, QUERY),
            own_cols(bias_all, D, HD),
            own_cols(bias_all, D + KV * HD, HD),
        ],
        axis=1,
    )

    cos, sin = rotary_tables((jnp.arange(LEN) + half * TOK) % LEN)
    normed, low, heads_out, logs = attend(
        scalar(half), x_rel, gain_one, proj_w, bias, cos, sin
    )
    out_y = hold(out_y, behind=[normed])
    out_w = [out_z, out_y, core_send(out_z), core_send(out_y)]
    a_rel, branch_own, branch_give = branch(heads_out, features, out_w)
    middle, second = call(
        second_kernel, [((TOK, D), f32), ((TOK, D), bf16)], x_own, branch_own, seq_send(branch_give), gain_two,
        us=2, store=[0, 1],
    )

    second_parts = gather_tokens(second)
    hidden, d_gate_up, d_second_own, d_second_give = feed_forward(second_parts, dy_parts, mlp_w)
    d_second = call(
        add_kernel, [((TOK, D), f32)] + [((TOK, D), bf16)] * 3, d_second_own, core_send(d_second_give)
    )
    mlp_term = ff_grad(second_parts, dy_parts, hidden, d_gate_up, [d_second[0]])
    mlp_part = lax.psum_scatter(
        mlp_term.reshape(D, 3 * FFT), ("z", "x"), scatter_dimension=0, tiled=True
    )
    d_middle, e, d_gain_two = d_middle_of(
        ring_collect(d_second, y_send), middle, gain_two, dy_own, [mlp_term]
    )
    down_own, down_give = down_terms(hidden, mlp_w, [e])

    e_other = seq_send(e)
    out_term = out_terms(a_rel, e, e_other, [down_give])
    (out_far,) = add_up([out_term[1], core_send(out_term[3])], fetch=True)
    (out_near,) = add_up([out_term[0], core_send(out_term[2])], fetch=True)
    out_got = cross_send(out_far)
    *proj_term, d_proj, d_bias_own = attend_back(
        scalar(half), e, e_other, out_w, features, low, logs, cos, sin, normed, [out_far]
    )
    dh_own, dh_give, d_gain_one = d_normed_of(d_proj, x_rel, proj_w)

    (proj_far,) = call(
        far_add_kernel, [((PIECE, COLS), bf16)], proj_term[1], core_send(proj_term[3]), core_send(proj_term[4]),
        fetch=range(3), after=[out_got], behind=[dh_own],
    )
    (proj_near,) = add_up([proj_term[0], core_send(proj_term[2])], fetch=True)
    bias_zero = jnp.zeros((1, QKV), f32)
    put = lambda a, v, start, width: lax.dynamic_update_slice_in_dim(a, v, start + side * width, 1)
    d_bias = put(bias_zero, d_bias_own[:, :QUERY], 0, QUERY)
    d_bias = put(d_bias, d_bias_own[:, QUERY : QUERY + HD], D, HD)
    d_bias = put(d_bias, d_bias_own[:, QUERY + HD :], D + KV * HD, HD)
    d_gain_rows = jnp.broadcast_to(d_gain_one, (8, D))
    d_gain_one = call(unpermute_kernel, [((8, D), f32)], rows, d_gain_rows, us=2)[0][:1]
    vec_term = jnp.concatenate([d_gain_one, d_gain_two, d_bias], axis=1)
    vec_term = jnp.pad(vec_term.reshape(64, 80), ((0, 0), (0, 48))).astype(bf16)
    pick_rel = (place[:, None] == blocks[None, :]).astype(bf16)
    vec_term = dot_tn(pick_rel, vec_term)
    vec_half = pair_reduce(vec_term, core_send)
    vec_got = pair_reduce(vec_half, cross_send)
    vec_term = jnp.pad(vec_got[:, None, :], ((0, 0), (0, ROWS - 1), (0, 0))).reshape(PIECE, HD)
    down = call(
        add_kernel, [((TOK, D), f32)] + [((TOK, D), bf16)] * 3, down_own, core_send(hold(down_give, proj_far)),
        after=[vec_half],
    )
    dh_got = seq_send(dh_give)
    attn_parts = call(
        far_kernel, [((4 * ROWS, COLS + HD + D), bf16)] * 4,
        proj_near, cross_send(proj_far), vec_term, out_near, out_got, after=[down[1], dh_got],
    )
    attn_near = ring_collect(attn_parts, z_send)
    down = ring_collect(down, y_send)
    (input_grad,) = call(
        input_grad_kernel, [((TOK, D), f32)], dh_own, dh_got, x_rel, gain_one, d_middle, rows,
        us=5, fetch=[0, 2, 4], store=[0], after=[attn_parts[0]],
    )
    attn_parts = add_up(attn_near, pieces=4, after=down[1:], behind=[input_grad])

    by_y = hold(mlp_part, behind=[input_grad]).reshape(2, 2, ROWS, 3 * FFT)
    near_rows = lax.dynamic_index_in_dim(by_y, yh, 0, keepdims=False)
    far_rows = lax.dynamic_index_in_dim(by_y, 1 - yh, 0, keepdims=False)
    block = ((4, ROWS, 3 * FFT), bf16)
    grads_keep, grads_give = call(
        core_kernel, [block, block], scalar(core),
        near_rows, ring_send(far_rows, "yh", 1), seq_send(near_rows), cross_send(far_rows), smem=1,
    )
    mlp_one, mlp_two, mlp_new = ff_adam(
        scalar(rank), grads_keep, core_send(grads_give), mlp_weight, mlp_moment_one, mlp_moment_two
    )
    (attn_part,) = add_up(ring_collect(attn_parts, x_send))
    attn_other = hold(seq_send(attn_part), behind=[mlp_one])
    vec_cols = slice(COLS, COLS + 80)
    vec_grad = attn_part[0, vec_cols].astype(f32) + attn_other[0, vec_cols].astype(f32)

    attn_one, attn_two, attn_new = call(
        attn_adam_kernel,
        [((ROWS, QKV + D), f32)] * 3,
        jnp.stack([side, inside.astype(side.dtype)]).astype(jnp.int32),
        attn_part,
        attn_other,
        attn_weight,
        attn_moment_one,
        attn_moment_two,
        smem=1,
    )

    total = down[0] + down[1].astype(f32) + down[2].astype(f32) + down[3].astype(f32)
    output = (middle + total).astype(bf16)[None]
    vec_one, vec_two, vec_new = adam_update(
        vectors, vector_moment_one, vector_moment_two, vec_grad, 0.5
    )
    return (
        output,
        input_grad[None],
        attn_one,
        attn_two,
        attn_new,
        mlp_one,
        mlp_two,
        mlp_new,
        vec_one,
        vec_two,
        vec_new,
    )


def solution(mesh):
    grid = Mesh(mesh.devices.reshape(2, 4, 2, 4, 2), ("seq",) + FSDP)
    tokens, rows, vector = P(FSDP, "seq", None), P(FSDP, None), P(FSDP)
    return jax.shard_map(
        shards,
        mesh=grid,
        in_specs=(tokens, tokens) + (rows,) * 6 + (vector,) * 3,
        out_specs=(tokens, tokens) + (rows,) * 6 + (vector,) * 3,
        check_vma=False,
    )
```

```python
import math

import jax
import jax.numpy as jnp
from jax import lax
from jax.experimental import pallas as pl
from jax.experimental.pallas import tpu as pltpu
from jax.sharding import Mesh
from jax.sharding import PartitionSpec as P

D = 1536
H = 12
KV = 2
HD = 128
FF = 8960
STEP = 10
QKV = 2048
ROWS = 24
TOK = 128
LEN = 256
HALF = D // 2
GROUP = H // KV
QUERY = GROUP * HD
COLS = QUERY + 2 * HD
FFT = 1152
UNIT = FFT // 3
PIECE = D // 4
LINE = HALF // 4
MIB = 1024 * 1024

norm_eps = 1e-06
rope_base = 1000000.0
f32 = jnp.float32
bf16 = jnp.bfloat16
contract_rows = (((0,), (0,)), ((), ()))
contract_cols = (((1,), (1,)), ((), ()))
score_scale = HD ** (-0.5)
FSDP = ("z", "yh", "x", "core")
SIZES = {"seq": 2, "z": 4, "yh": 2, "x": 4, "core": 2}


def dot(a, b):
    return jnp.dot(a, b, preferred_element_type=f32)


def dot_tn(a, b):
    return lax.dot_general(a, b, contract_rows, preferred_element_type=f32)


def dot_nt(a, b):
    return lax.dot_general(a, b, contract_cols, preferred_element_type=f32)


def split_dot_nt(a, b):
    high = a.astype(bf16)
    low = (a - high.astype(f32)).astype(bf16)
    return dot_nt(high, b) + dot_nt(low, b)


def ring_send(values, axis, shift):
    size = SIZES[axis]
    return lax.ppermute(values, axis, [(i, (i + shift) % size) for i in range(size)])


def x_send(values, shift):
    return ring_send(values, "x", shift)


def z_send(values, shift):
    return ring_send(values, "z", shift)


def y_send(values, shift):
    place = lambda y: (y % 2) * 2 + y // 2
    return lax.ppermute(
        values, ("seq", "yh"), [(place(i), place((i + shift) % 4)) for i in range(4)]
    )


def cross_send(values):
    return lax.ppermute(values, ("seq", "yh"), [(i, 3 - i) for i in range(4)])


def core_send(values):
    return ring_send(values, "core", 1)


def seq_send(values):
    return ring_send(values, "seq", 1)


def ring_parts(values, send):
    return [values, send(values, 1), send(values, -1), send(values, 2)]


def pair_reduce(values, send):
    rows = values.shape[0] // 2
    return values[:rows] + send(values[rows:].astype(bf16)).astype(f32)


def ring_collect(parts, send):
    return [parts[0], send(parts[1], -1), send(parts[2], 1), send(parts[3], 2)]


def gather_tokens(values):
    parts = ring_parts(values, y_send)
    return parts + [core_send(p) for p in parts]


def near(index):
    return jnp.where(index == 1, -1, jnp.where(index == 0, 0, index - 1))


def gathered_blocks(count):
    j = jnp.arange(count, dtype=jnp.int32)
    xi, zi, yi, ci = j % 4, (j // 4) % 4, (j // 16) % 2, j // 32
    z = (lax.axis_index("z") + near(zi) + 4) % 4
    x = (lax.axis_index("x") + near(xi) + 4) % 4
    yh = (lax.axis_index("yh") + yi) % 2
    core = (lax.axis_index("core") + ci) % 2
    return z * 16 + yh * 8 + x * 2 + core


def call(
    kernel, outs, *args, us=1, smem=0, fetch=(), raw=(), store=(), raw_outs=(), scratch=(), room=6, after=(), behind=(), late=(), early=False
):
    vmem, hbm = pl.BlockSpec(memory_space=pltpu.VMEM), pl.BlockSpec(memory_space=pltpu.HBM)
    fetch = [g if isinstance(g, tuple) else (g,) for g in fetch]
    far = set(raw) | {i for g in fetch for i in g}
    specs = [
        pl.BlockSpec(memory_space=pltpu.SMEM) if i < smem else hbm if i in far else vmem
        for i in range(len(args))
    ] + [pl.BlockSpec(memory_space=pl.ANY)] * len(after) + [hbm] * len(behind)
    after = list(after) + [in_hbm(a) for a in behind]
    buffers = []
    for g in fetch:
        rows = sum(args[i].shape[0] for i in g)
        buffers.append(((rows,) + args[g[0]].shape[1:], args[g[0]].dtype))
    buffers += [outs[i] for i in store]
    held = [pltpu.VMEM(shape, kind) for shape, kind in buffers]
    moves = max(1, sum(len(g) for g in fetch) + len(store))
    n_in, n_out, n_own = len(args), len(outs), len(scratch)

    def body(*refs):
        ins, refs = list(refs[:n_in]), refs[n_in + len(after) :]
        out_refs, own = list(refs[:n_out]), refs[n_out : n_out + n_own]
        held_refs, sems = refs[n_out + n_own : -1], refs[-1]
        copies, last, k = [], [], 0
        for n, (g, ref) in enumerate(zip(fetch, held_refs)):
            row = 0
            for i in g:
                rows = args[i].shape[0]
                copy = pltpu.make_async_copy(ins[i], ref.at[pl.ds(row, rows)], sems.at[k])
                (last if n in late else copies).append(copy)
                row, k = row + rows, k + 1
            ins[g[0]] = ref
        for copy in copies + last:
            copy.start()
        for copy in copies:
            copy.wait()

        def wait_late():
            for copy in last:
                copy.wait()

        drop = {i for g in fetch for i in g[1:]}
        ins = [ref for i, ref in enumerate(ins) if i not in drop]
        leaving, gone = [], []
        for i, ref in zip(store, held_refs[len(fetch) :]):
            leaving.append(pltpu.make_async_copy(ref, out_refs[i], sems.at[k]))
            out_refs[i] = ref
            k += 1

        def leave(n):
            gone.append(n)
            leaving[n].start()

        kernel(*([wait_late] if late else []), *([leave] if early else []), *ins, *out_refs, *own)
        for n, copy in enumerate(leaving):
            if n not in gone:
                copy.start()
        for copy in leaving:
            copy.wait()

    size = lambda shape, kind: math.prod(shape) * jnp.dtype(kind).itemsize
    used = sum(size(*b) for b in buffers)
    used += sum(size(b.shape, b.dtype) for b in scratch if hasattr(b, "shape") and b.memory_space == pltpu.VMEM)
    args = [
        in_hbm(a) if i in far else a
        for i, a in enumerate(args)
    ]
    leave = lambda i: pltpu.HBM if i in raw_outs or i in store else jax.ShapeDtypeStruct
    return pl.pallas_call(
        body,
        out_shape=tuple(leave(i)(shape, kind) for i, (shape, kind) in enumerate(outs)),
        in_specs=specs,
        out_specs=tuple(hbm if i in raw_outs or i in store else vmem for i in range(n_out)),
        scratch_shapes=list(scratch) + held + [pltpu.SemaphoreType.DMA((moves,))],
        cost_estimate=pl.CostEstimate(flops=us * 10**7, bytes_accessed=us * 10**4, transcendentals=0),
        compiler_params=pltpu.CompilerParams(vmem_limit_bytes=used + room * MIB),
    )(*args, *after)


def hold_kernel(*refs):
    pass


def in_hbm(values):
    return pltpu.with_memory_space_constraint(values, pltpu.HBM)


def hold(values, *after, behind=()):
    anywhere, hbm = pl.BlockSpec(memory_space=pl.ANY), pl.BlockSpec(memory_space=pltpu.HBM)
    return pl.pallas_call(
        hold_kernel,
        out_shape=jax.ShapeDtypeStruct(values.shape, values.dtype),
        in_specs=[anywhere] * (1 + len(after)) + [hbm] * len(behind),
        out_specs=anywhere,
        input_output_aliases={0: 0},
    )(values, *after, *(in_hbm(a) for a in behind))


def join_kernel(*refs):
    out_ref, row = refs[-1], 0
    for ref in refs[:-1]:
        out_ref[row : row + ref.shape[0], :] = ref[...]
        row += ref.shape[0]


def join(parts):
    rows = sum(p.shape[0] for p in parts)
    return call(join_kernel, [((rows, parts[0].shape[1]), bf16)], *parts)[0]


def sum_kernel(count, given, outs):
    groups = []
    for i in range(0, len(given), count):
        total = given[i][...].astype(f32)
        for ref in given[i + 1 : i + count]:
            total = total + ref[...].astype(f32)
        groups.append(total)
    rows, col = outs[0].shape[0], 0
    for total in groups:
        for i, ref in enumerate(outs):
            part = total[i * rows : (i + 1) * rows, :]
            ref[:, col : col + total.shape[1]] = part.astype(ref.dtype)
        col += total.shape[1]


def add_up(parts, pieces=1, count=None, after=(), behind=(), fetch=False):
    count = count or len(parts)
    cols = sum(p.shape[1] for p in parts[::count])
    outs = [((parts[0].shape[0] // pieces, cols), bf16)] * pieces
    kernel = lambda *refs: sum_kernel(count, refs[: len(parts)], refs[len(parts) :])
    fetch = range(len(parts)) if fetch else ()
    return call(kernel, outs, *parts, after=after, behind=behind, fetch=fetch)


def place(rows_ref, size, cols):
    row = lax.broadcasted_iota(jnp.int32, (size, cols.stop - cols.start), 0)
    return jnp.where(row == rows_ref[:1, cols], 1.0, 0.0).astype(bf16)


PIECES = [slice(i * PIECE, (i + 1) * PIECE) for i in range(4)]


def permute_kernel(rows_ref, *refs):
    out_ref = refs[-1]
    for cols in PIECES:
        here, row = place(rows_ref, D, cols), 0
        for ref in refs[:-1]:
            out_ref[row : row + ref.shape[0], cols] = dot(ref[...], here).astype(out_ref.dtype)
            row += ref.shape[0]


def unpermute_kernel(rows_ref, values_ref, out_ref):
    out = jnp.zeros(out_ref.shape, f32)
    for cols in PIECES:
        out += split_dot_nt(values_ref[:, cols], place(rows_ref, D, cols))
    out_ref[...] = out


def as_rows(rows):
    return jnp.broadcast_to(rows[None, :].astype(jnp.int32), (8, rows.shape[0]))


def rotary_tables(positions):
    half_dim = HD // 2
    freqs = rope_base ** (-jnp.arange(half_dim, dtype=f32) * 2.0 / HD)
    angles = positions.astype(f32)[:, None] * freqs[None, :]
    cos, sin = jnp.cos(angles), jnp.sin(angles)
    return jnp.concatenate([cos, cos], axis=1), jnp.concatenate([-sin, sin], axis=1)


def causal_mask(half):
    row = (lax.broadcasted_iota(jnp.int32, (LEN, LEN), 0) + half * TOK) % LEN
    col = (lax.broadcasted_iota(jnp.int32, (LEN, LEN), 1) + half * TOK) % LEN
    return row >= col


def norm_scale(values):
    return lax.rsqrt(jnp.mean(values * values, axis=-1, keepdims=True) + norm_eps)


def attend_kernel(
    wait_weights, half_ref, x_ref, gain_ref, w_ref, bias_ref, cos_ref, sin_ref,
    normed_ref, low_ref, out_ref, log_ref, qkv_ref,
):
    x = x_ref[...].astype(f32)
    normed_ref[...] = (x * norm_scale(x) * gain_ref[...]).astype(bf16)
    wait_weights()
    qkv_ref[...] = dot(normed_ref[...], w_ref[...]) + bias_ref[...]
    cos, sin = cos_ref[...], sin_ref[...]
    mask = causal_mask(half_ref[0])

    def rotated(start):
        z = qkv_ref[:, start : start + HD]
        return (z * cos + pltpu.roll(z, HD // 2, 1) * sin).astype(bf16)

    key = rotated(QUERY)
    low_ref[:, QUERY : QUERY + HD] = key
    value = qkv_ref[:, QUERY + HD :].astype(bf16)
    low_ref[:, QUERY + HD :] = value
    for h in range(GROUP):
        query = rotated(h * HD)
        low_ref[:, h * HD : (h + 1) * HD] = query
        scores = jnp.where(mask, dot_nt(query, key) * score_scale, -1e30)
        top = jnp.max(scores, axis=-1, keepdims=True)
        total = top + jnp.log(jnp.sum(jnp.exp(scores - top), axis=-1, keepdims=True))
        log_ref[h] = jnp.broadcast_to(total, (LEN, HD))
        probs = jnp.exp(scores - total).astype(bf16)
        out_ref[:, h * HD : (h + 1) * HD] = dot(probs, value).astype(bf16)


def attend(half, x_rel, gain, proj, bias, cos, sin):
    outs = [((LEN, D), bf16), ((LEN, COLS), bf16), ((LEN, QUERY), bf16), ((GROUP, LEN, HD), f32)]
    return call(
        attend_kernel, outs, half, x_rel, gain, *proj, bias, cos, sin,
        us=6, smem=1, fetch=[1, tuple(range(3, 11))], late=[1], store=[0, 1, 2, 3], scratch=[pltpu.VMEM((LEN, COLS), f32)],
    )


def branch_kernel(a_ref, rows_ref, w_ref, rel_ref, own_ref, give_ref):
    rel_ref[...] = dot(a_ref[...], place(rows_ref, HALF, slice(0, HALF))).astype(bf16)
    own_ref[...] = dot(rel_ref[:TOK, :], w_ref[...])
    give_ref[...] = dot(rel_ref[TOK:, :], w_ref[...]).astype(bf16)


def branch(a, rows, out_w):
    outs = [((LEN, HALF), bf16), ((TOK, D), f32), ((TOK, D), bf16)]
    return call(branch_kernel, outs, a, rows, *out_w, us=4, fetch=[0, (2, 3, 4, 5)], store=[0])


def second_kernel(x_ref, own_ref, got_ref, gain_ref, middle_ref, second_ref):
    middle = x_ref[...].astype(f32) + own_ref[...] + got_ref[...].astype(f32)
    middle_ref[...] = middle
    second_ref[...] = (middle * norm_scale(middle) * gain_ref[...]).astype(bf16)


def load_tokens(parts, whole, sems):
    copies = []
    for i, part in enumerate(parts):
        copies.append(pltpu.make_async_copy(part, whole.at[pl.ds(i * TOK, TOK), :], sems.at[i]))
        copies[-1].start()
    return copies


def ff_kernel(*refs):
    h_parts, dy_parts, refs = refs[:8], refs[8:16], refs[16:]
    w_ref, hid_out, dgu_out, own_ref, give_ref, h_all, dy_all, w, hid, dgu, h_sem, dy_sem, w_sem, out_sem = refs
    tokens = load_tokens(h_parts, h_all, h_sem) + load_tokens(dy_parts, dy_all, dy_sem)
    loads = []
    for j in range(3):
        for k, (start, width) in enumerate(((2 * UNIT * j, 2 * UNIT), (2 * FFT + UNIT * j, UNIT))):
            for y in range(2):
                copy = pltpu.make_async_copy(
                    w_ref.at[:, :, y, :, pl.ds(start, width)],
                    w.at[:, y, :, :, pl.ds(start, width)],
                    w_sem.at[j * 4 + k * 2 + y],
                )
                copy.start()
                loads.append(copy)
    for copy in tokens:
        copy.wait()
    tile = 512
    for j in range(3):
        for copy in loads[4 * j : 4 * j + 4]:
            copy.wait()

        @pl.loop(0, 8 * TOK // tile)
        def _(m):
            rows = pl.ds(pl.multiple_of(m * tile, tile), tile)
            pair = slice(2 * UNIT * j, 2 * UNIT * (j + 1))
            last = slice(2 * FFT + UNIT * j, 2 * FFT + UNIT * (j + 1))
            gate_up = dot(h_all[rows, :], w[:, :, :, :, pair].reshape(D, 2 * UNIT))
            d_hidden = dot(dy_all[rows, :], w[:, :, :, :, last].reshape(D, UNIT))
            gate, up = gate_up[:, :UNIT], gate_up[:, UNIT:]
            sigmoid_gate = jax.nn.sigmoid(gate)
            act = gate * sigmoid_gate
            hid[rows, UNIT * j : UNIT * (j + 1)] = (act * up).astype(bf16)
            d_gate = d_hidden * up * (sigmoid_gate * (1.0 + gate * (1.0 - sigmoid_gate)))
            dgu[rows, 2 * UNIT * j : 2 * UNIT * j + UNIT] = d_gate.astype(bf16)
            dgu[rows, 2 * UNIT * j + UNIT : 2 * UNIT * (j + 1)] = (d_hidden * act).astype(bf16)

    outs = [
        pltpu.make_async_copy(hid, hid_out, out_sem.at[0]),
        pltpu.make_async_copy(dgu, dgu_out, out_sem.at[1]),
    ]
    for copy in outs:
        copy.start()
    for z in range(2):
        cols = slice(2 * z * PIECE, 2 * (z + 1) * PIECE)
        wz = w[2 * z : 2 * (z + 1), :, :, :, : 2 * FFT].reshape(2 * PIECE, 2 * FFT)
        for i, ref in enumerate((own_ref, give_ref)):
            rows = slice(i * 4 * TOK, (i + 1) * 4 * TOK)
            ref[:, cols] = dot_nt(dgu[rows, :], wz).astype(ref.dtype)
    for copy in outs:
        copy.wait()


def feed_forward(h_parts, dy_parts, w):
    tokens = 8 * TOK
    outs = [
        ((tokens, FFT), bf16),
        ((tokens, 2 * FFT), bf16),
        ((4 * TOK, D), f32),
        ((4 * TOK, D), bf16),
    ]
    scratch = [
        pltpu.VMEM((tokens, D), bf16),
        pltpu.VMEM((tokens, D), bf16),
        pltpu.VMEM((4, 2, 4, 48, 3 * FFT), bf16),
        pltpu.VMEM((tokens, FFT), bf16),
        pltpu.VMEM((tokens, 2 * FFT), bf16),
        pltpu.SemaphoreType.DMA((8,)),
        pltpu.SemaphoreType.DMA((8,)),
        pltpu.SemaphoreType.DMA((12,)),
        pltpu.SemaphoreType.DMA((2,)),
    ]
    return call(
        ff_kernel, outs, *h_parts, *dy_parts, w, us=25, raw=range(17), raw_outs=(0, 1), scratch=scratch
    )


def ff_grad_kernel(*refs):
    h_parts, dy_parts, refs = refs[:8], refs[8:16], refs[16:]
    hid_ref, dgu_ref, term_ref, h_all, dy_all, hid, dgu, term, h_sem, dy_sem, in_sem, t_sem = refs
    last = load_tokens(dy_parts, dy_all, dy_sem) + [pltpu.make_async_copy(hid_ref, hid, in_sem.at[1])]
    last[-1].start()
    first = load_tokens(h_parts, h_all, h_sem) + [pltpu.make_async_copy(dgu_ref, dgu, in_sem.at[0])]
    first[-1].start()
    for copy in last:
        copy.wait()
    outs = []
    for z in range(4):
        cols = slice(z * PIECE, (z + 1) * PIECE)
        for start in (2 * FFT, 2 * FFT + 2 * UNIT, 0, 2 * UNIT, 4 * UNIT):
            width = min(2 * UNIT, 3 * FFT - start)
            if start >= 2 * FFT:
                out = dot_tn(dy_all[:, cols], hid[:, start - 2 * FFT : start - 2 * FFT + width])
            else:
                if z == 0 and start == 0:
                    for copy in first:
                        copy.wait()
                out = dot_tn(h_all[:, cols], dgu[:, start : start + width])
            term[z, :, :, :, start : start + width] = out.astype(bf16).reshape(2, 4, 48, width)
        for y in range(2):
            copy = pltpu.make_async_copy(term.at[z, y], term_ref.at[z, :, y], t_sem.at[z, y])
            copy.start()
            outs.append(copy)
    for copy in outs:
        copy.wait()


def ff_grad(h_parts, dy_parts, hid, dgu, after):
    tokens = 8 * TOK
    scratch = [
        pltpu.VMEM((tokens, D), bf16),
        pltpu.VMEM((tokens, D), bf16),
        pltpu.VMEM((tokens, FFT), bf16),
        pltpu.VMEM((tokens, 2 * FFT), bf16),
        pltpu.VMEM((4, 2, 4, 48, 3 * FFT), bf16),
        pltpu.SemaphoreType.DMA((8,)),
        pltpu.SemaphoreType.DMA((8,)),
        pltpu.SemaphoreType.DMA((2,)),
        pltpu.SemaphoreType.DMA((4, 2)),
    ]
    return call(
        ff_grad_kernel, [((4, 4, 2, 48, 3 * FFT), bf16)], *h_parts, *dy_parts, hid, dgu,
        us=17, raw=range(18), raw_outs=(0,), scratch=scratch, after=after,
    )[0]


def down_kernel(hid_ref, w_ref, own_ref, give_ref, w, w_sem):
    loads = []
    for z in range(4):
        for y in range(2):
            load = pltpu.make_async_copy(
                w_ref.at[z, :, y, :, pl.ds(2 * FFT, FFT)], w.at[z, y], w_sem.at[z, y]
            )
            load.start()
            loads.append(load)
    for z in range(2):
        for load in loads[4 * z : 4 * z + 4]:
            load.wait()
        cols = slice(2 * z * PIECE, 2 * (z + 1) * PIECE)
        wz = w[2 * z : 2 * (z + 1)].reshape(2 * PIECE, FFT)
        for i, ref in enumerate((own_ref, give_ref)):
            rows = slice(i * 4 * TOK, (i + 1) * 4 * TOK)
            ref[:, cols] = dot_nt(hid_ref[rows, :], wz).astype(ref.dtype)


def down_terms(hidden, w, after):
    outs = [((4 * TOK, D), f32), ((4 * TOK, D), bf16)]
    scratch = [pltpu.VMEM((4, 2, 4, 48, FFT), bf16), pltpu.SemaphoreType.DMA((4, 2))]
    return call(
        down_kernel, outs, hidden, w, us=8, fetch=[0], raw=(1,), store=[0], scratch=scratch, after=after
    )


def add_kernel(own_ref, got_ref, keep_ref, g1_ref, g2_ref, g3_ref):
    for i, ref in enumerate((keep_ref, g1_ref, g2_ref, g3_ref)):
        rows = slice(i * TOK, (i + 1) * TOK)
        ref[...] = (own_ref[rows, :] + got_ref[rows, :].astype(f32)).astype(ref.dtype)


def d_middle_kernel(p0, p1, p2, p3, middle_ref, gain_ref, dy_ref, d_middle_ref, e_ref, d_gain_ref):
    d_second = p0[...] + p1[...].astype(f32) + p2[...].astype(f32) + p3[...].astype(f32)
    middle = middle_ref[...]
    inv = norm_scale(middle)
    unit = middle * inv
    scaled = d_second * gain_ref[...]
    d_gain_ref[...] = jnp.sum(d_second * unit, axis=0, keepdims=True)
    d_middle = dy_ref[...].astype(f32) + inv * (
        scaled - unit * jnp.mean(scaled * unit, axis=-1, keepdims=True)
    )
    d_middle_ref[...] = d_middle
    e_ref[...] = d_middle.astype(bf16)


def d_middle_of(parts, middle, gain, dy, behind):
    outs = [((TOK, D), f32), ((TOK, D), bf16), ((1, D), f32)]
    return call(
        d_middle_kernel, outs, *parts, middle, gain, dy, us=20000, fetch=[4, 6], store=[0], behind=behind
    )


def out_term_kernel(a_ref, e0_ref, e1_ref, t0, t1, t2, t3):
    total = dot_tn(a_ref[:TOK, :], e0_ref[...]) + dot_tn(a_ref[TOK:, :], e1_ref[...])
    for i, ref in enumerate((t0, t1, t2, t3)):
        ref[...] = total[i * LINE : (i + 1) * LINE, :].astype(bf16)


def out_terms(a_rel, e, e_other, after):
    outs = [((LINE, D), bf16)] * 4
    return call(out_term_kernel, outs, a_rel, e, e_other, us=2, fetch=[0], store=range(4), room=10, after=after)


def attend_back_kernel(
    wait_normed, leave, half_ref, e0_ref, e1_ref, out_w_ref, rows_ref, low_ref, log_ref, cos_ref, sin_ref, normed_ref,
    t0, t1, t2, t3, t4, out_ref, sum_ref, grad_ref,
):
    cos, sin = cos_ref[...], sin_ref[...]
    mask = causal_mask(half_ref[0])
    here = place(rows_ref, HALF, slice(0, HALF))
    for i, e_ref in enumerate((e0_ref, e1_ref)):
        rel = dot_nt(e_ref[...], out_w_ref[...]).astype(bf16)
        grad_ref[i * TOK : (i + 1) * TOK, :] = dot_nt(rel, here).astype(bf16)
    key = low_ref[:, QUERY : QUERY + HD]
    value = low_ref[:, QUERY + HD :]

    def unrotated(z):
        return (z * cos - pltpu.roll(z, HD // 2, 1) * sin).astype(bf16)

    def put(start, block):
        out_ref[:, start : start + HD] = block
        sum_ref[:, start : start + HD] = jnp.sum(block.astype(f32), axis=0, keepdims=True)

    d_key = jnp.zeros((LEN, HD), f32)
    d_value = jnp.zeros((LEN, HD), f32)
    for h in range(GROUP):
        query = low_ref[:, h * HD : (h + 1) * HD]
        grad = grad_ref[:, h * HD : (h + 1) * HD]
        scores = jnp.where(mask, dot_nt(query, key) * score_scale, -1e30)
        total = log_ref[h]
        probs = jnp.exp(scores - jnp.concatenate([total, total], axis=1))
        d_probs = dot_nt(grad, value)
        delta = jnp.sum(probs * d_probs, axis=-1, keepdims=True)
        d_scores = (probs * (d_probs - delta)).astype(bf16)
        put(h * HD, unrotated(dot(d_scores, key) * score_scale))
        d_key += dot_tn(d_scores, query)
        d_value += dot_tn(probs.astype(bf16), grad)
    put(QUERY, unrotated(d_key * score_scale))
    put(QUERY + HD, d_value.astype(bf16))
    leave(5)
    wait_normed()
    last = dot_tn(normed_ref[:, 3 * PIECE :], out_ref[...]).astype(bf16)
    t3[...] = last[:LINE, :]
    leave(3)
    t4[...] = last[LINE:, :]
    leave(4)
    for i, ref in enumerate((t0, t1, t2)):
        ref[...] = dot_tn(normed_ref[:, i * PIECE : (i + 1) * PIECE], out_ref[...]).astype(bf16)
        leave(i)


def attend_back(half, e, e_other, out_w, rows, low, logs, cos, sin, normed, after):
    outs = [((PIECE, COLS), bf16)] * 3 + [((LINE, COLS), bf16)] * 2
    outs += [((LEN, COLS), bf16), ((1, COLS), f32)]
    return call(
        attend_back_kernel, outs, half, e, e_other, *out_w, rows, low, logs, cos, sin, normed,
        us=9, smem=1, fetch=[(3, 4, 5, 6), 8, 9, 12], late=[3], early=True, store=range(6),
        scratch=[pltpu.VMEM((LEN, QUERY), bf16)],
        room=8, after=after,
    )


def d_normed_kernel(d_ref, x_ref, w_ref, own_ref, give_ref, d_gain_ref):
    x = x_ref[...].astype(f32)
    d_normed = dot_nt(d_ref[...], w_ref[...])
    own_ref[...] = d_normed[:TOK, :]
    give_ref[...] = d_normed[TOK:, :].astype(bf16)
    d_gain_ref[...] = jnp.sum(d_normed * (x * norm_scale(x)), axis=0, keepdims=True)


def d_normed_of(d_proj, x_rel, proj):
    outs = [((TOK, D), f32), ((TOK, D), bf16), ((1, D), f32)]
    return call(
        d_normed_kernel, outs, d_proj, x_rel, *proj, us=3, fetch=[0, 1, tuple(range(2, 10))], store=[0, 1], room=8
    )


def input_grad_kernel(own_ref, got_ref, x_ref, gain_ref, d_middle_ref, rows_ref, out_ref):
    scaled = (own_ref[...] + got_ref[...].astype(f32)) * gain_ref[...]
    x = x_ref[:TOK, :].astype(f32)
    inv = norm_scale(x)
    unit = x * inv
    through = inv * (scaled - unit * jnp.mean(scaled * unit, axis=-1, keepdims=True))
    total = d_middle_ref[...]
    for cols in PIECES:
        total += split_dot_nt(through[:, cols], place(rows_ref, D, cols))
    out_ref[...] = total


def cut_kernel(rank_ref, weight_ref, keep_ref, send_ref, held_ref, sem):
    col = lax.broadcasted_iota(jnp.int32, (ROWS, UNIT), 1)
    ranks = [rank_ref[0] ^ flip for flip in (1, 7, 0, 6)]
    starts = [jnp.minimum(rank * FFT, FF - FFT) for rank in ranks]
    copies = []
    for n, start in enumerate(starts):
        for k in range(3):
            first = pl.multiple_of(k * FF + start, 128)
            copies.append(
                pltpu.make_async_copy(
                    weight_ref.at[:, pl.ds(first, FFT)], held_ref.at[n, k], sem.at[n, k]
                )
            )
            copies[-1].start()
    for n, (rank, start) in enumerate(zip(ranks, starts)):
        ref, i = (send_ref, n) if n < 2 else (keep_ref, n - 2)
        for copy in copies[3 * n : 3 * n + 3]:
            copy.wait()
        for j in range(3):
            inside = col >= rank * FFT - start - j * UNIT
            for k, to in enumerate((2 * UNIT * j, 2 * UNIT * j + UNIT, 2 * FFT + UNIT * j)):
                piece = held_ref[n, k, :, j * UNIT : (j + 1) * UNIT]
                ref[i, :, to : to + UNIT] = jnp.where(inside, piece, 0.0).astype(bf16)


def cut(rank, weight):
    scratch = [pltpu.VMEM((4, 3, ROWS, FFT), f32), pltpu.SemaphoreType.DMA((4, 3))]
    outs = [((2, ROWS, 3 * FFT), bf16)] * 2
    return call(cut_kernel, outs, rank, weight, us=2, smem=1, raw=(1,), scratch=scratch)


def near_kernel(flag_ref, own, before, after, across, low_ref, high_ref, vec_ref, out_ref):
    for i, ref in enumerate((own, before, after, across)):
        rows = slice(i * 4 * ROWS, (i + 1) * 4 * ROWS)
        half = slice(i % 2 * 4 * ROWS, (i % 2 + 1) * 4 * ROWS)
        (low_ref if i < 2 else high_ref)[half, :] = ref[:, :COLS]
        vec_ref[rows, :] = ref[:, COLS : COLS + HD]
    rest = slice(COLS + HD, COLS + HD + D)
    first = jnp.where(flag_ref[0] == 1, own[:, rest], across[:, rest])
    second = jnp.where(flag_ref[1] == 1, after[:, rest], before[:, rest])
    out_ref[: 4 * ROWS, :] = first
    out_ref[4 * ROWS :, :] = second


def far_add_kernel(own, low, high, out_ref):
    out_ref[:LINE, :] = (own[:LINE, :].astype(f32) + low[...].astype(f32)).astype(bf16)
    out_ref[LINE:, :] = (own[LINE:, :].astype(f32) + high[...].astype(f32)).astype(bf16)


def far_kernel(proj, proj_got, vec, out, out_got, o0, o1, o2, o3):
    total = proj[...].astype(f32) + proj_got[...].astype(f32)
    rest = out[...].astype(f32) + out_got[...].astype(f32)
    for i, ref in enumerate((o0, o1, o2, o3)):
        rows = slice(i * 4 * ROWS, (i + 1) * 4 * ROWS)
        ref[:, :COLS] = total[rows, :].astype(bf16)
        ref[:, COLS : COLS + HD] = vec[rows, :].astype(bf16)
        half = slice(0, 4 * ROWS) if i in (0, 3) else slice(4 * ROWS, 8 * ROWS)
        ref[:, COLS + HD :] = rest[half, :].astype(bf16)


def order_kernel(place_ref, keep_ref, got_ref, *outs):
    place = place_ref[0]
    for i, ref in enumerate(outs):
        ref[place] = keep_ref[i]
        ref[1 - place] = got_ref[i]


def attn_cut_kernel(side_ref, weight_ref, vec_ref, out_ref):
    side = side_ref[0]
    for start, width, to in ((0, QUERY, 0), (D, HD, QUERY), (D + KV * HD, HD, QUERY + HD)):
        first = pl.multiple_of(start + side * width, 128)
        out_ref[:, to : to + width] = weight_ref[:, pl.ds(first, width)].astype(bf16)
    out_ref[:, COLS : COLS + HD] = vec_ref[...]
    out_ref[:, COLS + HD :] = weight_ref[:, QKV:].astype(bf16)


def adam_update(weight, moment_one, moment_two, gradient, step_rate):
    moment_one = 0.9 * moment_one + 0.1 * gradient
    moment_two = 0.95 * moment_two + 0.05 * gradient * gradient
    first_hat = moment_one / (1.0 - 0.9**STEP)
    second_hat = moment_two / (1.0 - 0.95**STEP)
    updated = weight - step_rate * (first_hat / (jnp.sqrt(second_hat) + 1e-08) + 0.1 * weight)
    return (moment_one, moment_two, updated)


def core_kernel(core_ref, p0, p1, p2, p3, keep_ref, give_ref):
    core = core_ref[0]
    for i, part in enumerate((p0, p1, p2, p3)):
        keep_ref[i] = part[core]
        give_ref[i] = part[1 - core]


def ff_adam_kernel(rank_ref, keep_ref, got_ref, *refs):
    given, results, held, sems = refs[:3], refs[3:6], refs[6:9], refs[9]
    third = lambda ref, k: ref.at[:, pl.ds(k * FF, FF)]
    loads = [[pltpu.make_async_copy(third(a, k), third(b, k), sems.at[i, k]) for i, (a, b) in enumerate(zip(given, held))] for k in range(3)]
    stores = [[pltpu.make_async_copy(third(a, k), third(b, k), sems.at[3 + i, k]) for i, (a, b) in enumerate(zip(held, results))] for k in range(3)]
    for group in loads:
        for copy in group:
            copy.start()

    def put(block, cols):
        weight, one, two = (ref[:, cols] for ref in held)
        one, two, weight = adam_update(weight, one, two, block.astype(f32), 0.02)
        for ref, value in zip(held, (weight, one, two)):
            ref[:, cols] = value

    for k in range(3):
        for copy in loads[k]:
            copy.wait()
        for flip in range(8):
            grad = (keep_ref, got_ref)[flip % 2]
            rank = rank_ref[0] ^ flip
            for j in range(3):
                first = 2 * FFT + UNIT * j if k == 2 else 2 * UNIT * j + UNIT * k

                @pl.when(rank < 7)
                def _():
                    start = pl.multiple_of(k * FF + rank * FFT + j * UNIT, 128)
                    put(grad[flip // 2, :, first : first + UNIT], pl.ds(start, UNIT))

                skip = max(0, 8 * FFT - FF - j * UNIT)
                if skip < UNIT:

                    @pl.when(rank == 7)
                    def _():
                        start = k * FF + FF - FFT + j * UNIT + skip
                        put(grad[flip // 2, :, first + skip : first + UNIT], slice(start, start + UNIT - skip))

        for copy in stores[k]:
            copy.start()
    for group in stores:
        for copy in group:
            copy.wait()


def ff_adam(rank, keep, got, weight, moment_one, moment_two):
    shape = (ROWS, 3 * FF)
    scratch = [pltpu.VMEM(shape, f32)] * 3 + [pltpu.SemaphoreType.DMA((6, 3))]
    weight, one, two = call(
        ff_adam_kernel, [(shape, f32)] * 3, rank, keep, got, weight, moment_one, moment_two,
        smem=1, raw=(3, 4, 5), raw_outs=(0, 1, 2), scratch=scratch,
    )
    return one, two, weight


def attn_adam_kernel(flag_ref, part_ref, other_ref, w_ref, one_ref, two_ref, one_out, two_out, w_out):
    def put(grad, start):
        cols = slice(start, start + grad.shape[1])
        results = adam_update(w_ref[:, cols], one_ref[:, cols], two_ref[:, cols], grad, 0.05)
        for ref, value in zip((one_out, two_out, w_out), results):
            ref[:, cols] = value

    part, other = part_ref[...].astype(f32), other_ref[...].astype(f32)
    own_first = flag_ref[0] == 0
    first = jnp.where(own_first, part[:, :COLS], other[:, :COLS])
    last = jnp.where(own_first, other[:, :COLS], part[:, :COLS])
    put(first[:, :QUERY], 0)
    put(last[:, :QUERY], QUERY)
    put(first[:, QUERY : QUERY + HD], D)
    put(last[:, QUERY : QUERY + HD], D + HD)
    put(first[:, QUERY + HD :], D + KV * HD)
    put(last[:, QUERY + HD :], D + KV * HD + HD)
    put(jnp.where(flag_ref[1] == 1, part[:, COLS + HD :], other[:, COLS + HD :]), QKV)


def shards(
    inputs,
    cotangent,
    attn_weight,
    attn_moment_one,
    attn_moment_two,
    mlp_weight,
    mlp_moment_one,
    mlp_moment_two,
    vectors,
    vector_moment_one,
    vector_moment_two,
):
    half = lax.axis_index("seq")
    yh, core = lax.axis_index("yh"), lax.axis_index("core")
    side = half ^ yh
    rank = half * 4 + yh * 2 + core
    scalar = lambda v: v.astype(jnp.int32).reshape(1)
    x_own, dy_own = inputs[0], cotangent[0]

    vec_own = jnp.pad(vectors.astype(bf16)[None, :], ((0, 15), (0, 48)))
    vec_pair = jnp.concatenate([vec_own[:1], cross_send(vec_own)[:1]])
    vec_block = jnp.concatenate([vec_pair, core_send(jnp.pad(vec_pair, ((0, 14), (0, 0))))[:2]])
    vec_block = jnp.pad(vec_block, ((0, ROWS - 4), (0, 0)))

    mlp_keep, mlp_give = cut(scalar(rank), mlp_weight)
    mlp_got = core_send(mlp_give)
    (attn_block,) = call(
        attn_cut_kernel, [((ROWS, COLS + HD + D), bf16)], scalar(side), attn_weight, vec_block, smem=1, fetch=[1]
    )
    block = ((2, ROWS, 3 * FFT), bf16)
    mlp_near, mlp_far = call(
        order_kernel, [block, block], scalar(core), mlp_keep, mlp_got, smem=1, after=[attn_block]
    )
    mlp_far = cross_send(mlp_far)
    attn_x = join(ring_parts(attn_block, x_send))

    blocks = gathered_blocks(64)
    rows = as_rows((blocks[:, None] * ROWS + jnp.arange(ROWS, dtype=jnp.int32)[None, :]).reshape(D))
    z = lax.axis_index("z")
    inside = z // 2 == side
    first_z = jnp.where(inside, z, z ^ 2)
    j = jnp.arange(HALF, dtype=jnp.int32)
    r, xi, zi, yi, ci = j % 24, (j // 24) % 4, (j // 96) % 2, (j // 192) % 2, j // 384
    feature = ((first_z ^ zi) % 2) * 384 + (yh ^ yi) * 192 + (core ^ ci) * 24 + r
    features = as_rows(feature + (lax.axis_index("x") + near(xi) + 4) % 4 * 48)
    (x_rel,) = call(permute_kernel, [((LEN, D), bf16)], rows, x_own, seq_send(x_own), us=2, store=[0])
    dy_parts = gather_tokens(hold(dy_own, attn_x))

    flags = jnp.stack([inside, inside == (z % 2 == 0)]).astype(jnp.int32)
    part = ((2 * 4 * ROWS, COLS), bf16)
    *proj_z, vec_z, out_z = call(
        near_kernel, [part, part, ((4 * 4 * ROWS, HD), bf16), ((2 * 4 * ROWS, D), bf16)], flags,
        *ring_parts(attn_x, z_send), smem=1, after=dy_parts[1:4], behind=[x_rel],
    )

    (mlp_block,) = call(
        order_kernel, [((2,) + block[0], bf16)], scalar(yh), mlp_near[None], mlp_far[None], smem=1, after=[vec_z]
    )
    mlp_w = lax.all_gather(mlp_block.reshape(4 * ROWS, 3 * FFT), ("z", "x"), axis=0, tiled=True)
    mlp_w = mlp_w.reshape(4, 4, 2, 48, 3 * FFT)

    proj_y = [cross_send(p) for p in proj_z]
    out_y = cross_send(out_z)
    proj_w = proj_z + proj_y
    proj_w = proj_w + [core_send(p) for p in proj_w]

    place = jnp.arange(64, dtype=jnp.int32)
    by_vector = blocks[(place % 4) % 2 * 16 + (place % 4) // 2 * 32 + place // 4]
    pick = (place[:, None] == by_vector[None, :]).astype(bf16)
    vec_rel = vec_z.reshape(16, ROWS, HD)[:, :4].reshape(64, HD)
    vec_all = dot(pick, vec_rel)[:, :80].reshape(1, 5120)
    gain_rows = jnp.broadcast_to(vec_all[:, :D].astype(bf16), (16, D))
    gain_one = call(permute_kernel, [((16, D), f32)], rows, gain_rows, us=1)[0][:1]
    gain_two = vec_all[:, D : 2 * D]
    bias_all = vec_all[:, 2 * D :]
    own_cols = lambda a, start, width: lax.dynamic_slice_in_dim(a, start + side * width, width, 1)
    bias = jnp.concatenate(
        [
            own_cols(bias_all, 0, QUERY),
            own_cols(bias_all, D, HD),
            own_cols(bias_all, D + KV * HD, HD),
        ],
        axis=1,
    )

    cos, sin = rotary_tables((jnp.arange(LEN) + half * TOK) % LEN)
    normed, low, heads_out, logs = attend(
        scalar(half), x_rel, gain_one, proj_w, bias, cos, sin
    )
    out_y = hold(out_y, behind=[normed])
    out_w = [out_z, out_y, core_send(out_z), core_send(out_y)]
    a_rel, branch_own, branch_give = branch(heads_out, features, out_w)
    middle, second = call(
        second_kernel, [((TOK, D), f32), ((TOK, D), bf16)], x_own, branch_own, seq_send(branch_give), gain_two,
        us=2, store=[0, 1],
    )

    second_parts = gather_tokens(second)
    hidden, d_gate_up, d_second_own, d_second_give = feed_forward(second_parts, dy_parts, mlp_w)
    d_second = call(
        add_kernel, [((TOK, D), f32)] + [((TOK, D), bf16)] * 3, d_second_own, core_send(d_second_give)
    )
    mlp_term = ff_grad(second_parts, dy_parts, hidden, d_gate_up, [d_second[0]])
    mlp_part = lax.psum_scatter(
        mlp_term.reshape(D, 3 * FFT), ("z", "x"), scatter_dimension=0, tiled=True
    )
    d_middle, e, d_gain_two = d_middle_of(
        ring_collect(d_second, y_send), middle, gain_two, dy_own, [mlp_term]
    )
    down_own, down_give = down_terms(hidden, mlp_w, [e])

    e_other = seq_send(e)
    out_term = out_terms(a_rel, e, e_other, [down_give])
    (out_far,) = add_up([out_term[1], core_send(out_term[3])], fetch=True)
    (out_near,) = add_up([out_term[0], core_send(out_term[2])], fetch=True)
    out_got = cross_send(out_far)
    *proj_term, d_proj, d_bias_own = attend_back(
        scalar(half), e, e_other, out_w, features, low, logs, cos, sin, normed, [out_far]
    )
    dh_own, dh_give, d_gain_one = d_normed_of(d_proj, x_rel, proj_w)

    (proj_far,) = call(
        far_add_kernel, [((PIECE, COLS), bf16)], proj_term[1], core_send(proj_term[3]), core_send(proj_term[4]),
        fetch=range(3), after=[out_got], behind=[dh_own],
    )
    (proj_near,) = add_up([proj_term[0], core_send(proj_term[2])], fetch=True)
    bias_zero = jnp.zeros((1, QKV), f32)
    put = lambda a, v, start, width: lax.dynamic_update_slice_in_dim(a, v, start + side * width, 1)
    d_bias = put(bias_zero, d_bias_own[:, :QUERY], 0, QUERY)
    d_bias = put(d_bias, d_bias_own[:, QUERY : QUERY + HD], D, HD)
    d_bias = put(d_bias, d_bias_own[:, QUERY + HD :], D + KV * HD, HD)
    d_gain_rows = jnp.broadcast_to(d_gain_one, (8, D))
    d_gain_one = call(unpermute_kernel, [((8, D), f32)], rows, d_gain_rows, us=2)[0][:1]
    vec_term = jnp.concatenate([d_gain_one, d_gain_two, d_bias], axis=1)
    vec_term = jnp.pad(vec_term.reshape(64, 80), ((0, 0), (0, 48))).astype(bf16)
    pick_rel = (place[:, None] == blocks[None, :]).astype(bf16)
    vec_term = dot_tn(pick_rel, vec_term)
    vec_half = pair_reduce(vec_term, core_send)
    vec_got = pair_reduce(vec_half, cross_send)
    vec_term = jnp.pad(vec_got[:, None, :], ((0, 0), (0, ROWS - 1), (0, 0))).reshape(PIECE, HD)
    down = call(
        add_kernel, [((TOK, D), f32)] + [((TOK, D), bf16)] * 3, down_own, core_send(hold(down_give, proj_far)),
        after=[vec_half],
    )
    dh_got = seq_send(dh_give)
    attn_parts = call(
        far_kernel, [((4 * ROWS, COLS + HD + D), bf16)] * 4,
        proj_near, cross_send(proj_far), vec_term, out_near, out_got, after=[down[1], dh_got], store=range(4),
    )
    attn_near = ring_collect(attn_parts, z_send)
    down = ring_collect(down, y_send)
    (input_grad,) = call(
        input_grad_kernel, [((TOK, D), f32)], dh_own, dh_got, x_rel, gain_one, d_middle, rows,
        us=5, fetch=[0, 2, 4], store=[0], after=[attn_parts[0]],
    )
    attn_parts = add_up(attn_near, pieces=4, after=down[1:], behind=[input_grad])

    by_y = hold(mlp_part, behind=[input_grad]).reshape(2, 2, ROWS, 3 * FFT)
    near_rows = lax.dynamic_index_in_dim(by_y, yh, 0, keepdims=False)
    far_rows = lax.dynamic_index_in_dim(by_y, 1 - yh, 0, keepdims=False)
    block = ((4, ROWS, 3 * FFT), bf16)
    grads_keep, grads_give = call(
        core_kernel, [block, block], scalar(core),
        near_rows, ring_send(far_rows, "yh", 1), seq_send(near_rows), cross_send(far_rows), smem=1,
    )
    mlp_one, mlp_two, mlp_new = ff_adam(
        scalar(rank), grads_keep, core_send(grads_give), mlp_weight, mlp_moment_one, mlp_moment_two
    )
    (attn_part,) = add_up(ring_collect(attn_parts, x_send))
    attn_other = hold(seq_send(attn_part), behind=[mlp_one])
    vec_cols = slice(COLS, COLS + 80)
    vec_grad = attn_part[0, vec_cols].astype(f32) + attn_other[0, vec_cols].astype(f32)

    attn_one, attn_two, attn_new = call(
        attn_adam_kernel,
        [((ROWS, QKV + D), f32)] * 3,
        jnp.stack([side, inside.astype(side.dtype)]).astype(jnp.int32),
        attn_part,
        attn_other,
        attn_weight,
        attn_moment_one,
        attn_moment_two,
        smem=1,
    )

    total = down[0] + down[1].astype(f32) + down[2].astype(f32) + down[3].astype(f32)
    output = (middle + total).astype(bf16)[None]
    vec_one, vec_two, vec_new = adam_update(
        vectors, vector_moment_one, vector_moment_two, vec_grad, 0.5
    )
    return (
        output,
        input_grad[None],
        attn_one,
        attn_two,
        attn_new,
        mlp_one,
        mlp_two,
        mlp_new,
        vec_one,
        vec_two,
        vec_new,
    )


def solution(mesh):
    grid = Mesh(mesh.devices.reshape(2, 4, 2, 4, 2), ("seq",) + FSDP)
    tokens, rows, vector = P(FSDP, "seq", None), P(FSDP, None), P(FSDP)
    return jax.shard_map(
        shards,
        mesh=grid,
        in_specs=(tokens, tokens) + (rows,) * 6 + (vector,) * 3,
        out_specs=(tokens, tokens) + (rows,) * 6 + (vector,) * 3,
        check_vma=False,
    )
```
